32 devices in a mesh: groups: 2 (over y), pool: 4 (over z), heads: 2 (over x), rep: 2 (over core).
Axes of the slice: x: 2, y: 2, z: 4, core: 2. Of those that a mesh axis runs over, the one named last changes fastest.
Arguments:
- queries: bfloat16 [4, 4, 8192], P(('groups', 'rep'), 'pool', 'heads'), parts along dimension 0, may hold values from -64 to 64
- latents: bfloat16 [4, 4, 4096, 1024], P(('groups', 'rep'), None, 'pool', 'heads'), parts along dimension 0, may hold values from -6 to 6
- key_latent_maps: bfloat16 [512, 1024], P(None, 'heads'), may hold values from -0.25 to 0.25
- value_latent_maps: bfloat16 [512, 1024], P(None, 'heads'), may hold values from -0.25 to 0.25
- out_weight: bfloat16 [8192, 8192], P('heads', ('pool', 'rep')), may hold values from -2 to 2
- lengths: int32 [4, 4], P(('groups', 'rep')), parts along dimension 0, may hold values from 2048 to 4096, as said below
- selected: int32 [4, 4, 4], P(('groups', 'rep')), parts along dimension 0, may hold values from 0 to 31, as said below
Outputs:
- mixed: bfloat16 [4, 4, 8192], P(('groups', 'rep'), 'heads', 'pool'), parts along dimension 0
The draws below stay inside these ranges and needn't reach their ends.
There are 2 independent parts, one for each index of `groups`. The reference program is written for one: setup_inputs(seed, part) draws one part's arguments, and reference() takes and returns one part's arrays. A program takes and returns all parts, laid end to end along the dimension named above; an argument that names none is the same for every part. Nothing has to cross between parts.
Inputs may be any that keep to these rules, and one draw needn't show every extreme that they name: `lengths`: in every draw one sequence has exactly 2048 cached tokens and another exactly 4096. Each sequence's 4 block indices are distinct and ascending, and every selected block holds at least one token below the sequence's length. Of the blocks 8 k to 8 k + 8 - 1 (any k) at most 2 are selected for one sequence, and in every draw some sequence has exactly 2 selected there.
All inputs are finite; a program needn't handle non-finite values.
Results may differ from the reference program's by a relative error of at most 0.0095.
The reference program's roundings to bfloat16 on the way count: a program that leaves them out, or rounds other values in their place, can miss the bound.
Values may be sent and summed in bfloat16 or wider, within the bound.
No kernel may reach another device: no remote copies, remote signals or barrier semaphores. Data moves between devices by JAX's collectives and lax.ppermute only.
A program may use at most 128 MiB of HBM per device.

```python
import jax
import jax.numpy as jnp
from jax import lax

D = 8192
NQ = 64
KEY_VALUE_HEADS = 8
HEAD_SIZE = 128
LATENT_RANK = 512
LANE = 64
BLOCK = 128
BPS = 8
CAP = 2
QUERY_PER_GROUP = 8
QW = 8192
HALF = 4
CTX = 4096
NSEL = 4
SELECTED_TOKENS = 512
N_POOL = 4
N_REP = 2


def context_lengths(key):
    seq_total = N_REP * HALF
    first_key, second_key, third_key = jax.random.split(key, 3)
    shortest = CTX // 2
    drawn = jax.random.randint(first_key, (seq_total,), shortest, CTX + 1)
    first_pos = jax.random.randint(second_key, (), 0, seq_total)
    second_pos = (first_pos + 1 + jax.random.randint(third_key, (), 0, seq_total - 1)) % seq_total
    position = jnp.arange(seq_total, dtype=jnp.int32)
    drawn = jnp.where(position == first_pos, shortest, jnp.where(position == second_pos, CTX, drawn))
    return drawn.astype(jnp.int32)


def draw_lengths(key, part):
    return context_lengths(key).reshape(N_REP, HALF)


def draw_selected(key, part):
    seq_lengths = context_lengths(key)
    key = jax.random.fold_in(key, 5)
    seq_total = N_REP * HALF
    block_total = BPS * N_POOL
    live_blocks = (seq_lengths + BLOCK - 1) // BLOCK
    noise_bits = jax.random.randint(key, (seq_total, block_total), 0, 65536)
    block_ids = jnp.arange(block_total, dtype=jnp.int32)
    block_score = noise_bits * block_total + block_ids[None, :]
    block_score = jnp.where(block_ids[None, :] < live_blocks[:, None], block_score, -1)
    group_ids = block_ids // BPS
    same_group = group_ids[:, None] == group_ids[None, :]
    outranks = (block_score[:, None, :] > block_score[:, :, None]) & same_group[None, :, :]
    group_rank = jnp.sum(outranks.astype(jnp.int32), axis=2)
    eligible = (block_score >= 0) & (group_rank < CAP)
    pick_score = jnp.where(eligible, block_score, -2 - block_ids[None, :])
    best_values, picked = lax.top_k(pick_score, NSEL)
    picked = jnp.sort(picked.astype(jnp.int32), axis=1)
    return picked.reshape(N_REP, HALF, NSEL).astype(jnp.int32)


def draw_queries(key, part):
    key = jax.random.fold_in(key, 7)
    first_key = jax.random.fold_in(key, 0)
    drawn = jnp.clip(jax.random.normal(first_key, (N_REP, HALF, NQ, HEAD_SIZE), jnp.float32), -6.0, 6.0)
    return drawn.reshape(N_REP, HALF, QW).astype(jnp.bfloat16)


def steps_of(rng, dims, pieces, smallest, top_value):
    level = 1.0
    for axis_at, blocks in pieces:
        heights = jax.random.uniform(jax.random.fold_in(jax.random.fold_in(rng, 6), axis_at), (blocks,), jnp.float32, smallest / len(pieces), top_value / len(pieces))
        level = level * jnp.repeat(jnp.exp(heights), dims[axis_at] // blocks).reshape((-1,) + (1,) * (len(dims) - 1 - axis_at))
    return level


def centred(key, dims, spread, limit, shards=(), held_as=jnp.bfloat16):
    result = jax.random.normal(key, dims, jnp.float32) * spread
    if len(shards) > 0:
        result = steps_of(key, dims, shards, -0.22, 0.18) * result
    return jnp.clip(result, min=-limit, max=limit).astype(held_as)


def setup_inputs(seed: int = 0, part: int = 0) -> dict:
    seeds = jax.random.split(jax.random.key(seed), 8)
    part_splits = jax.random.split(jax.random.fold_in(seeds[7], part), 8)
    queries = draw_queries(jax.random.fold_in(jax.random.fold_in(seeds[7], part), 71), part)
    latents = centred(part_splits[1], (N_REP, HALF, CTX, 2 * LATENT_RANK), 1.0, 6.0, ((0, 2), (2, 4), (3, 2)))
    key_latent_maps = centred(seeds[2], (LATENT_RANK, KEY_VALUE_HEADS * HEAD_SIZE), LATENT_RANK ** -0.5, 0.25, ((1, 2),))
    value_latent_maps = centred(seeds[3], (LATENT_RANK, KEY_VALUE_HEADS * HEAD_SIZE), LATENT_RANK ** -0.5, 0.25, ((1, 2),))
    out_weight = centred(seeds[4], (QW, D), 8 ** -0.5, 2.0, ((0, 2), (1, 8)))
    lengths = draw_lengths(jax.random.fold_in(jax.random.fold_in(seeds[7], part), 71), part)
    selected = draw_selected(jax.random.fold_in(jax.random.fold_in(seeds[7], part), 71), part)
    return dict(queries=queries, latents=latents, key_latent_maps=key_latent_maps, value_latent_maps=value_latent_maps, out_weight=out_weight, lengths=lengths, selected=selected)


ROPE_BASE = 500000.0
MASKED = -1.0e30


def rope_angles(positions, head_width):
    half_width = head_width // 2
    exponents = jnp.arange(half_width, dtype=jnp.float32) * (2.0 / head_width)
    frequency = jnp.power(jnp.float32(ROPE_BASE), -exponents)
    angles = positions.astype(jnp.float32)[..., None] * frequency
    return jnp.cos(angles), jnp.sin(angles)


def rotate(values, cosine_part, sine_part):
    half_width = values.shape[-1] // 2
    front_half = values[..., :half_width]
    back_half = values[..., half_width:]
    return jnp.concatenate([front_half * cosine_part - back_half * sine_part, back_half * cosine_part + front_half * sine_part], axis=-1)


def reference(queries, latents, key_latent_maps, value_latent_maps, out_weight, lengths, selected):
    seq_total = N_REP * HALF
    flat_queries = queries.reshape(seq_total, QW)
    flat_latents = latents.reshape(seq_total, CTX, 2 * LATENT_RANK)
    flat_lengths = lengths.reshape(seq_total)
    flat_picks = selected.reshape(seq_total, NSEL)
    value_latent_table = value_latent_maps.reshape(LATENT_RANK, KEY_VALUE_HEADS, HEAD_SIZE).astype(jnp.float32)

    def attend(inputs):
        single_query_row, latent_seq, length, picked = inputs
        blocks = latent_seq.reshape(BPS * N_POOL, BLOCK, 2 * LATENT_RANK)
        paired = jnp.take(blocks, picked, axis=0).reshape(SELECTED_TOKENS, LATENT_RANK // LANE, 2, LANE)
        key_latent_rows = paired[:, :, 0, :].reshape(SELECTED_TOKENS, LATENT_RANK)
        value_lat = paired[:, :, 1, :].reshape(SELECTED_TOKENS, LATENT_RANK)
        positions = (picked[:, None] * BLOCK + jnp.arange(BLOCK, dtype=jnp.int32)[None, :]).reshape(SELECTED_TOKENS)
        rebuilt_key_rows = jnp.dot(key_latent_rows, key_latent_maps, preferred_element_type=jnp.float32).reshape(SELECTED_TOKENS, KEY_VALUE_HEADS, HEAD_SIZE)
        cosine_part, sine_part = rope_angles(positions, HEAD_SIZE)
        rebuilt_key_rows = rotate(rebuilt_key_rows, cosine_part[:, None, :], sine_part[:, None, :]).astype(jnp.bfloat16)
        query_head_rows = single_query_row.astype(jnp.float32).reshape(KEY_VALUE_HEADS, QUERY_PER_GROUP, HEAD_SIZE)
        query_cos, query_sin = rope_angles(length, HEAD_SIZE)
        query_rot = rotate(query_head_rows, query_cos, query_sin).astype(jnp.bfloat16)
        scores = jnp.einsum("gqd,sgd->gqs", query_rot.astype(jnp.float32), rebuilt_key_rows.astype(jnp.float32)) * (HEAD_SIZE ** -0.5)
        scores = jnp.where(positions[None, None, :] < length, scores, MASKED)
        row_max = jnp.max(scores, axis=-1, keepdims=True)
        weights = jnp.exp(scores - row_max)
        row_total = jnp.sum(weights, axis=-1, keepdims=True)
        attention = (weights / row_total).astype(jnp.bfloat16)
        context = jnp.einsum("gqs,sr->gqr", attention.astype(jnp.float32), value_lat.astype(jnp.float32)).astype(jnp.bfloat16)
        heads_out = jnp.einsum("gqr,rgd->gqd", context.astype(jnp.float32), value_latent_table).astype(jnp.bfloat16)
        return heads_out.reshape(QW)

    outputs = lax.map(attend, (flat_queries, flat_latents, flat_lengths, flat_picks))
    mixed_out = jnp.dot(outputs, out_weight, preferred_element_type=jnp.float32).astype(jnp.bfloat16)
    return mixed_out.reshape(N_REP, HALF, D)
```

```python
import functools

import jax
import jax.numpy as jnp
import numpy as np
from jax import lax
from jax.experimental import pallas as pl
from jax.experimental.pallas import tpu as pltpu
from jax.sharding import PartitionSpec as P

HEAD_SIZE = 128
LANE = 64
BLOCK = 128
CAP = 2
QUERY_PER_GROUP = 8

ROPE_BASE = 500000.0
MASKED = -1e30
FAR = 1 << 29

SMEM = pl.BlockSpec(memory_space=pltpu.SMEM)
VMEM = pl.BlockSpec(memory_space=pltpu.VMEM)
ANY = pl.BlockSpec(memory_space=pl.ANY)


def frequencies():
    half = HEAD_SIZE // 2
    exponents = np.arange(half, dtype=np.float32) * np.float32(2.0 / HEAD_SIZE)
    freq = np.power(np.float64(ROPE_BASE), -exponents.astype(np.float64)).astype(np.float32)
    return np.concatenate([freq, freq])


def rope_tables(positions):
    angles = positions.astype(jnp.float32)[..., None] * jnp.asarray(frequencies())
    sign = jnp.asarray(np.where(np.arange(HEAD_SIZE) < HEAD_SIZE // 2, -1.0, 1.0).astype(np.float32))
    return jnp.cos(angles), jnp.sin(angles) * sign


def shift(value, axes, size, step):
    return lax.ppermute(value, axes, [(i, (i + step) % size) for i in range(size)])


def params(mib, **more):
    return pltpu.CompilerParams(vmem_limit_bytes=mib << 20, **more)


def slot_blocks(sel_ref, seq, sel_count, shard, shard_blocks):
    first = jnp.int32(-1)
    second = jnp.int32(-1)
    for i in range(sel_count):
        block = sel_ref[seq, i]
        here = block // shard_blocks == shard
        second = jnp.where(here & (first >= 0), block, second)
        first = jnp.where(here & (first < 0), block, first)
    return first, second


def gather_kernel(pools, sel_count, sel_ref, lat_ref, keys_ref, *rest):
    value_refs = rest[:pools]
    raw, sems = rest[pools:]
    shard_blocks = lat_ref.shape[2] // BLOCK
    columns = lat_ref.shape[3]
    width = columns // 2
    me = lax.axis_index("pool")
    copies = []
    for k in range(pools):
        seq = lax.rem(me + k, pools)
        for c, block in enumerate(slot_blocks(sel_ref, seq, sel_count, me, shard_blocks)):
            local = jnp.maximum(block - me * shard_blocks, 0)
            row = pl.multiple_of(local * BLOCK, BLOCK)
            at = (k * CAP + c) * BLOCK
            copies.append(
                pltpu.make_async_copy(
                    lat_ref.at[0, seq, pl.ds(row, BLOCK), :],
                    raw.at[pl.ds(at, BLOCK), :],
                    sems.at[k * CAP + c],
                )
            )
            copies[-1].start()
    source = lax.broadcasted_iota(jnp.int32, (columns, columns), 0)
    target = lax.broadcasted_iota(jnp.int32, (columns, columns), 1)
    is_value = (target >= width).astype(jnp.int32)
    within = target - is_value * width
    wanted = (within // LANE) * (2 * LANE) + is_value * LANE + within % LANE
    pick = (source == wanted).astype(jnp.float32).astype(jnp.bfloat16)
    rows = CAP * BLOCK
    for k in range(pools):
        for c in range(CAP):
            copies[k * CAP + c].wait()
        packed = jnp.dot(
            raw[k * rows : (k + 1) * rows, :], pick, preferred_element_type=jnp.float32
        ).astype(jnp.bfloat16)
        keys_ref[k * rows : (k + 1) * rows, :] = packed[:, :width]
        value_refs[k][...] = packed[:, width:]


def score_kernel(pools, heads, sel_count, shard_blocks, sel_ref, len_ref, map_ref, cos_ref, sin_ref, *rest):
    key_refs = rest[:heads]
    query_refs = rest[heads : heads + pools]
    out_refs = rest[heads + pools :]
    me = lax.axis_index("pool")
    head = lax.axis_index("heads")
    width = key_refs[0].shape[1]
    groups = map_ref.shape[1] // HEAD_SIZE
    rows = CAP * BLOCK
    maps = []
    for j in range(heads):
        owner = lax.rem(head - j + heads, heads)
        maps.append(map_ref[pl.ds(pl.multiple_of(owner * width, width), width), :])
    column = lax.broadcasted_iota(jnp.int32, (QUERY_PER_GROUP, rows), 1)
    for k in range(pools):
        seq = lax.rem(me + k, pools)
        first, second = slot_blocks(sel_ref, seq, sel_count, me, shard_blocks)
        first = jnp.where(first < 0, FAR, first * BLOCK)
        second = jnp.where(second < 0, FAR, second * BLOCK)
        position = jnp.where(column < BLOCK, first + column, second + column - BLOCK)
        live = position < len_ref[seq]
        at = slice(k * rows, (k + 1) * rows)
        rebuilt = jnp.dot(key_refs[0][at, :], maps[0], preferred_element_type=jnp.float32)
        for j in range(1, heads):
            rebuilt += jnp.dot(key_refs[j][at, :], maps[j], preferred_element_type=jnp.float32)
        cosine = cos_ref[at, :]
        sine = sin_ref[at, :]
        for g in range(groups):
            one = rebuilt[:, g * HEAD_SIZE : (g + 1) * HEAD_SIZE]
            turned = (one * cosine + pltpu.roll(one, HEAD_SIZE // 2, 1) * sine).astype(jnp.bfloat16)
            mine = slice(g * QUERY_PER_GROUP, (g + 1) * QUERY_PER_GROUP)
            scores = lax.dot_general(
                query_refs[k][mine, :].astype(jnp.bfloat16), turned, (((1,), (1,)), ((), ())),
                preferred_element_type=jnp.float32,
            ) * (HEAD_SIZE ** -0.5)
            out_refs[k][mine, :] = jnp.where(live, scores, MASKED)


def compact_kernel(pools, sel_count, shard_blocks, sel_ref, *rest):
    value_refs = rest[:pools]
    out_ref, sem = rest[pools:]
    me = lax.axis_index("pool")
    place = jnp.int32(0)
    for k in range(pools):
        owner = lax.rem(me - k + pools, pools)
        for c, block in enumerate(slot_blocks(sel_ref, me, sel_count, owner, shard_blocks)):
            @pl.when(block >= 0)
            def _(k=k, c=c, place=place):
                pltpu.make_async_copy(
                    value_refs[k].at[pl.ds(c * BLOCK, BLOCK), :],
                    out_ref.at[pl.ds(pl.multiple_of(place * BLOCK, BLOCK), BLOCK), :],
                    sem,
                ).start()
            place = place + (block >= 0).astype(jnp.int32)
    pltpu.make_async_copy(out_ref, out_ref, sem).wait()


def attend_kernel(pools, heads, sel_count, shard_blocks, sel_ref, map_ref, *rest):
    score_refs = rest[:pools]
    value_refs = rest[pools : pools + heads]
    out_ref, dense = rest[pools + heads :]
    me = lax.axis_index("pool")
    head = lax.axis_index("heads")
    width = value_refs[0].shape[1]
    groups = map_ref.shape[1] // HEAD_SIZE
    scores = [ref[...] for ref in score_refs]
    top = functools.reduce(jnp.maximum, [jnp.max(s, axis=1, keepdims=True) for s in scores])
    weights = [jnp.exp(s - top) for s in scores]
    total = functools.reduce(jnp.add, [jnp.sum(w, axis=1, keepdims=True) for w in weights])
    place = jnp.int32(0)
    for k in range(pools):
        owner = lax.rem(me - k + pools, pools)
        attention = weights[k] / total
        for c, block in enumerate(slot_blocks(sel_ref, me, sel_count, owner, shard_blocks)):
            @pl.when(block >= 0)
            def _(c=c, place=place, attention=attention):
                dense[:, pl.ds(pl.multiple_of(place * BLOCK, BLOCK), BLOCK)] = attention[
                    :, c * BLOCK : (c + 1) * BLOCK
                ]
            place = place + (block >= 0).astype(jnp.int32)
    attention = dense[...].astype(jnp.bfloat16)
    mixed = [None] * groups
    for j in range(heads):
        owner = lax.rem(head - j + heads, heads)
        context = jnp.dot(
            attention, value_refs[j][...], preferred_element_type=jnp.float32
        ).astype(jnp.bfloat16)
        rows = pl.ds(pl.multiple_of(owner * width, width), width)
        for g in range(groups):
            part = jnp.dot(
                context[g * QUERY_PER_GROUP : (g + 1) * QUERY_PER_GROUP, :],
                map_ref[rows, g * HEAD_SIZE : (g + 1) * HEAD_SIZE],
                preferred_element_type=jnp.float32,
            )
            mixed[g] = part if j == 0 else mixed[g] + part
    for g in range(groups):
        for q in range(QUERY_PER_GROUP):
            at = (g * QUERY_PER_GROUP + q) * HEAD_SIZE
            out_ref[:, at : at + HEAD_SIZE] = mixed[g][q : q + 1, :].astype(jnp.bfloat16)


def project_kernel(pools, heads, reps, steps, *refs):
    total = pools * reps
    row_refs = refs[:total]
    weight_ref = refs[total]
    out_refs = refs[total + 1 : total + 1 + heads * reps]
    rows, acc = refs[total + 1 + heads * reps :]
    step = pl.program_id(0)
    depth = weight_ref.shape[0]

    @pl.when(step == 0)
    def _():
        for n in range(total):
            rows[n : n + 1, :] = row_refs[n][...].astype(jnp.float32)
        acc[...] = jnp.zeros_like(acc)

    left = rows[:, pl.ds(pl.multiple_of(step * depth, depth), depth)].astype(jnp.bfloat16)
    acc[...] += jnp.dot(left, weight_ref[...], preferred_element_type=jnp.float32)

    @pl.when(step == steps - 1)
    def _():
        here = lax.axis_index("pool") * reps + lax.axis_index("rep")
        at = lax.axis_index("heads") * reps + lax.axis_index("rep")
        count = heads * reps
        each = pools // heads
        for d in range(count):
            target = lax.rem(at + d, count)
            for u in range(each):
                source = ((target // reps) * each + u) * reps + lax.rem(target, reps)
                n = lax.rem(here - source + total, total)
                out_refs[d][u : u + 1, :] = acc[pl.ds(n, 1), :]


def finish_kernel(heads, reps, *refs):
    count = heads * reps
    part_refs = refs[:count]
    out_ref, acc = refs[count:]
    at = lax.axis_index("heads") * reps + lax.axis_index("rep")
    width = part_refs[0].shape[1]
    acc[...] = jnp.zeros_like(acc)
    for d in range(count):
        source = lax.rem(at - d + count, count)
        columns = pl.ds(pl.multiple_of(lax.rem(source, reps) * width, width), width)
        acc[:, columns] += part_refs[d][...]
    out_ref[0] = acc[...].astype(jnp.bfloat16)


def per_device(queries, latents, key_latent_maps, value_latent_maps, out_weight, lengths, selected):
    pools = lax.axis_size("pool")
    heads = lax.axis_size("heads")
    reps = lax.axis_size("rep")
    me = lax.axis_index("pool")
    picks = selected[0]
    spans = lengths[0]
    half_seqs, sel_count = picks.shape
    assert half_seqs == pools and pools % heads == 0
    shard_blocks = latents.shape[2] // BLOCK
    width = latents.shape[3] // 2
    rows = CAP * BLOCK
    own_width = value_latent_maps.shape[1]
    own_heads = own_width // HEAD_SIZE * QUERY_PER_GROUP
    bf16, f32 = jnp.bfloat16, jnp.float32
    shape = jax.ShapeDtypeStruct

    packed = pl.pallas_call(
        functools.partial(gather_kernel, pools, sel_count),
        out_shape=[shape((pools * rows, width), bf16)] + [shape((rows, width), bf16)] * pools,
        in_specs=[SMEM, ANY],
        out_specs=[VMEM] * (pools + 1),
        scratch_shapes=[
            pltpu.VMEM((pools * rows, 2 * width), bf16),
            pltpu.SemaphoreType.DMA((pools * CAP,)),
        ],
        compiler_params=params(40),
        name="gather",
    )(picks, latents)
    keys, values = packed[0], packed[1:]
    key_parts = [keys] + [shift(keys, "heads", heads, j) for j in range(1, heads)]
    value_parts = [values[0]] + [shift(values[k], "pool", pools, k) for k in range(1, pools)]

    query_cos, query_sin = rope_tables(spans[me])
    query = queries[0].astype(f32).reshape(own_heads, HEAD_SIZE)
    query = (query * query_cos + jnp.roll(query, HEAD_SIZE // 2, axis=1) * query_sin).astype(bf16)
    query_parts = [query] + [shift(query, "pool", pools, pools - k) for k in range(1, pools)]

    order = (me + jnp.arange(pools, dtype=jnp.int32)) % pools
    near = picks[order]
    here = near // shard_blocks == me
    rank = jnp.cumsum(here.astype(jnp.int32), axis=1) - 1
    match = here[:, :, None] & (rank[:, :, None] == jnp.arange(CAP, dtype=jnp.int32))
    slots = jnp.sum(jnp.where(match, near[:, :, None], 0), axis=1)
    positions = (slots[:, :, None] * BLOCK + jnp.arange(BLOCK, dtype=jnp.int32)).reshape(-1)
    cosine, sine = rope_tables(positions)

    dense = pl.pallas_call(
        functools.partial(compact_kernel, pools, sel_count, shard_blocks),
        out_shape=shape((sel_count * BLOCK, width), bf16),
        in_specs=[SMEM] + [ANY] * pools,
        out_specs=ANY,
        scratch_shapes=[pltpu.SemaphoreType.DMA],
        compiler_params=params(16),
        name="compact",
    )(picks, *value_parts)
    dense_parts = [dense] + [shift(dense, "heads", heads, j) for j in range(1, heads)]

    scores = pl.pallas_call(
        functools.partial(score_kernel, pools, heads, sel_count, shard_blocks),
        out_shape=[shape((own_heads, rows), f32)] * pools,
        in_specs=[SMEM, SMEM] + [VMEM] * (3 + heads + pools),
        out_specs=[VMEM] * pools,
        compiler_params=params(40),
        name="score",
    )(picks, spans, key_latent_maps, cosine, sine, *key_parts, *query_parts)
    score_parts = [scores[0]] + [shift(scores[k], "pool", pools, k) for k in range(1, pools)]

    mine = pl.pallas_call(
        functools.partial(attend_kernel, pools, heads, sel_count, shard_blocks),
        out_shape=shape((1, own_heads * HEAD_SIZE), bf16),
        in_specs=[SMEM] + [VMEM] * (1 + pools + heads),
        out_specs=VMEM,
        scratch_shapes=[pltpu.VMEM((own_heads, sel_count * BLOCK), f32)],
        compiler_params=params(40),
        name="attend",
    )(picks, value_latent_maps, *score_parts, *dense_parts)
    row_parts = [mine] + [
        shift(mine, ("pool", "rep"), pools * reps, n) for n in range(1, pools * reps)
    ]

    features, own_columns = out_weight.shape
    depth = min(features, 512)
    steps = features // depth
    each = pools // heads
    whole = lambda i: (0, 0)
    partial = pl.pallas_call(
        functools.partial(project_kernel, pools, heads, reps, steps),
        out_shape=[shape((each, own_columns), f32)] * (heads * reps),
        grid=(steps,),
        in_specs=[pl.BlockSpec((1, features), whole)] * (pools * reps)
        + [pl.BlockSpec((depth, own_columns), lambda i: (i, 0))],
        out_specs=[pl.BlockSpec((each, own_columns), whole)] * (heads * reps),
        scratch_shapes=[
            pltpu.VMEM((pools * reps, features), f32),
            pltpu.VMEM((pools * reps, own_columns), f32),
        ],
        compiler_params=params(40),
        name="project",
    )(*row_parts, out_weight)
    final_parts = [partial[0]] + [
        shift(partial[d], ("heads", "rep"), heads * reps, d) for d in range(1, heads * reps)
    ]
    return pl.pallas_call(
        functools.partial(finish_kernel, heads, reps),
        out_shape=shape((1, each, reps * own_columns), bf16),
        in_specs=[VMEM] * (heads * reps),
        out_specs=VMEM,
        scratch_shapes=[pltpu.VMEM((each, reps * own_columns), f32)],
        name="finish",
    )(*final_parts)


def solution(mesh):
    return jax.shard_map(
        per_device,
        mesh=mesh,
        in_specs=(
            P(("groups", "rep"), "pool", "heads"),
            P(("groups", "rep"), None, "pool", "heads"),
            P(None, "heads"),
            P(None, "heads"),
            P("heads", ("pool", "rep")),
            P(("groups", "rep"), None),
            P(("groups", "rep"), None, None),
        ),
        out_specs=P(("groups", "rep"), "heads", "pool"),
        check_vma=False,
    )
```

```python
import functools

import jax
import jax.numpy as jnp
import numpy as np
from jax import lax
from jax.experimental import pallas as pl
from jax.experimental.pallas import tpu as pltpu
from jax.sharding import PartitionSpec as P

HEAD_SIZE = 128
LANE = 64
BLOCK = 128
CAP = 2
QUERY_PER_GROUP = 8

ROPE_BASE = 500000.0
MASKED = -1e30
FAR = 1 << 29

SMEM = pl.BlockSpec(memory_space=pltpu.SMEM)
VMEM = pl.BlockSpec(memory_space=pltpu.VMEM)
ANY = pl.BlockSpec(memory_space=pl.ANY)
HBM = pl.BlockSpec(memory_space=pltpu.HBM)


def frequencies():
    half = HEAD_SIZE // 2
    exponents = np.arange(half, dtype=np.float32) * np.float32(2.0 / HEAD_SIZE)
    freq = np.power(np.float64(ROPE_BASE), -exponents.astype(np.float64)).astype(np.float32)
    return np.concatenate([freq, freq])[None, :]


def swap(value, axes, size, step):
    return lax.ppermute(value, axes, [(i, i ^ step) for i in range(size)])


def in_hbm(value):
    return pltpu.with_memory_space_constraint(value, pltpu.HBM)


def in_vmem(value):
    return pltpu.with_memory_space_constraint(value, pltpu.VMEM)


def params(mib, **more):
    return pltpu.CompilerParams(vmem_limit_bytes=mib << 20, **more)


def slot_blocks(sel_ref, seq, shard, shard_blocks):
    first = jnp.int32(-1)
    second = jnp.int32(-1)
    for i in range(sel_ref.shape[2]):
        block = sel_ref[0, seq, i]
        here = (block >= shard * shard_blocks) & (block < (shard + 1) * shard_blocks)
        second = jnp.where(here & (first >= 0), block, second)
        first = jnp.where(here & (first < 0), block, first)
    return first, second


def pack_queries(rows, width):
    if width >= HEAD_SIZE:
        each = rows.shape[0] // (width // HEAD_SIZE)
        return [rows[i * each : (i + 1) * each, :] for i in range(width // HEAD_SIZE)], 1
    return [rows[:, i * width : (i + 1) * width] for i in range(HEAD_SIZE // width)], 0


def unpack_queries(packed, width):
    if width >= HEAD_SIZE:
        return jnp.concatenate(
            [packed[:, i * HEAD_SIZE : (i + 1) * HEAD_SIZE] for i in range(width // HEAD_SIZE)], axis=0
        )
    each = packed.shape[0] // (HEAD_SIZE // width)
    return jnp.concatenate(
        [packed[i * each : (i + 1) * each, :] for i in range(HEAD_SIZE // width)], axis=1
    )


def gather_kernel(pools, sel_ref, len_ref, lat_ref, query_ref, freq_ref, near_ref, far_ref, *rest):
    pay_refs = rest[:pools]
    raw, query, sems = rest[pools:]
    shard_blocks = lat_ref.shape[2] // BLOCK
    columns = lat_ref.shape[3]
    width = columns // 2
    rows = CAP * BLOCK
    me = lax.axis_index("pool")
    copies = []
    for k in range(pools):
        seq = me ^ k
        for c, block in enumerate(slot_blocks(sel_ref, seq, me, shard_blocks)):
            local = jnp.maximum(block - me * shard_blocks, 0)
            copies.append(
                pltpu.make_async_copy(
                    lat_ref.at[0, seq, pl.ds(pl.multiple_of(local * BLOCK, BLOCK), BLOCK), :],
                    raw.at[pl.ds((k * CAP + c) * BLOCK, BLOCK), :],
                    sems.at[k * CAP + c],
                )
            )
            copies[-1].start()
    lane = lax.broadcasted_iota(jnp.int32, (1, HEAD_SIZE), 1)
    angle = len_ref[0, me].astype(jnp.float32) * freq_ref[...]
    cosine = jnp.cos(angle)
    sine = jnp.where(lane < HEAD_SIZE // 2, -jnp.sin(angle), jnp.sin(angle))
    for n in range(query.shape[0]):
        query[n : n + 1, :] = query_ref[0, :, n * HEAD_SIZE : (n + 1) * HEAD_SIZE].astype(jnp.float32)
    turned = query[...] * cosine + pltpu.roll(query[...], HEAD_SIZE // 2, 1) * sine
    pieces, axis = pack_queries(turned, width)
    packed_query = jnp.concatenate(pieces, axis=axis).astype(jnp.bfloat16)
    chunk = min(4 * LANE, columns)
    half = chunk // 2
    source = lax.broadcasted_iota(jnp.int32, (chunk, chunk), 0)
    target = lax.broadcasted_iota(jnp.int32, (chunk, chunk), 1)
    within = target & (half - 1)
    wanted = ((within >> 6) << 7) + (within & (LANE - 1)) + jnp.where(target >= half, LANE, 0)
    pick = (source == wanted).astype(jnp.float32).astype(jnp.bfloat16)
    for k in range(pools - 1, -1, -1):
        for c in range(CAP):
            copies[k * CAP + c].wait()
        keys_ref, at = (far_ref, k - pools // 2) if k >= pools // 2 else (near_ref, k)
        for j in range(columns // chunk):
            packed = jnp.dot(
                raw[k * rows : (k + 1) * rows, j * chunk : (j + 1) * chunk], pick,
                preferred_element_type=jnp.float32,
            ).astype(jnp.bfloat16)
            keys_ref[at * rows : (at + 1) * rows, j * half : (j + 1) * half] = packed[:, :half]
            pay_refs[k][:rows, j * half : (j + 1) * half] = packed[:, half:]
        pay_refs[k][rows:, :] = packed_query


def table_kernel(
    pools, shard_blocks, sel_ref, len_ref, freq_ref, after_ref, key_map_ref, value_map_ref,
    cos_ref, sin_ref, live_ref, place_ref, key_out_ref, value_out_ref, sems,
):
    del after_ref
    loads = [
        pltpu.make_async_copy(key_map_ref, key_out_ref, sems.at[0]),
        pltpu.make_async_copy(value_map_ref, value_out_ref, sems.at[1]),
    ]
    for load in loads:
        load.start()
    me = lax.axis_index("pool")
    lane = lax.broadcasted_iota(jnp.int32, (BLOCK, HEAD_SIZE), 1)
    row = lax.broadcasted_iota(jnp.int32, (BLOCK, HEAD_SIZE), 0)
    front = lane < HEAD_SIZE // 2
    across = lax.broadcasted_iota(jnp.int32, (1, BLOCK), 1)
    place = jnp.int32(0)
    for k in range(pools):
        seq = me ^ k
        found = slot_blocks(sel_ref, seq, me, shard_blocks)
        one, two = [jnp.maximum(block, 0) * BLOCK for block in found]
        angle = (jnp.where(front, one, two) + row).astype(jnp.float32) * freq_ref[...]
        for ref, table, sign in ((cos_ref, jnp.cos(angle), 1.0), (sin_ref, jnp.sin(angle), -1.0)):
            turned = pltpu.roll(table, HEAD_SIZE // 2, 1)
            at = k * CAP * BLOCK
            ref[at : at + BLOCK, :] = jnp.where(front, sign * table, turned)
            ref[at + BLOCK : at + 2 * BLOCK, :] = jnp.where(front, sign * turned, table)
        mine = slot_blocks(sel_ref, me, seq, shard_blocks)
        for c in range(CAP):
            start = jnp.where(found[c] < 0, FAR, found[c] * BLOCK)
            live_ref[k : k + 1, c * BLOCK : (c + 1) * BLOCK] = (start + across < len_ref[0, seq]).astype(jnp.int32)
            at = (k * CAP + c) * BLOCK
            used = mine[c] >= 0
            place_ref[:, at : at + BLOCK] = jnp.where(used, place, -1) + 0 * across
            place = place + used.astype(jnp.int32)
    for load in loads:
        load.wait()


def score_kernel(first, count, heads, map_ref, cos_ref, sin_ref, live_ref, *rest):
    key_refs = rest[:heads]
    pay_refs = rest[heads : heads + count]
    out_refs = rest[heads + count :]
    head = lax.axis_index("heads")
    width = key_refs[0].shape[1]
    groups = map_ref.shape[1] // HEAD_SIZE
    rows = CAP * BLOCK
    maps = []
    for j in range(heads):
        owner = head ^ j
        maps.append(map_ref[pl.ds(pl.multiple_of(owner * width, width), width), :])
    for i in range(count):
        k = first + i
        live = live_ref[k : k + 1, :] > 0
        queries = unpack_queries(pay_refs[i][rows:, :], width)
        at = slice(i * rows, (i + 1) * rows)
        rebuilt = jnp.dot(key_refs[0][at, :], maps[0], preferred_element_type=jnp.float32)
        for j in range(1, heads):
            rebuilt += jnp.dot(key_refs[j][at, :], maps[j], preferred_element_type=jnp.float32)
        cosine = cos_ref[k * rows : (k + 1) * rows, :]
        sine = sin_ref[k * rows : (k + 1) * rows, :]
        for g in range(groups):
            one = rebuilt[:, g * HEAD_SIZE : (g + 1) * HEAD_SIZE]
            turned = (one * cosine + pltpu.roll(one, HEAD_SIZE // 2, 1) * sine).astype(jnp.bfloat16)
            mine = slice(g * QUERY_PER_GROUP, (g + 1) * QUERY_PER_GROUP)
            scores = lax.dot_general(
                queries[mine, :], turned, (((1,), (1,)), ((), ())), preferred_element_type=jnp.float32
            ) * (HEAD_SIZE ** -0.5)
            out_refs[i][mine, :] = jnp.where(live, scores, MASKED)


def compact_kernel(pools, shard_blocks, sel_ref, after_ref, *rest):
    del after_ref
    pay_refs = rest[:pools]
    out_ref, sem = rest[pools:]
    me = lax.axis_index("pool")
    place = jnp.int32(0)
    for k in range(pools):
        for c, block in enumerate(slot_blocks(sel_ref, me, me ^ k, shard_blocks)):
            @pl.when(block >= 0)
            def _(k=k, c=c, place=place):
                pltpu.make_async_copy(
                    pay_refs[k].at[pl.ds(c * BLOCK, BLOCK), :],
                    out_ref.at[pl.ds(pl.multiple_of(place * BLOCK, BLOCK), BLOCK), :],
                    sem,
                ).start()
            place = place + (block >= 0).astype(jnp.int32)
    pltpu.make_async_copy(out_ref, out_ref, sem).wait()


def attend_kernel(pools, heads, map_ref, place_ref, *rest):
    score_refs = rest[:pools]
    value_refs = rest[pools : pools + heads]
    out_ref = rest[pools + heads]
    head = lax.axis_index("heads")
    width = value_refs[0].shape[1]
    groups = map_ref.shape[1] // HEAD_SIZE
    scores = [ref[...] for ref in score_refs]
    top = functools.reduce(jnp.maximum, [jnp.max(s, axis=1, keepdims=True) for s in scores])
    weights = [jnp.exp(s - top) for s in scores]
    total = functools.reduce(jnp.add, [jnp.sum(w, axis=1, keepdims=True) for w in weights])
    slots = []
    for k in range(pools):
        attention = weights[k] / total
        for c in range(CAP):
            at = (k * CAP + c) * BLOCK
            slots.append((place_ref[:, at : at + BLOCK], attention[:, c * BLOCK : (c + 1) * BLOCK]))
    dense = []
    for i in range(value_refs[0].shape[0] // BLOCK):
        chosen = jnp.zeros_like(slots[0][1])
        for place, attention in slots:
            chosen = jnp.where(place == i, attention, chosen)
        dense.append(chosen)
    attention = jnp.concatenate(dense, axis=1).astype(jnp.bfloat16)
    mixed = [None] * groups
    for j in range(heads):
        owner = head ^ j
        context = jnp.dot(
            attention, value_refs[j][...], preferred_element_type=jnp.float32
        ).astype(jnp.bfloat16)
        rows = pl.ds(pl.multiple_of(owner * width, width), width)
        for g in range(groups):
            part = jnp.dot(
                context[g * QUERY_PER_GROUP : (g + 1) * QUERY_PER_GROUP, :],
                map_ref[rows, g * HEAD_SIZE : (g + 1) * HEAD_SIZE],
                preferred_element_type=jnp.float32,
            )
            mixed[g] = part if j == 0 else mixed[g] + part
    for g in range(groups):
        for q in range(QUERY_PER_GROUP):
            at = (g * QUERY_PER_GROUP + q) * HEAD_SIZE
            out_ref[:, at : at + HEAD_SIZE] = mixed[g][q : q + 1, :].astype(jnp.bfloat16)


def pair_kernel(*refs):
    for i, ref in enumerate(refs[:-1]):
        refs[-1][i : i + 1, :] = ref[...].astype(jnp.float32).astype(jnp.bfloat16)


def project_kernel(pools, heads, reps, *refs):
    row_refs = refs[:pools]
    weight_ref = refs[pools]
    out_refs = refs[pools + 1 : pools + 1 + heads * reps]
    acc = refs[pools + 1 + heads * reps]
    left = jnp.concatenate([ref[...].astype(jnp.float32) for ref in row_refs], axis=0).astype(jnp.bfloat16)
    acc[...] = jnp.dot(left, weight_ref[...], preferred_element_type=jnp.float32)
    here = lax.axis_index("pool") * reps + lax.axis_index("rep")
    at = lax.axis_index("heads") * reps + lax.axis_index("rep")
    each = pools // heads
    for d in range(heads * reps):
        target = at ^ d
        for u in range(each):
            source = ((target // reps) * each + u) * reps + target % reps
            out_refs[d][u : u + 1, :] = acc[pl.ds(here ^ source, 1), :]


def per_device(queries, latents, key_latent_maps, value_latent_maps, out_weight, lengths, selected):
    pools = lax.axis_size("pool")
    heads = lax.axis_size("heads")
    reps = lax.axis_size("rep")
    half_seqs, sel_count = selected.shape[1:]
    assert half_seqs == pools and pools % heads == 0
    shard_blocks = latents.shape[2] // BLOCK
    width = latents.shape[3] // 2
    rows = CAP * BLOCK
    own_heads = queries.shape[2] // HEAD_SIZE
    query_rows = queries.shape[2] // width
    bf16, f32, i32 = jnp.bfloat16, jnp.float32, jnp.int32
    shape = jax.ShapeDtypeStruct
    freq = jnp.asarray(frequencies())

    packed = pl.pallas_call(
        functools.partial(gather_kernel, pools),
        out_shape=[shape((pools // 2 * rows, width), bf16)] * 2
        + [shape((rows + query_rows, width), bf16)] * pools,
        in_specs=[SMEM, SMEM, HBM, VMEM, VMEM],
        out_specs=[VMEM] * (pools + 2),
        scratch_shapes=[
            pltpu.VMEM((pools * rows, 2 * width), bf16),
            pltpu.VMEM((own_heads, HEAD_SIZE), f32),
            pltpu.SemaphoreType.DMA((pools * CAP,)),
        ],
        compiler_params=params(16),
        name="gather",
    )(in_hbm(selected), in_hbm(lengths), in_hbm(latents), in_hbm(queries), in_hbm(freq))
    near, far, pays = packed[0], packed[1], packed[2:]
    pay_parts = [pays[0]] + [swap(pays[k], "pool", pools, k) for k in range(1, pools)]
    far_parts = [far] + [swap(far, "heads", heads, j) for j in range(1, heads)]
    near_parts = [near] + [swap(near, "heads", heads, j) for j in range(1, heads)]

    cosine, sine, live, place, key_maps, value_maps = pl.pallas_call(
        functools.partial(table_kernel, pools, shard_blocks),
        out_shape=[shape((pools * rows, HEAD_SIZE), f32)] * 2
        + [shape((pools, rows), i32), shape((1, pools * rows), i32)]
        + [shape(key_latent_maps.shape, bf16), shape(value_latent_maps.shape, bf16)],
        in_specs=[SMEM, SMEM, VMEM, ANY, ANY, ANY],
        out_specs=[VMEM] * 6,
        scratch_shapes=[pltpu.SemaphoreType.DMA((2,))],
        compiler_params=params(16),
        name="tables",
    )(in_hbm(selected), in_hbm(lengths), in_hbm(freq), far, in_hbm(key_latent_maps), in_hbm(value_latent_maps))

    dense = pl.pallas_call(
        functools.partial(compact_kernel, pools, shard_blocks),
        out_shape=shape((sel_count * BLOCK, width), bf16),
        in_specs=[SMEM] + [ANY] * (pools + 1),
        out_specs=ANY,
        scratch_shapes=[pltpu.SemaphoreType.DMA],
        compiler_params=params(8),
        name="compact",
    )(in_hbm(selected), place, *pay_parts)
    dense_parts = [dense] + [swap(dense, "heads", heads, j) for j in range(1, heads)]

    def score(first, count, key_parts):
        return pl.pallas_call(
            functools.partial(score_kernel, first, count, heads),
            out_shape=[shape((own_heads, rows), f32)] * count,
            in_specs=[VMEM] * (4 + heads + count),
            out_specs=[VMEM] * count,
            compiler_params=params(20),
            name="score",
        )(key_maps, cosine, sine, live, *key_parts, *pay_parts[first : first + count])

    middle = pools // 2
    far_scores = score(middle, middle, far_parts)
    near_scores = score(0, middle, near_parts)
    scores = [*near_scores, *far_scores]
    score_parts = [scores[0]] + [swap(scores[k], "pool", pools, k) for k in range(1, pools)]

    mine = pl.pallas_call(
        functools.partial(attend_kernel, pools, heads),
        out_shape=shape((1, own_heads * HEAD_SIZE), bf16),
        in_specs=[VMEM] * (2 + pools + heads),
        out_specs=VMEM,
        compiler_params=params(16),
        name="attend",
    )(value_maps, place, *score_parts, *dense_parts)
    pair = pl.pallas_call(
        pair_kernel,
        out_shape=shape((reps, own_heads * HEAD_SIZE), bf16),
        in_specs=[VMEM] * reps,
        out_specs=VMEM,
        compiler_params=params(4),
        name="pair",
    )(mine, *[swap(mine, "rep", reps, r) for r in range(1, reps)])
    row_parts = [pair] + [swap(pair, "pool", pools, k) for k in range(1, pools)]

    features, own_columns = out_weight.shape
    each = pools // heads
    partial = pl.pallas_call(
        functools.partial(project_kernel, pools, heads, reps),
        out_shape=[shape((each, own_columns), f32)] * (heads * reps),
        in_specs=[VMEM] * (pools + 1),
        out_specs=[VMEM] * (heads * reps),
        scratch_shapes=[pltpu.VMEM((pools * reps, own_columns), f32)],
        compiler_params=params(24),
        name="project",
    )(*row_parts, in_vmem(out_weight))
    parts = [partial[0]] + [
        swap(partial[d], ("heads", "rep"), heads * reps, d) for d in range(1, heads * reps)
    ]
    blocks = [sum(parts[h * reps + r] for h in range(heads)) for r in range(reps)]
    rep = lax.axis_index("rep")
    columns = []
    for r in range(reps):
        columns.append(functools.reduce(
            lambda kept, d: jnp.where(rep ^ d == r, blocks[d], kept), range(1, reps), blocks[0]))
    return jnp.concatenate(columns, axis=1).astype(bf16)[None]


def solution(mesh):
    return jax.shard_map(
        per_device,
        mesh=mesh,
        in_specs=(
            P(("groups", "rep"), "pool", "heads"),
            P(("groups", "rep"), None, "pool", "heads"),
            P(None, "heads"),
            P(None, "heads"),
            P("heads", ("pool", "rep")),
            P(("groups", "rep"), None),
            P(("groups", "rep"), None, None),
        ),
        out_specs=P(("groups", "rep"), "heads", "pool"),
        check_vma=False,
    )
```

```python
import functools

import jax
import jax.numpy as jnp
import numpy as np
from jax import lax
from jax.experimental import pallas as pl
from jax.experimental.pallas import tpu as pltpu
from jax.sharding import PartitionSpec as P

HEAD_SIZE = 128
LANE = 64
BLOCK = 128
CAP = 2
QUERY_PER_GROUP = 8

ROPE_BASE = 500000.0
MASKED = -1e30
FAR = 1 << 29

SMEM = pl.BlockSpec(memory_space=pltpu.SMEM)
VMEM = pl.BlockSpec(memory_space=pltpu.VMEM)
ANY = pl.BlockSpec(memory_space=pl.ANY)
HBM = pl.BlockSpec(memory_space=pltpu.HBM)


def frequencies():
    half = HEAD_SIZE // 2
    exponents = np.arange(half, dtype=np.float32) * np.float32(2.0 / HEAD_SIZE)
    freq = np.power(np.float64(ROPE_BASE), -exponents.astype(np.float64)).astype(np.float32)
    return np.concatenate([freq, freq])[None, :]


def swap(value, axes, size, step):
    return lax.ppermute(value, axes, [(i, i ^ step) for i in range(size)])


def in_hbm(value):
    return pltpu.with_memory_space_constraint(value, pltpu.HBM)


def in_vmem(value):
    return pltpu.with_memory_space_constraint(value, pltpu.VMEM)


def params(mib, **more):
    return pltpu.CompilerParams(vmem_limit_bytes=mib << 20, **more)


def slot_blocks(sel_ref, seq, shard, shard_blocks):
    first = jnp.int32(-1)
    second = jnp.int32(-1)
    for i in range(sel_ref.shape[2]):
        block = sel_ref[0, seq, i]
        here = (block >= shard * shard_blocks) & (block < (shard + 1) * shard_blocks)
        second = jnp.where(here & (first >= 0), block, second)
        first = jnp.where(here & (first < 0), block, first)
    return first, second


def gather_kernel(pools, sel_ref, lat_ref, query_ref, line_ref, near_ref, far_ref, *rest):
    value_refs = rest[:pools]
    raw, sems = rest[pools:]
    shard_blocks = lat_ref.shape[2] // BLOCK
    columns = lat_ref.shape[3]
    width = columns // 2
    rows = CAP * BLOCK
    me = lax.axis_index("pool")
    copies = {}
    for k in range(pools - 1, -1, -1):
        seq = me ^ k
        for c, block in enumerate(slot_blocks(sel_ref, seq, me, shard_blocks)):
            local = jnp.maximum(block - me * shard_blocks, 0)
            copies[k, c] = pltpu.make_async_copy(
                lat_ref.at[0, seq, pl.ds(pl.multiple_of(local * BLOCK, BLOCK), BLOCK), :],
                raw.at[pl.ds((k * CAP + c) * BLOCK, BLOCK), :],
                sems.at[k * CAP + c],
            )
            copies[k, c].start()
    line_ref[...] = query_ref[0]
    chunk = min(4 * LANE, columns)
    half = chunk // 2
    source = lax.broadcasted_iota(jnp.int32, (chunk, chunk), 0)
    target = lax.broadcasted_iota(jnp.int32, (chunk, chunk), 1)
    within = target & (half - 1)
    wanted = ((within >> 6) << 7) + (within & (LANE - 1)) + jnp.where(target >= half, LANE, 0)
    pick = (source == wanted).astype(jnp.float32).astype(jnp.bfloat16)
    for k in range(pools - 1, -1, -1):
        for c in range(CAP):
            copies[k, c].wait()
        keys_ref, at = (far_ref, k - pools // 2) if k >= pools // 2 else (near_ref, k)
        for j in range(columns // chunk):
            packed = jnp.dot(
                raw[k * rows : (k + 1) * rows, j * chunk : (j + 1) * chunk], pick,
                preferred_element_type=jnp.float32,
            ).astype(jnp.bfloat16)
            keys_ref[at * rows : (at + 1) * rows, j * half : (j + 1) * half] = packed[:, :half]
            value_refs[k][:, j * half : (j + 1) * half] = packed[:, half:]


def table_kernel(
    pools, shard_blocks, sel_ref, len_ref, freq_ref, after_ref, key_map_ref, value_map_ref,
    cos_ref, sin_ref, turn_ref, live_ref, place_ref, key_out_ref, value_out_ref, sems,
):
    del after_ref
    loads = [
        pltpu.make_async_copy(key_map_ref, key_out_ref, sems.at[0]),
        pltpu.make_async_copy(value_map_ref, value_out_ref, sems.at[1]),
    ]
    for load in loads:
        load.start()
    me = lax.axis_index("pool")
    lane = lax.broadcasted_iota(jnp.int32, (BLOCK, HEAD_SIZE), 1)
    row = lax.broadcasted_iota(jnp.int32, (BLOCK, HEAD_SIZE), 0)
    front = lane < HEAD_SIZE // 2
    across = lax.broadcasted_iota(jnp.int32, (1, BLOCK), 1)
    place = jnp.int32(0)
    for k in range(pools):
        turn_ref[k : k + 1, :] = len_ref[0, me ^ k].astype(jnp.float32) * freq_ref[...]
    angle = turn_ref[0:pools, :]
    turn_ref[0:pools, :] = jnp.cos(angle)
    turn_ref[pools:, :] = jnp.where(front[:1, :], -jnp.sin(angle), jnp.sin(angle))
    for k in range(pools):
        seq = me ^ k
        found = slot_blocks(sel_ref, seq, me, shard_blocks)
        one, two = [jnp.maximum(block, 0) * BLOCK for block in found]
        angle = (jnp.where(front, one, two) + row).astype(jnp.float32) * freq_ref[...]
        for ref, table, sign in ((cos_ref, jnp.cos(angle), 1.0), (sin_ref, jnp.sin(angle), -1.0)):
            turned = pltpu.roll(table, HEAD_SIZE // 2, 1)
            at = k * CAP * BLOCK
            ref[at : at + BLOCK, :] = jnp.where(front, sign * table, turned)
            ref[at + BLOCK : at + 2 * BLOCK, :] = jnp.where(front, sign * turned, table)
        mine = slot_blocks(sel_ref, me, seq, shard_blocks)
        for c in range(CAP):
            start = jnp.where(found[c] < 0, FAR, found[c] * BLOCK)
            live_ref[k : k + 1, c * BLOCK : (c + 1) * BLOCK] = (start + across < len_ref[0, seq]).astype(jnp.int32)
            at = (k * CAP + c) * BLOCK
            used = mine[c] >= 0
            place_ref[:, at : at + BLOCK] = jnp.where(used, place, -1) + 0 * across
            place = place + used.astype(jnp.int32)
    for load in loads:
        load.wait()


def score_kernel(first, count, heads, pools, map_ref, cos_ref, sin_ref, turn_ref, live_ref, query_ref, after_ref, *rest):
    del after_ref
    key_refs = rest[:heads]
    out_refs = rest[heads : heads + count]
    head = lax.axis_index("heads")
    width = key_refs[0].shape[1]
    groups = map_ref.shape[1] // HEAD_SIZE
    rows = CAP * BLOCK
    maps = []
    for j in range(heads):
        owner = head ^ j
        maps.append(map_ref[pl.ds(pl.multiple_of(owner * width, width), width), :])
    for i in range(count):
        k = first + i
        live = live_ref[k : k + 1, :] > 0
        line = query_ref[i : i + 1, :].astype(jnp.float32)
        query = jnp.concatenate(
            [line[:, n * HEAD_SIZE : (n + 1) * HEAD_SIZE] for n in range(groups * QUERY_PER_GROUP)], axis=0
        )
        query = query * turn_ref[k : k + 1, :] + pltpu.roll(query, HEAD_SIZE // 2, 1) * turn_ref[
            pools + k : pools + k + 1, :
        ]
        queries = query.astype(jnp.bfloat16)
        at = slice(i * rows, (i + 1) * rows)
        rebuilt = jnp.dot(key_refs[0][at, :], maps[0], preferred_element_type=jnp.float32)
        for j in range(1, heads):
            rebuilt += jnp.dot(key_refs[j][at, :], maps[j], preferred_element_type=jnp.float32)
        cosine = cos_ref[k * rows : (k + 1) * rows, :]
        sine = sin_ref[k * rows : (k + 1) * rows, :]
        for g in range(groups):
            one = rebuilt[:, g * HEAD_SIZE : (g + 1) * HEAD_SIZE]
            turned = (one * cosine + pltpu.roll(one, HEAD_SIZE // 2, 1) * sine).astype(jnp.bfloat16)
            mine = slice(g * QUERY_PER_GROUP, (g + 1) * QUERY_PER_GROUP)
            scores = lax.dot_general(
                queries[mine, :], turned, (((1,), (1,)), ((), ())), preferred_element_type=jnp.float32
            ) * (HEAD_SIZE ** -0.5)
            out_refs[i][mine, :] = jnp.where(live, scores, MASKED)


def compact_kernel(pools, shard_blocks, sel_ref, *rest):
    value_refs = rest[:pools][::-1]
    out_ref, sem = rest[-2:]
    me = lax.axis_index("pool")
    place = jnp.int32(0)
    for k in range(pools):
        for c, block in enumerate(slot_blocks(sel_ref, me, me ^ k, shard_blocks)):
            @pl.when(block >= 0)
            def _(k=k, c=c, place=place):
                pltpu.make_async_copy(
                    value_refs[k].at[pl.ds(c * BLOCK, BLOCK), :],
                    out_ref.at[pl.ds(pl.multiple_of(place * BLOCK, BLOCK), BLOCK), :],
                    sem,
                ).start()
            place = place + (block >= 0).astype(jnp.int32)
    pltpu.make_async_copy(out_ref, out_ref, sem).wait()


def attend_kernel(pools, heads, map_ref, place_ref, *rest):
    score_refs = rest[:pools][::-1]
    value_refs = rest[pools : pools + heads]
    out_ref = rest[pools + heads]
    head = lax.axis_index("heads")
    width = value_refs[0].shape[1]
    groups = map_ref.shape[1] // HEAD_SIZE
    scores = [ref[...] for ref in score_refs]
    top = functools.reduce(jnp.maximum, [jnp.max(s, axis=1, keepdims=True) for s in scores])
    weights = [jnp.exp(s - top) for s in scores]
    total = functools.reduce(jnp.add, [jnp.sum(w, axis=1, keepdims=True) for w in weights])
    slots = []
    for k in range(pools):
        attention = weights[k] / total
        for c in range(CAP):
            at = (k * CAP + c) * BLOCK
            slots.append((place_ref[:, at : at + BLOCK], attention[:, c * BLOCK : (c + 1) * BLOCK]))
    dense = []
    for i in range(value_refs[0].shape[0] // BLOCK):
        chosen = jnp.zeros_like(slots[0][1])
        for place, attention in slots:
            chosen = jnp.where(place == i, attention, chosen)
        dense.append(chosen)
    attention = jnp.concatenate(dense, axis=1).astype(jnp.bfloat16)
    mixed = [None] * groups
    for j in range(heads):
        owner = head ^ j
        context = jnp.dot(
            attention, value_refs[j][...], preferred_element_type=jnp.float32
        ).astype(jnp.bfloat16)
        rows = pl.ds(pl.multiple_of(owner * width, width), width)
        for g in range(groups):
            part = jnp.dot(
                context[g * QUERY_PER_GROUP : (g + 1) * QUERY_PER_GROUP, :],
                map_ref[rows, g * HEAD_SIZE : (g + 1) * HEAD_SIZE],
                preferred_element_type=jnp.float32,
            )
            mixed[g] = part if j == 0 else mixed[g] + part
    for g in range(groups):
        for q in range(QUERY_PER_GROUP):
            at = (g * QUERY_PER_GROUP + q) * HEAD_SIZE
            out_ref[:, at : at + HEAD_SIZE] = mixed[g][q : q + 1, :].astype(jnp.bfloat16)


def join_kernel(*refs):
    rows = [ref[...].reshape(-1, ref.shape[-1]).astype(jnp.float32) for ref in refs[:-1]]
    refs[-1][...] = jnp.concatenate(rows, axis=0).astype(jnp.bfloat16)


def project_kernel(pools, heads, reps, own_ref, far_ref, weight_ref, *rest):
    out_refs = rest[:heads]
    acc = rest[heads]
    left = jnp.concatenate(
        [own_ref[...].astype(jnp.float32), far_ref[...].astype(jnp.float32)], axis=0
    ).astype(jnp.bfloat16)
    acc[...] = jnp.dot(left, weight_ref[...], preferred_element_type=jnp.float32)
    pool = lax.axis_index("pool")
    head = lax.axis_index("heads")
    each = pools // heads
    for j in range(heads):
        for t in range(reps):
            for u in range(each):
                n = (pool ^ ((head ^ j) * each + u)) * reps + t
                out_refs[j][t * each + u : t * each + u + 1, :] = acc[pl.ds(n, 1), :]


def sum_kernel(reps, *refs):
    part_refs, out_refs = refs[:-reps], refs[-reps:]
    total = functools.reduce(jnp.add, [ref[...] for ref in part_refs])
    each = total.shape[0] // reps
    for t in range(reps):
        out_refs[t][...] = total[t * each : (t + 1) * each, :].astype(jnp.bfloat16)


def place_kernel(reps, *refs):
    out_ref = refs[reps]
    rep = lax.axis_index("rep")
    width = refs[0].shape[1]
    for t in range(reps):
        out_ref[0, :, pl.ds(pl.multiple_of((rep ^ t) * width, width), width)] = refs[t][...]


def per_device(queries, latents, key_latent_maps, value_latent_maps, out_weight, lengths, selected):
    pools = lax.axis_size("pool")
    heads = lax.axis_size("heads")
    reps = lax.axis_size("rep")
    half_seqs, sel_count = selected.shape[1:]
    assert half_seqs == pools and pools % heads == 0
    shard_blocks = latents.shape[2] // BLOCK
    width = latents.shape[3] // 2
    rows = CAP * BLOCK
    own_heads = queries.shape[2] // HEAD_SIZE
    bf16, f32, i32 = jnp.bfloat16, jnp.float32, jnp.int32
    shape = jax.ShapeDtypeStruct
    freq = jnp.asarray(frequencies())

    def join(*blocks):
        return pl.pallas_call(
            join_kernel,
            out_shape=shape((sum(block.size for block in blocks) // queries.shape[2], queries.shape[2]), bf16),
            in_specs=[VMEM] * len(blocks),
            out_specs=VMEM,
            compiler_params=params(4),
            name="join",
        )(*blocks)

    packed = pl.pallas_call(
        functools.partial(gather_kernel, pools),
        out_shape=[shape((1, queries.shape[2]), bf16)]
        + [shape((pools // 2 * rows, width), bf16)] * 2
        + [shape((rows, width), bf16)] * pools,
        in_specs=[SMEM, HBM, VMEM],
        out_specs=[VMEM] * (pools + 3),
        scratch_shapes=[
            pltpu.VMEM((pools * rows, 2 * width), bf16),
            pltpu.SemaphoreType.DMA((pools * CAP,)),
        ],
        compiler_params=params(16),
        name="gather",
    )(in_hbm(selected), in_hbm(latents), in_hbm(queries))
    line, near, far, values = packed[0], packed[1], packed[2], packed[3:]
    value_parts = {k: swap(values[k], "pool", pools, k) for k in range(pools - 1, 0, -1)}
    value_parts = [values[0]] + [value_parts[k] for k in range(1, pools)]
    far_parts = [far] + [swap(far, "heads", heads, j) for j in range(1, heads)]
    near_parts = [near] + [swap(near, "heads", heads, j) for j in range(1, heads)]
    middle = pools // 2
    near_queries = line
    step = 1
    while step < middle:
        near_queries = join(near_queries, swap(near_queries, "pool", pools, step))
        step *= 2
    far_queries = swap(near_queries, "pool", pools, middle)

    cosine, sine, turn, live, place, key_maps, value_maps = pl.pallas_call(
        functools.partial(table_kernel, pools, shard_blocks),
        out_shape=[shape((pools * rows, HEAD_SIZE), f32)] * 2
        + [shape((2 * pools, HEAD_SIZE), f32), shape((pools, rows), i32), shape((1, pools * rows), i32)]
        + [shape(key_latent_maps.shape, bf16), shape(value_latent_maps.shape, bf16)],
        in_specs=[SMEM, SMEM, VMEM, ANY, ANY, ANY],
        out_specs=[VMEM] * 7,
        scratch_shapes=[pltpu.SemaphoreType.DMA((2,))],
        compiler_params=params(16),
        name="tables",
    )(in_hbm(selected), in_hbm(lengths), in_hbm(freq), near_queries, in_hbm(key_latent_maps), in_hbm(value_latent_maps))

    def score(first, count, key_parts, query_parts, after):
        return pl.pallas_call(
            functools.partial(score_kernel, first, count, heads, pools),
            out_shape=[shape((own_heads, rows), f32)] * count,
            in_specs=[VMEM] * 6 + [ANY] + [VMEM] * heads,
            out_specs=[VMEM] * count,
            compiler_params=params(20),
            name="score",
        )(key_maps, cosine, sine, turn, live, query_parts, after, *key_parts)

    far_scores = score(middle, middle, far_parts, far_queries, near_queries)
    near_scores = score(0, middle, near_parts, near_queries, far_scores[0])
    scores = [*near_scores, *far_scores]
    score_parts = {k: swap(scores[k], "pool", pools, k) for k in range(pools - 1, 0, -1)}
    score_parts = [scores[0]] + [score_parts[k] for k in range(1, pools)]
    dense = pl.pallas_call(
        functools.partial(compact_kernel, pools, shard_blocks),
        out_shape=shape((sel_count * BLOCK, width), bf16),
        in_specs=[SMEM] + [ANY] * (2 * pools - middle),
        out_specs=ANY,
        scratch_shapes=[pltpu.SemaphoreType.DMA],
        compiler_params=params(8),
        name="compact",
    )(in_hbm(selected), *value_parts[::-1], *score_parts[:middle - 1 : -1])
    dense_parts = [dense] + [swap(dense, "heads", heads, j) for j in range(1, heads)]


    mine = pl.pallas_call(
        functools.partial(attend_kernel, pools, heads),
        out_shape=shape((1, own_heads * HEAD_SIZE), bf16),
        in_specs=[VMEM] * (2 + pools + heads),
        out_specs=VMEM,
        compiler_params=params(16),
        name="attend",
    )(value_maps, place, *score_parts[::-1], *dense_parts)
    own_rows = join(mine, *[swap(mine, "rep", reps, r) for r in range(1, reps)])
    step = 1
    while step < middle:
        own_rows = join(own_rows, swap(own_rows, "pool", pools, step))
        step *= 2
    far_rows = swap(own_rows, "pool", pools, middle)

    own_columns = out_weight.shape[1]
    each = pools // heads
    parts = pl.pallas_call(
        functools.partial(project_kernel, pools, heads, reps),
        out_shape=[shape((reps * each, own_columns), f32)] * heads,
        in_specs=[VMEM] * 3,
        out_specs=[VMEM] * heads,
        scratch_shapes=[pltpu.VMEM((pools * reps, own_columns), f32)],
        compiler_params=params(24),
        name="project",
    )(own_rows, far_rows, in_vmem(out_weight))
    sums = pl.pallas_call(
        functools.partial(sum_kernel, reps),
        out_shape=[shape((each, own_columns), bf16)] * reps,
        in_specs=[VMEM] * heads,
        out_specs=[VMEM] * reps,
        compiler_params=params(4),
        name="sum",
    )(parts[0], *[swap(parts[j], "heads", heads, j) for j in range(1, heads)])
    return pl.pallas_call(
        functools.partial(place_kernel, reps),
        out_shape=shape((1, each, reps * own_columns), bf16),
        in_specs=[VMEM] * reps,
        out_specs=VMEM,
        compiler_params=params(4),
        name="place",
    )(sums[0], *[swap(sums[t], "rep", reps, t) for t in range(1, reps)])


def solution(mesh):
    return jax.shard_map(
        per_device,
        mesh=mesh,
        in_specs=(
            P(("groups", "rep"), "pool", "heads"),
            P(("groups", "rep"), None, "pool", "heads"),
            P(None, "heads"),
            P(None, "heads"),
            P("heads", ("pool", "rep")),
            P(("groups", "rep"), None),
            P(("groups", "rep"), None, None),
        ),
        out_specs=P(("groups", "rep"), "heads", "pool"),
        check_vma=False,
    )
```

```python
import functools

import jax
import jax.numpy as jnp
import numpy as np
from jax import lax
from jax.experimental import pallas as pl
from jax.experimental.pallas import tpu as pltpu
from jax.sharding import PartitionSpec as P

HEAD_SIZE = 128
LANE = 64
BLOCK = 128
CAP = 2
QUERY_PER_GROUP = 8

ROPE_BASE = 500000.0
MASKED = -1e30
FAR = 1 << 29

SMEM = pl.BlockSpec(memory_space=pltpu.SMEM)
VMEM = pl.BlockSpec(memory_space=pltpu.VMEM)
ANY = pl.BlockSpec(memory_space=pl.ANY)
HBM = pl.BlockSpec(memory_space=pltpu.HBM)


def frequencies():
    half = HEAD_SIZE // 2
    exponents = np.arange(half, dtype=np.float32) * np.float32(2.0 / HEAD_SIZE)
    freq = np.power(np.float64(ROPE_BASE), -exponents.astype(np.float64)).astype(np.float32)
    return np.concatenate([freq, freq])[None, :]


def swap(value, axes, size, step):
    return lax.ppermute(value, axes, [(i, i ^ step) for i in range(size)])


def in_hbm(value):
    return pltpu.with_memory_space_constraint(value, pltpu.HBM)


def in_vmem(value):
    return pltpu.with_memory_space_constraint(value, pltpu.VMEM)


def params(mib, **more):
    return pltpu.CompilerParams(vmem_limit_bytes=mib << 20, **more)


def slot_blocks(sel_ref, seq, shard, shard_blocks):
    first = jnp.int32(-1)
    second = jnp.int32(-1)
    for i in range(sel_ref.shape[2]):
        block = sel_ref[0, seq, i]
        here = (block >= shard * shard_blocks) & (block < (shard + 1) * shard_blocks)
        second = jnp.where(here & (first >= 0), block, second)
        first = jnp.where(here & (first < 0), block, first)
    return first, second


def heads_to_rows(line, lanes):
    count = line.shape[1] // HEAD_SIZE
    rows = jnp.concatenate([line[:, n * HEAD_SIZE : (n + 1) * HEAD_SIZE] for n in range(count)], axis=0)
    return jnp.concatenate([rows[:, i : i + lanes] for i in range(0, HEAD_SIZE, lanes)], axis=0)


def rows_to_heads(rows):
    pieces = HEAD_SIZE // rows.shape[1]
    count = rows.shape[0] // pieces
    return jnp.concatenate([rows[i * count : (i + 1) * count, :] for i in range(pieces)], axis=1)


def gather_kernel(pools, sel_ref, lat_ref, query_ref, near_ref, far_ref, *rest):
    value_refs = rest[:-2]
    raw, sems = rest[-2:]
    shard_blocks = lat_ref.shape[2] // BLOCK
    columns = lat_ref.shape[3]
    width = columns // 2
    rows = CAP * BLOCK
    me = lax.axis_index("pool")
    copies = {}
    for k in range(pools - 1, -1, -1):
        seq = me ^ k
        for c, block in enumerate(slot_blocks(sel_ref, seq, me, shard_blocks)):
            local = jnp.maximum(block - me * shard_blocks, 0)
            copies[k, c] = pltpu.make_async_copy(
                lat_ref.at[0, seq, pl.ds(pl.multiple_of(local * BLOCK, BLOCK), BLOCK), :],
                raw.at[pl.ds((k * CAP + c) * BLOCK, BLOCK), :],
                sems.at[k * CAP + c],
            )
            copies[k, c].start()
    queries = heads_to_rows(query_ref[0].astype(jnp.float32), value_refs[0].shape[1]).astype(jnp.bfloat16)
    chunk = min(4 * LANE, columns)
    half = chunk // 2
    source = lax.broadcasted_iota(jnp.int32, (chunk, chunk), 0)
    target = lax.broadcasted_iota(jnp.int32, (chunk, chunk), 1)
    within = target & (half - 1)
    wanted = ((within >> 6) << 7) + (within & (LANE - 1)) + jnp.where(target >= half, LANE, 0)
    pick = (source == wanted).astype(jnp.float32).astype(jnp.bfloat16)
    for k in range(pools - 1, -1, -1):
        for c in range(CAP):
            copies[k, c].wait()
        keys_ref, at = (far_ref, k - pools // 2) if k >= pools // 2 else (near_ref, k)
        for j in range(columns // chunk):
            packed = jnp.dot(
                raw[k * rows : (k + 1) * rows, j * chunk : (j + 1) * chunk], pick,
                preferred_element_type=jnp.float32,
            ).astype(jnp.bfloat16)
            keys_ref[at * rows : (at + 1) * rows, j * half : (j + 1) * half] = packed[:, :half]
            value_refs[j * pools + k][:rows, :] = packed[:, half:]
        value_refs[k][rows:, :] = queries


def table_kernel(pools, shard_blocks, sel_ref, len_ref, freq_ref, key_map_ref, value_map_ref, *rest):
    held = (len(rest) - 8) // 2
    cos_ref, sin_ref, turn_ref, live_ref, place_ref, key_out_ref, value_out_ref = rest[held : held + 7]
    sems = rest[-1]
    loads = [
        pltpu.make_async_copy(key_map_ref, key_out_ref, sems.at[0]),
        pltpu.make_async_copy(value_map_ref, value_out_ref, sems.at[1]),
    ]
    for load in loads:
        load.start()
    me = lax.axis_index("pool")
    lane = lax.broadcasted_iota(jnp.int32, (BLOCK, HEAD_SIZE), 1)
    row = lax.broadcasted_iota(jnp.int32, (BLOCK, HEAD_SIZE), 0)
    front = lane < HEAD_SIZE // 2
    across = lax.broadcasted_iota(jnp.int32, (1, BLOCK), 1)
    place = jnp.int32(0)
    for k in range(pools):
        turn_ref[k : k + 1, :] = len_ref[0, me ^ k].astype(jnp.float32) * freq_ref[...]
    angle = turn_ref[0:pools, :]
    turn_ref[0:pools, :] = jnp.cos(angle)
    turn_ref[pools:, :] = jnp.where(front[:1, :], -jnp.sin(angle), jnp.sin(angle))
    for k in range(pools):
        seq = me ^ k
        found = slot_blocks(sel_ref, seq, me, shard_blocks)
        one, two = [jnp.maximum(block, 0) * BLOCK for block in found]
        angle = (jnp.where(front, one, two) + row).astype(jnp.float32) * freq_ref[...]
        for ref, table, sign in ((cos_ref, jnp.cos(angle), 1.0), (sin_ref, jnp.sin(angle), -1.0)):
            turned = pltpu.roll(table, HEAD_SIZE // 2, 1)
            at = k * CAP * BLOCK
            ref[at : at + BLOCK, :] = jnp.where(front, sign * table, turned)
            ref[at + BLOCK : at + 2 * BLOCK, :] = jnp.where(front, sign * turned, table)
        mine = slot_blocks(sel_ref, me, seq, shard_blocks)
        for c in range(CAP):
            start = jnp.where(found[c] < 0, FAR, found[c] * BLOCK)
            live_ref[k : k + 1, c * BLOCK : (c + 1) * BLOCK] = (start + across < len_ref[0, seq]).astype(jnp.int32)
            at = (k * CAP + c) * BLOCK
            used = mine[c] >= 0
            place_ref[:, at : at + BLOCK] = jnp.where(used, place, -1) + 0 * across
            place = place + used.astype(jnp.int32)
    for load in loads:
        load.wait()


def score_kernel(first, count, heads, pools, map_ref, cos_ref, sin_ref, turn_ref, live_ref, after_ref, *rest):
    del after_ref
    key_refs = rest[:heads]
    pay_refs = rest[heads : heads + count][::-1]
    out_refs = rest[heads + count :]
    head = lax.axis_index("heads")
    width = key_refs[0].shape[1]
    groups = map_ref.shape[1] // HEAD_SIZE
    rows = CAP * BLOCK
    maps = []
    for j in range(heads):
        owner = head ^ j
        maps.append(map_ref[pl.ds(pl.multiple_of(owner * width, width), width), :])
    for i in range(count):
        k = first + i
        live = live_ref[k : k + 1, :] > 0
        query = rows_to_heads(pay_refs[i][rows:, :].astype(jnp.float32))
        query = query * turn_ref[k : k + 1, :] + pltpu.roll(query, HEAD_SIZE // 2, 1) * turn_ref[
            pools + k : pools + k + 1, :
        ]
        queries = query.astype(jnp.bfloat16)
        at = slice(i * rows, (i + 1) * rows)
        rebuilt = jnp.dot(key_refs[0][at, :], maps[0], preferred_element_type=jnp.float32)
        for j in range(1, heads):
            rebuilt += jnp.dot(key_refs[j][at, :], maps[j], preferred_element_type=jnp.float32)
        cosine = cos_ref[k * rows : (k + 1) * rows, :]
        sine = sin_ref[k * rows : (k + 1) * rows, :]
        for g in range(groups):
            one = rebuilt[:, g * HEAD_SIZE : (g + 1) * HEAD_SIZE]
            turned = (one * cosine + pltpu.roll(one, HEAD_SIZE // 2, 1) * sine).astype(jnp.bfloat16)
            mine = slice(g * QUERY_PER_GROUP, (g + 1) * QUERY_PER_GROUP)
            scores = lax.dot_general(
                queries[mine, :], turned, (((1,), (1,)), ((), ())), preferred_element_type=jnp.float32
            ) * (HEAD_SIZE ** -0.5)
            out_refs[i][mine, :] = jnp.where(live, scores, MASKED)


def compact_kernel(pools, shard_blocks, sel_ref, *rest):
    value_refs = rest[:pools][::-1]
    out_ref, sem = rest[-2:]
    me = lax.axis_index("pool")
    place = jnp.int32(0)
    for k in range(pools):
        for c, block in enumerate(slot_blocks(sel_ref, me, me ^ k, shard_blocks)):
            @pl.when(block >= 0)
            def _(k=k, c=c, place=place):
                pltpu.make_async_copy(
                    value_refs[k].at[pl.ds(c * BLOCK, BLOCK), :],
                    out_ref.at[pl.ds(pl.multiple_of(place * BLOCK, BLOCK), BLOCK), :],
                    sem,
                ).start()
            place = place + (block >= 0).astype(jnp.int32)
    pltpu.make_async_copy(out_ref, out_ref, sem).wait()


def attend_kernel(pools, heads, chunks, map_ref, place_ref, *rest):
    score_refs = rest[:pools][::-1]
    value_refs = rest[pools : pools + heads * chunks]
    out_ref = rest[-1]
    head = lax.axis_index("heads")
    width = value_refs[0].shape[1]
    groups = map_ref.shape[1] // HEAD_SIZE
    scores = [ref[...] for ref in score_refs]
    top = functools.reduce(jnp.maximum, [jnp.max(s, axis=1, keepdims=True) for s in scores])
    weights = [jnp.exp(s - top) for s in scores]
    total = functools.reduce(jnp.add, [jnp.sum(w, axis=1, keepdims=True) for w in weights])
    slots = []
    for k in range(pools):
        attention = weights[k] / total
        for c in range(CAP):
            at = (k * CAP + c) * BLOCK
            slots.append((place_ref[:, at : at + BLOCK], attention[:, c * BLOCK : (c + 1) * BLOCK]))
    dense = []
    for i in range(value_refs[0].shape[0] // BLOCK):
        chosen = jnp.zeros_like(slots[0][1])
        for place, attention in slots:
            chosen = jnp.where(place == i, attention, chosen)
        dense.append(chosen)
    attention = jnp.concatenate(dense, axis=1).astype(jnp.bfloat16)
    mixed = [None] * groups
    for j in range(heads * chunks):
        owner = (head ^ (j // chunks)) * chunks + j % chunks
        context = jnp.dot(
            attention, value_refs[j][...], preferred_element_type=jnp.float32
        ).astype(jnp.bfloat16)
        rows = pl.ds(pl.multiple_of(owner * width, width), width)
        for g in range(groups):
            part = jnp.dot(
                context[g * QUERY_PER_GROUP : (g + 1) * QUERY_PER_GROUP, :],
                map_ref[rows, g * HEAD_SIZE : (g + 1) * HEAD_SIZE],
                preferred_element_type=jnp.float32,
            )
            mixed[g] = part if j == 0 else mixed[g] + part
    for g in range(groups):
        for q in range(QUERY_PER_GROUP):
            at = (g * QUERY_PER_GROUP + q) * HEAD_SIZE
            out_ref[:, at : at + HEAD_SIZE] = mixed[g][q : q + 1, :].astype(jnp.bfloat16)


def join_kernel(*refs):
    rows = [ref[...].reshape(-1, ref.shape[-1]).astype(jnp.float32) for ref in refs[:-1]]
    refs[-1][...] = jnp.concatenate(rows, axis=0).astype(jnp.bfloat16)


def project_kernel(pools, heads, reps, weight_ref, *rest):
    row_refs = rest[:pools][::-1]
    out_refs = rest[pools:-1]
    acc = rest[-1]
    left = jnp.concatenate([ref[...].astype(jnp.float32) for ref in row_refs], axis=0).astype(jnp.bfloat16)
    acc[...] = jnp.dot(left, weight_ref[...], preferred_element_type=jnp.float32)
    pool = lax.axis_index("pool")
    head = lax.axis_index("heads")
    each = pools // heads
    for d in range(heads * reps):
        for u in range(each):
            n = (pool ^ ((head ^ (d // reps)) * each + u)) * reps + d % reps
            out_refs[d][u : u + 1, :] = acc[pl.ds(n, 1), :]


def finish_kernel(heads, reps, *refs):
    out_ref = refs[-1]
    refs = refs[:-1][::-1]
    rep = lax.axis_index("rep")
    width = refs[0].shape[1]
    for t in range(reps):
        total = functools.reduce(jnp.add, [refs[j * reps + t][...] for j in range(heads)])
        columns = pl.ds(pl.multiple_of((rep ^ t) * width, width), width)
        out_ref[0, :, columns] = total.astype(jnp.bfloat16)


def per_device(queries, latents, key_latent_maps, value_latent_maps, out_weight, lengths, selected):
    pools = lax.axis_size("pool")
    heads = lax.axis_size("heads")
    reps = lax.axis_size("rep")
    half_seqs, sel_count = selected.shape[1:]
    assert half_seqs == pools and pools % heads == 0
    shard_blocks = latents.shape[2] // BLOCK
    width = latents.shape[3] // 2
    rows = CAP * BLOCK
    own_heads = queries.shape[2] // HEAD_SIZE
    bf16, f32, i32 = jnp.bfloat16, jnp.float32, jnp.int32
    shape = jax.ShapeDtypeStruct
    freq = jnp.asarray(frequencies())

    def join(*blocks):
        return pl.pallas_call(
            join_kernel,
            out_shape=shape((sum(block.size for block in blocks) // queries.shape[2], queries.shape[2]), bf16),
            in_specs=[VMEM] * len(blocks),
            out_specs=VMEM,
            compiler_params=params(4),
            name="join",
        )(*blocks)

    def exchange(value, axis, size):
        taken = {step: swap(value, axis, size, step) for step in range(size - 1, 0, -1)}
        return [value] + [taken[step] for step in range(1, size)]

    def scatter(blocks, axis, size):
        taken = {step: swap(blocks[step], axis, size, step) for step in range(size - 1, 0, -1)}
        return [blocks[0]] + [taken[step] for step in range(1, size)]

    middle = pools // 2
    chunks = max(1, width // (2 * LANE))
    query_rows = queries.shape[2] // (width // chunks)
    packed = pl.pallas_call(
        functools.partial(gather_kernel, pools),
        out_shape=[shape((middle * rows, width), bf16)] * 2
        + [shape((rows + query_rows, width // chunks), bf16)] * pools
        + [shape((rows, width // chunks), bf16)] * (pools * (chunks - 1)),
        in_specs=[SMEM, HBM, VMEM],
        out_specs=[VMEM] * (pools * chunks + 2),
        scratch_shapes=[
            pltpu.VMEM((pools * rows, 2 * width), bf16),
            pltpu.SemaphoreType.DMA((pools * CAP,)),
        ],
        compiler_params=params(16),
        name="gather",
    )(in_hbm(selected), in_hbm(latents), in_hbm(queries))
    near, far, values = packed[0], packed[1], packed[2:]
    far_parts = exchange(far, "heads", heads)
    near_parts = exchange(near, "heads", heads)

    later = values[pools * (chunks - 1) :]
    cosine, sine, turn, live, place, key_maps, value_maps, *later = pl.pallas_call(
        functools.partial(table_kernel, pools, shard_blocks),
        out_shape=[shape((pools * rows, HEAD_SIZE), f32)] * 2
        + [shape((2 * pools, HEAD_SIZE), f32), shape((pools, rows), i32), shape((1, pools * rows), i32)]
        + [shape(key_latent_maps.shape, bf16), shape(value_latent_maps.shape, bf16)]
        + [shape(block.shape, bf16) for block in later],
        in_specs=[SMEM, SMEM, VMEM] + [ANY] * (2 + pools),
        out_specs=[VMEM] * 7 + [ANY] * pools,
        scratch_shapes=[pltpu.SemaphoreType.DMA((2,))],
        input_output_aliases={5 + k: 7 + k for k in range(pools)},
        compiler_params=params(16),
        name="tables",
    )(
        in_hbm(selected), in_hbm(lengths), in_hbm(freq), in_hbm(key_latent_maps),
        in_hbm(value_latent_maps), *later,
    )
    values = [*values[: pools * (chunks - 1)], *later]
    value_parts = [scatter(values[c * pools : (c + 1) * pools], "pool", pools) for c in range(chunks)]

    def score(first, count, key_parts, after):
        pays = value_parts[0][first : first + count]
        return pl.pallas_call(
            functools.partial(score_kernel, first, count, heads, pools),
            out_shape=[shape((own_heads, rows), f32)] * count,
            in_specs=[VMEM] * 5 + [ANY] + [VMEM] * (heads + count),
            out_specs=[VMEM] * count,
            compiler_params=params(20),
            cost_estimate=pl.CostEstimate(flops=0, transcendentals=0, bytes_accessed=3 << 20),
            name="score",
        )(key_maps, cosine, sine, turn, live, after, *key_parts, *pays[::-1])

    def compact(parts, *after):
        return pl.pallas_call(
            functools.partial(compact_kernel, pools, shard_blocks),
            out_shape=shape((sel_count * BLOCK, width // chunks), bf16),
            in_specs=[SMEM] + [ANY] * (pools + len(after)),
            out_specs=ANY,
            scratch_shapes=[pltpu.SemaphoreType.DMA],
            compiler_params=params(8),
            cost_estimate=pl.CostEstimate(flops=0, transcendentals=0, bytes_accessed=3 << 20),
            name="compact",
        )(in_hbm(selected), *parts[::-1], *after)

    far_scores = score(middle, middle, far_parts, place)
    dense = []
    for c in range(chunks - 1):
        dense.append(compact(value_parts[c], far_scores[0]))
    near_scores = score(0, middle, near_parts, dense[0] if dense else far_scores[0])
    score_parts = scatter([*near_scores, *far_scores], "pool", pools)
    dense.append(compact(value_parts[-1], near_scores[0], *score_parts[middle:]))
    dense = [exchange(block, "heads", heads) for block in dense]
    dense_parts = [dense[c][j] for j in range(heads) for c in range(chunks)]

    mine = pl.pallas_call(
        functools.partial(attend_kernel, pools, heads, chunks),
        out_shape=shape((1, own_heads * HEAD_SIZE), bf16),
        in_specs=[VMEM] * (2 + pools + heads * chunks),
        out_specs=VMEM,
        compiler_params=params(16),
        name="attend",
    )(value_maps, place, *score_parts[::-1], *dense_parts)
    own_rows = join(*exchange(mine, "rep", reps))
    row_parts = exchange(own_rows, "pool", pools)

    own_columns = out_weight.shape[1]
    each = pools // heads
    parts = pl.pallas_call(
        functools.partial(project_kernel, pools, heads, reps),
        out_shape=[shape((each, own_columns), f32)] * (heads * reps),
        in_specs=[VMEM] * (pools + 1),
        out_specs=[VMEM] * (heads * reps),
        scratch_shapes=[pltpu.VMEM((pools * reps, own_columns), f32)],
        compiler_params=params(24),
        name="project",
    )(in_vmem(out_weight), *row_parts[::-1])
    return pl.pallas_call(
        functools.partial(finish_kernel, heads, reps),
        out_shape=shape((1, each, reps * own_columns), bf16),
        in_specs=[VMEM] * (heads * reps),
        out_specs=VMEM,
        compiler_params=params(4),
        name="finish",
    )(*scatter(parts, ("heads", "rep"), heads * reps)[::-1])


def solution(mesh):
    return jax.shard_map(
        per_device,
        mesh=mesh,
        in_specs=(
            P(("groups", "rep"), "pool", "heads"),
            P(("groups", "rep"), None, "pool", "heads"),
            P(None, "heads"),
            P(None, "heads"),
            P("heads", ("pool", "rep")),
            P(("groups", "rep"), None),
            P(("groups", "rep"), None, None),
        ),
        out_specs=P(("groups", "rep"), "heads", "pool"),
        check_vma=False,
    )
```

```python
import functools

import jax
import jax.numpy as jnp
import numpy as np
from jax import lax
from jax.experimental import pallas as pl
from jax.experimental.pallas import tpu as pltpu
from jax.sharding import PartitionSpec as P

HEAD_SIZE = 128
LANE = 64
BLOCK = 128
CAP = 2
QUERY_PER_GROUP = 8

ROPE_BASE = 500000.0
MASKED = -1e30
FAR = 1 << 29

SMEM = pl.BlockSpec(memory_space=pltpu.SMEM)
VMEM = pl.BlockSpec(memory_space=pltpu.VMEM)
ANY = pl.BlockSpec(memory_space=pl.ANY)
HBM = pl.BlockSpec(memory_space=pltpu.HBM)


def frequencies():
    half = HEAD_SIZE // 2
    exponents = np.arange(half, dtype=np.float32) * np.float32(2.0 / HEAD_SIZE)
    freq = np.power(np.float64(ROPE_BASE), -exponents.astype(np.float64)).astype(np.float32)
    return np.concatenate([freq, freq])[None, :]


def swap(value, axes, size, step):
    return lax.ppermute(value, axes, [(i, i ^ step) for i in range(size)])


def in_hbm(value):
    return pltpu.with_memory_space_constraint(value, pltpu.HBM)


def in_vmem(value):
    return pltpu.with_memory_space_constraint(value, pltpu.VMEM)


def params(mib, **more):
    return pltpu.CompilerParams(vmem_limit_bytes=mib << 20, **more)


def slot_blocks(sel_ref, seq, shard, shard_blocks):
    first = jnp.int32(-1)
    second = jnp.int32(-1)
    for i in range(sel_ref.shape[2]):
        block = sel_ref[0, seq, i]
        here = (block >= shard * shard_blocks) & (block < (shard + 1) * shard_blocks)
        second = jnp.where(here & (first >= 0), block, second)
        first = jnp.where(here & (first < 0), block, first)
    return first, second


def heads_to_rows(line, lanes):
    count = line.shape[1] // HEAD_SIZE
    rows = jnp.concatenate([line[:, n * HEAD_SIZE : (n + 1) * HEAD_SIZE] for n in range(count)], axis=0)
    if lanes < HEAD_SIZE:
        return jnp.concatenate([rows[:, i : i + lanes] for i in range(0, HEAD_SIZE, lanes)], axis=0)
    each = count * HEAD_SIZE // lanes
    return jnp.concatenate([rows[i : i + each, :] for i in range(0, count, each)], axis=1)


def rows_to_heads(rows):
    count, lanes = rows.shape
    if lanes < HEAD_SIZE:
        each = count * lanes // HEAD_SIZE
        return jnp.concatenate([rows[i : i + each, :] for i in range(0, count, each)], axis=1)
    return jnp.concatenate([rows[:, i : i + HEAD_SIZE] for i in range(0, lanes, HEAD_SIZE)], axis=0)


def gather_kernel(pools, sel_ref, lat_ref, query_ref, near_ref, far_ref, *rest):
    value_refs = rest[:-2]
    raw, sems = rest[-2:]
    shard_blocks = lat_ref.shape[2] // BLOCK
    columns = lat_ref.shape[3]
    width = columns // 2
    rows = CAP * BLOCK
    me = lax.axis_index("pool")
    copies = {}
    for k in range(pools - 1, -1, -1):
        seq = me ^ k
        for c, block in enumerate(slot_blocks(sel_ref, seq, me, shard_blocks)):
            local = jnp.maximum(block - me * shard_blocks, 0)
            copies[k, c] = pltpu.make_async_copy(
                lat_ref.at[0, seq, pl.ds(pl.multiple_of(local * BLOCK, BLOCK), BLOCK), :],
                raw.at[pl.ds((k * CAP + c) * BLOCK, BLOCK), :],
                sems.at[k * CAP + c],
            )
            copies[k, c].start()
    queries = heads_to_rows(query_ref[0].astype(jnp.float32), value_refs[0].shape[1]).astype(jnp.bfloat16)
    chunk = min(4 * LANE, columns)
    half = chunk // 2
    source = lax.broadcasted_iota(jnp.int32, (chunk, chunk), 0)
    target = lax.broadcasted_iota(jnp.int32, (chunk, chunk), 1)
    within = target & (half - 1)
    wanted = ((within >> 6) << 7) + (within & (LANE - 1)) + jnp.where(target >= half, LANE, 0)
    pick = (source == wanted).astype(jnp.float32).astype(jnp.bfloat16)
    for k in range(pools - 1, -1, -1):
        for c in range(CAP):
            copies[k, c].wait()
        keys_ref, at = (far_ref, k - pools // 2) if k >= pools // 2 else (near_ref, k)
        for j in range(columns // chunk):
            packed = jnp.dot(
                raw[k * rows : (k + 1) * rows, j * chunk : (j + 1) * chunk], pick,
                preferred_element_type=jnp.float32,
            ).astype(jnp.bfloat16)
            keys_ref[at * rows : (at + 1) * rows, j * half : (j + 1) * half] = packed[:, :half]
            value_refs[k][:rows, j * half : (j + 1) * half] = packed[:, half:]
        value_refs[k][rows:, :] = queries


def table_kernel(pools, shard_blocks, sel_ref, len_ref, freq_ref, key_map_ref, value_map_ref, held_ref, *rest):
    cos_ref, sin_ref, turn_ref, live_ref, place_ref, key_out_ref, value_out_ref = rest[:7]
    sems = rest[-1]
    loads = [
        pltpu.make_async_copy(key_map_ref, key_out_ref, sems.at[0]),
        pltpu.make_async_copy(value_map_ref, value_out_ref, sems.at[1]),
    ]
    for load in loads:
        load.start()
    me = lax.axis_index("pool")
    lane = lax.broadcasted_iota(jnp.int32, (BLOCK, HEAD_SIZE), 1)
    row = lax.broadcasted_iota(jnp.int32, (BLOCK, HEAD_SIZE), 0)
    front = lane < HEAD_SIZE // 2
    across = lax.broadcasted_iota(jnp.int32, (1, BLOCK), 1)
    place = jnp.int32(0)
    for k in range(pools):
        turn_ref[k : k + 1, :] = len_ref[0, me ^ k].astype(jnp.float32) * freq_ref[...]
    angle = turn_ref[0:pools, :]
    turn_ref[0:pools, :] = jnp.cos(angle)
    turn_ref[pools:, :] = jnp.where(front[:1, :], -jnp.sin(angle), jnp.sin(angle))
    for k in range(pools):
        seq = me ^ k
        found = slot_blocks(sel_ref, seq, me, shard_blocks)
        one, two = [jnp.maximum(block, 0) * BLOCK for block in found]
        angle = (jnp.where(front, one, two) + row).astype(jnp.float32) * freq_ref[...]
        for ref, table, sign in ((cos_ref, jnp.cos(angle), 1.0), (sin_ref, jnp.sin(angle), -1.0)):
            turned = pltpu.roll(table, HEAD_SIZE // 2, 1)
            at = k * CAP * BLOCK
            ref[at : at + BLOCK, :] = jnp.where(front, sign * table, turned)
            ref[at + BLOCK : at + 2 * BLOCK, :] = jnp.where(front, sign * turned, table)
        mine = slot_blocks(sel_ref, me, seq, shard_blocks)
        for c in range(CAP):
            start = jnp.where(found[c] < 0, FAR, found[c] * BLOCK)
            live_ref[k : k + 1, c * BLOCK : (c + 1) * BLOCK] = (start + across < len_ref[0, seq]).astype(jnp.int32)
            at = (k * CAP + c) * BLOCK
            used = mine[c] >= 0
            place_ref[:, at : at + BLOCK] = jnp.where(used, place, -1) + 0 * across
            place = place + used.astype(jnp.int32)
    for load in loads:
        load.wait()


def score_kernel(first, count, heads, pools, map_ref, cos_ref, sin_ref, turn_ref, live_ref, after_ref, *rest):
    del after_ref
    key_refs = rest[:heads]
    pay_refs = rest[heads : heads + count][::-1]
    out_refs = rest[heads + count :]
    head = lax.axis_index("heads")
    width = key_refs[0].shape[1]
    groups = map_ref.shape[1] // HEAD_SIZE
    rows = CAP * BLOCK
    maps = []
    for j in range(heads):
        owner = head ^ j
        maps.append(map_ref[pl.ds(pl.multiple_of(owner * width, width), width), :])
    for i in range(count):
        k = first + i
        live = live_ref[k : k + 1, :] > 0
        query = rows_to_heads(pay_refs[i][rows:, :].astype(jnp.float32))
        query = query * turn_ref[k : k + 1, :] + pltpu.roll(query, HEAD_SIZE // 2, 1) * turn_ref[
            pools + k : pools + k + 1, :
        ]
        queries = query.astype(jnp.bfloat16)
        at = slice(i * rows, (i + 1) * rows)
        rebuilt = jnp.dot(key_refs[0][at, :], maps[0], preferred_element_type=jnp.float32)
        for j in range(1, heads):
            rebuilt += jnp.dot(key_refs[j][at, :], maps[j], preferred_element_type=jnp.float32)
        cosine = cos_ref[k * rows : (k + 1) * rows, :]
        sine = sin_ref[k * rows : (k + 1) * rows, :]
        for g in range(groups):
            one = rebuilt[:, g * HEAD_SIZE : (g + 1) * HEAD_SIZE]
            turned = (one * cosine + pltpu.roll(one, HEAD_SIZE // 2, 1) * sine).astype(jnp.bfloat16)
            mine = slice(g * QUERY_PER_GROUP, (g + 1) * QUERY_PER_GROUP)
            scores = lax.dot_general(
                queries[mine, :], turned, (((1,), (1,)), ((), ())), preferred_element_type=jnp.float32
            ) * (HEAD_SIZE ** -0.5)
            out_refs[i][mine, :] = jnp.where(live, scores, MASKED)


def compact_kernel(pools, place_ref, after_ref, *rest):
    del after_ref
    value_refs = rest[:pools][::-1]
    out_ref = rest[pools]
    width = out_ref.shape[1]
    spare = pools * CAP - out_ref.shape[0] // BLOCK
    for i in range(out_ref.shape[0] // BLOCK):
        chosen = jnp.zeros((BLOCK, width), jnp.float32)
        for slot in range(i, i + spare + 1):
            place = place_ref[:, slot * BLOCK : slot * BLOCK + LANE]
            place = jnp.concatenate([place] * (width // LANE), axis=1)
            k, c = slot // CAP, slot % CAP
            block = value_refs[k][c * BLOCK : (c + 1) * BLOCK, :].astype(jnp.float32)
            chosen = jnp.where(place == i, block, chosen)
        out_ref[i * BLOCK : (i + 1) * BLOCK, :] = chosen.astype(jnp.bfloat16)


def attend_kernel(pools, heads, map_ref, place_ref, *rest):
    score_refs = rest[:pools][::-1]
    value_refs = rest[pools : pools + heads]
    out_ref = rest[-1]
    head = lax.axis_index("heads")
    width = value_refs[0].shape[1]
    groups = map_ref.shape[1] // HEAD_SIZE
    scores = [ref[...] for ref in score_refs]
    top = functools.reduce(jnp.maximum, [jnp.max(s, axis=1, keepdims=True) for s in scores])
    weights = [jnp.exp(s - top) for s in scores]
    total = functools.reduce(jnp.add, [jnp.sum(w, axis=1, keepdims=True) for w in weights])
    slots = []
    for k in range(pools):
        attention = weights[k] / total
        for c in range(CAP):
            at = (k * CAP + c) * BLOCK
            slots.append((place_ref[:, at : at + BLOCK], attention[:, c * BLOCK : (c + 1) * BLOCK]))
    dense = []
    kept = value_refs[0].shape[0] // BLOCK
    for i in range(kept):
        chosen = jnp.zeros_like(slots[0][1])
        for place, attention in slots[i : i + len(slots) - kept + 1]:
            chosen = jnp.where(place == i, attention, chosen)
        dense.append(chosen)
    attention = jnp.concatenate(dense, axis=1).astype(jnp.bfloat16)
    mixed = [None] * groups
    for j in range(heads):
        owner = head ^ j
        context = jnp.dot(
            attention, value_refs[j][...], preferred_element_type=jnp.float32
        ).astype(jnp.bfloat16)
        rows = pl.ds(pl.multiple_of(owner * width, width), width)
        for g in range(groups):
            part = jnp.dot(
                context[g * QUERY_PER_GROUP : (g + 1) * QUERY_PER_GROUP, :],
                map_ref[rows, g * HEAD_SIZE : (g + 1) * HEAD_SIZE],
                preferred_element_type=jnp.float32,
            )
            mixed[g] = part if j == 0 else mixed[g] + part
    for g in range(groups):
        for q in range(QUERY_PER_GROUP):
            at = (g * QUERY_PER_GROUP + q) * HEAD_SIZE
            out_ref[:, at : at + HEAD_SIZE] = mixed[g][q : q + 1, :].astype(jnp.bfloat16)


def join_kernel(*refs):
    rows = [ref[...].reshape(-1, ref.shape[-1]).astype(jnp.float32) for ref in refs[:-1]]
    refs[-1][...] = jnp.concatenate(rows, axis=0).astype(jnp.bfloat16)


def project_kernel(pools, heads, reps, weight_ref, *rest):
    row_refs = rest[:pools][::-1]
    out_refs = rest[pools:-1]
    acc = rest[-1]
    left = jnp.concatenate([ref[...].astype(jnp.float32) for ref in row_refs], axis=0).astype(jnp.bfloat16)
    acc[...] = jnp.dot(left, weight_ref[...], preferred_element_type=jnp.float32)
    pool = lax.axis_index("pool")
    head = lax.axis_index("heads")
    each = pools // heads
    for d in range(heads * reps):
        for u in range(each):
            n = (pool ^ ((head ^ (d // reps)) * each + u)) * reps + d % reps
            out_refs[d][u : u + 1, :] = acc[pl.ds(n, 1), :]


def finish_kernel(heads, reps, *refs):
    out_ref = refs[-1]
    refs = refs[:-1][::-1]
    rep = lax.axis_index("rep")
    width = refs[0].shape[1]
    for t in range(reps):
        total = functools.reduce(jnp.add, [refs[j * reps + t][...] for j in range(heads)])
        columns = pl.ds(pl.multiple_of((rep ^ t) * width, width), width)
        out_ref[0, :, columns] = total.astype(jnp.bfloat16)


def per_device(queries, latents, key_latent_maps, value_latent_maps, out_weight, lengths, selected):
    pools = lax.axis_size("pool")
    heads = lax.axis_size("heads")
    reps = lax.axis_size("rep")
    half_seqs, sel_count = selected.shape[1:]
    assert half_seqs == pools and pools % heads == 0
    shard_blocks = latents.shape[2] // BLOCK
    width = latents.shape[3] // 2
    rows = CAP * BLOCK
    own_heads = queries.shape[2] // HEAD_SIZE
    bf16, f32, i32 = jnp.bfloat16, jnp.float32, jnp.int32
    shape = jax.ShapeDtypeStruct
    freq = jnp.asarray(frequencies())

    def join(*blocks):
        return pl.pallas_call(
            join_kernel,
            out_shape=shape((sum(block.size for block in blocks) // queries.shape[2], queries.shape[2]), bf16),
            in_specs=[VMEM] * len(blocks),
            out_specs=VMEM,
            compiler_params=params(4),
            name="join",
        )(*blocks)

    def exchange(value, axis, size):
        taken = {step: swap(value, axis, size, step) for step in range(size - 1, 0, -1)}
        return [value] + [taken[step] for step in range(1, size)]

    def scatter(blocks, axis, size):
        taken = {step: swap(blocks[step], axis, size, step) for step in range(size - 1, 0, -1)}
        return [blocks[0]] + [taken[step] for step in range(1, size)]

    middle = pools // 2
    query_rows = queries.shape[2] // width
    packed = pl.pallas_call(
        functools.partial(gather_kernel, pools),
        out_shape=[shape((middle * rows, width), bf16)] * 2
        + [shape((rows + query_rows, width), bf16)] * pools,
        in_specs=[SMEM, HBM, VMEM],
        out_specs=[VMEM] * (pools + 2),
        scratch_shapes=[
            pltpu.VMEM((pools * rows, 2 * width), bf16),
            pltpu.SemaphoreType.DMA((pools * CAP,)),
        ],
        compiler_params=params(16),
        name="gather",
    )(in_hbm(selected), in_hbm(latents), in_hbm(queries))
    near, far, values = packed[0], packed[1], packed[2:]
    far_parts = exchange(far, "heads", heads)
    near_parts = exchange(near, "heads", heads)

    cosine, sine, turn, live, place, key_maps, value_maps, held = pl.pallas_call(
        functools.partial(table_kernel, pools, shard_blocks),
        out_shape=[shape((pools * rows, HEAD_SIZE), f32)] * 2
        + [shape((2 * pools, HEAD_SIZE), f32), shape((pools, rows), i32), shape((1, pools * rows), i32)]
        + [shape(key_latent_maps.shape, bf16), shape(value_latent_maps.shape, bf16)]
        + [shape(values[1].shape, bf16)],
        in_specs=[SMEM, SMEM, VMEM] + [ANY] * 3,
        out_specs=[VMEM] * 7 + [ANY],
        scratch_shapes=[pltpu.SemaphoreType.DMA((2,))],
        input_output_aliases={5: 7},
        compiler_params=params(16),
        cost_estimate=pl.CostEstimate(flops=0, transcendentals=0, bytes_accessed=10 << 20),
        name="tables",
    )(
        in_hbm(selected), in_hbm(lengths), in_hbm(freq), in_hbm(key_latent_maps),
        in_hbm(value_latent_maps), values[1],
    )
    value_parts = scatter([values[0], held, *values[2:]], "pool", pools)

    def score(first, count, key_parts, after):
        pays = value_parts[first : first + count]
        return pl.pallas_call(
            functools.partial(score_kernel, first, count, heads, pools),
            out_shape=[shape((own_heads, rows), f32)] * count,
            in_specs=[VMEM] * 5 + [ANY] + [VMEM] * (heads + count),
            out_specs=[VMEM] * count,
            compiler_params=params(20),
            cost_estimate=pl.CostEstimate(flops=0, transcendentals=0, bytes_accessed=3 << 20),
            name="score",
        )(key_maps, cosine, sine, turn, live, after, *key_parts, *pays[::-1])

    far_scores = score(middle, middle, far_parts, place)
    dense = pl.pallas_call(
        functools.partial(compact_kernel, pools),
        out_shape=shape((sel_count * BLOCK, width), bf16),
        in_specs=[VMEM, ANY] + [VMEM] * pools,
        out_specs=VMEM,
        compiler_params=params(16),
        cost_estimate=pl.CostEstimate(flops=0, transcendentals=0, bytes_accessed=3 << 20),
        name="compact",
    )(place, far_scores[0], *value_parts[::-1])
    near_scores = score(0, middle, near_parts, dense)
    dense_parts = exchange(dense, "heads", heads)
    score_parts = scatter([*near_scores, *far_scores], "pool", pools)

    mine = pl.pallas_call(
        functools.partial(attend_kernel, pools, heads),
        out_shape=shape((1, own_heads * HEAD_SIZE), bf16),
        in_specs=[VMEM] * (2 + pools + heads),
        out_specs=VMEM,
        compiler_params=params(16),
        name="attend",
    )(value_maps, place, *score_parts[::-1], *dense_parts)
    own_rows = join(*exchange(mine, "rep", reps))
    row_parts = exchange(own_rows, "pool", pools)

    own_columns = out_weight.shape[1]
    each = pools // heads
    parts = pl.pallas_call(
        functools.partial(project_kernel, pools, heads, reps),
        out_shape=[shape((each, own_columns), f32)] * (heads * reps),
        in_specs=[VMEM] * (pools + 1),
        out_specs=[VMEM] * (heads * reps),
        scratch_shapes=[pltpu.VMEM((pools * reps, own_columns), f32)],
        compiler_params=params(24),
        name="project",
    )(in_vmem(out_weight), *row_parts[::-1])
    return pl.pallas_call(
        functools.partial(finish_kernel, heads, reps),
        out_shape=shape((1, each, reps * own_columns), bf16),
        in_specs=[VMEM] * (heads * reps),
        out_specs=VMEM,
        compiler_params=params(4),
        name="finish",
    )(*scatter(parts, ("heads", "rep"), heads * reps)[::-1])


def solution(mesh):
    return jax.shard_map(
        per_device,
        mesh=mesh,
        in_specs=(
            P(("groups", "rep"), "pool", "heads"),
            P(("groups", "rep"), None, "pool", "heads"),
            P(None, "heads"),
            P(None, "heads"),
            P("heads", ("pool", "rep")),
            P(("groups", "rep"), None),
            P(("groups", "rep"), None, None),
        ),
        out_specs=P(("groups", "rep"), "heads", "pool"),
        check_vma=False,
    )
```

```python
import functools

import jax
import jax.numpy as jnp
import numpy as np
from jax import lax
from jax.experimental import pallas as pl
from jax.experimental.pallas import tpu as pltpu
from jax.sharding import PartitionSpec as P

HEAD_SIZE = 128
LANE = 64
BLOCK = 128
CAP = 2
QUERY_PER_GROUP = 8

ROPE_BASE = 500000.0
MASKED = -1e30
FAR = 1 << 29

SMEM = pl.BlockSpec(memory_space=pltpu.SMEM)
VMEM = pl.BlockSpec(memory_space=pltpu.VMEM)
ANY = pl.BlockSpec(memory_space=pl.ANY)
HBM = pl.BlockSpec(memory_space=pltpu.HBM)


def rotary_tables(blocks):
    half = HEAD_SIZE // 2
    exponents = np.arange(half, dtype=np.float32) * np.float32(2.0 / HEAD_SIZE)
    freq = np.power(np.float64(ROPE_BASE), -exponents.astype(np.float64)).astype(np.float32)
    freq = np.concatenate([freq, freq]).astype(np.float64)[None, :]
    coarse = np.arange(-(-(blocks + 1) // 8) * 8)[:, None] * BLOCK * freq
    fine = np.arange(BLOCK)[:, None] * freq
    return [f(angle).astype(np.float32) for angle in (coarse, fine) for f in (np.cos, np.sin)]


def swap(value, axes, size, step):
    return lax.ppermute(value, axes, [(i, i ^ step) for i in range(size)])


def in_hbm(value):
    return pltpu.with_memory_space_constraint(value, pltpu.HBM)


def in_vmem(value):
    return pltpu.with_memory_space_constraint(value, pltpu.VMEM)


def params(mib, **more):
    return pltpu.CompilerParams(vmem_limit_bytes=mib << 20, **more)


def slot_blocks(sel_ref, seq, shard, shard_blocks):
    first = jnp.int32(-1)
    second = jnp.int32(-1)
    for i in range(sel_ref.shape[2]):
        block = sel_ref[0, seq, i]
        here = (block >= shard * shard_blocks) & (block < (shard + 1) * shard_blocks)
        second = jnp.where(here & (first >= 0), block, second)
        first = jnp.where(here & (first < 0), block, first)
    return first, second


def heads_to_rows(line, lanes):
    count = line.shape[1] // HEAD_SIZE
    rows = jnp.concatenate([line[:, n * HEAD_SIZE : (n + 1) * HEAD_SIZE] for n in range(count)], axis=0)
    if lanes < HEAD_SIZE:
        return jnp.concatenate([rows[:, i : i + lanes] for i in range(0, HEAD_SIZE, lanes)], axis=0)
    each = count * HEAD_SIZE // lanes
    return jnp.concatenate([rows[i : i + each, :] for i in range(0, count, each)], axis=1)


def rows_to_heads(rows):
    count, lanes = rows.shape
    if lanes < HEAD_SIZE:
        each = count * lanes // HEAD_SIZE
        return jnp.concatenate([rows[i : i + each, :] for i in range(0, count, each)], axis=1)
    return jnp.concatenate([rows[:, i : i + HEAD_SIZE] for i in range(0, lanes, HEAD_SIZE)], axis=0)


def gather_kernel(pools, sel_ref, lat_ref, query_ref, near_ref, far_ref, *rest):
    value_refs = rest[:-2]
    raw, sems = rest[-2:]
    shard_blocks = lat_ref.shape[2] // BLOCK
    columns = lat_ref.shape[3]
    width = columns // 2
    rows = CAP * BLOCK
    me = lax.axis_index("pool")
    copies = {}
    for k in range(pools - 1, -1, -1):
        seq = me ^ k
        for c, block in enumerate(slot_blocks(sel_ref, seq, me, shard_blocks)):
            local = jnp.maximum(block - me * shard_blocks, 0)
            copies[k, c] = pltpu.make_async_copy(
                lat_ref.at[0, seq, pl.ds(pl.multiple_of(local * BLOCK, BLOCK), BLOCK), :],
                raw.at[pl.ds((k * CAP + c) * BLOCK, BLOCK), :],
                sems.at[k * CAP + c],
            )
            copies[k, c].start()
    queries = heads_to_rows(query_ref[0].astype(jnp.float32), value_refs[0].shape[1]).astype(jnp.bfloat16)
    chunk = min(4 * LANE, columns)
    half = chunk // 2
    source = lax.broadcasted_iota(jnp.int32, (chunk, chunk), 0)
    target = lax.broadcasted_iota(jnp.int32, (chunk, chunk), 1)
    within = target & (half - 1)
    wanted = ((within >> 6) << 7) + (within & (LANE - 1)) + jnp.where(target >= half, LANE, 0)
    pick = (source == wanted).astype(jnp.float32).astype(jnp.bfloat16)
    for copy in copies.values():
        copy.wait()
    for k in range(pools - 1, -1, -1):
        keys_ref, at = (far_ref, k - pools // 2) if k >= pools // 2 else (near_ref, k)
        for j in range(columns // chunk):
            packed = jnp.dot(
                raw[k * rows : (k + 1) * rows, j * chunk : (j + 1) * chunk], pick,
                preferred_element_type=jnp.float32,
            ).astype(jnp.bfloat16)
            keys_ref[at * rows : (at + 1) * rows, j * half : (j + 1) * half] = packed[:, :half]
            value_refs[k][:rows, j * half : (j + 1) * half] = packed[:, half:]
        value_refs[k][rows:, :] = queries


def table_kernel(
    pools, shard_blocks, sel_ref, len_ref, coarse_cos_ref, coarse_sin_ref, fine_cos_ref, fine_sin_ref,
    key_map_ref, value_map_ref, *rest,
):
    cos_ref, sin_ref, turn_ref, live_ref, place_ref, key_out_ref, value_out_ref = rest[2:9]
    sems = rest[-1]
    loads = [
        pltpu.make_async_copy(key_map_ref, key_out_ref, sems.at[0]),
        pltpu.make_async_copy(value_map_ref, value_out_ref, sems.at[1]),
    ]
    for load in loads:
        load.start()
    me = lax.axis_index("pool")
    front = lax.broadcasted_iota(jnp.int32, (1, HEAD_SIZE), 1) < HEAD_SIZE // 2
    across = lax.broadcasted_iota(jnp.int32, (1, BLOCK), 1)

    def turned(block, fine_cos, fine_sin):
        coarse_cos = coarse_cos_ref[pl.ds(block, 1), :]
        coarse_sin = coarse_sin_ref[pl.ds(block, 1), :]
        sine = coarse_sin * fine_cos + coarse_cos * fine_sin
        return coarse_cos * fine_cos - coarse_sin * fine_sin, jnp.where(front, -sine, sine)

    place = jnp.int32(0)
    for k in range(pools):
        seq = me ^ k
        length = len_ref[0, seq]
        rest_of = length & (BLOCK - 1)
        cosine, sine = turned(
            length >> 7, fine_cos_ref[pl.ds(rest_of, 1), :], fine_sin_ref[pl.ds(rest_of, 1), :]
        )
        turn_ref[k : k + 1, :] = cosine
        turn_ref[pools + k : pools + k + 1, :] = sine
        found = slot_blocks(sel_ref, seq, me, shard_blocks)
        mine = slot_blocks(sel_ref, me, seq, shard_blocks)
        for c in range(CAP):
            at = (k * CAP + c) * BLOCK
            cosine, sine = turned(jnp.maximum(found[c], 0), fine_cos_ref[...], fine_sin_ref[...])
            cos_ref[at : at + BLOCK, :] = cosine
            sin_ref[at : at + BLOCK, :] = sine
            start = jnp.where(found[c] < 0, FAR, found[c] * BLOCK)
            live_ref[k : k + 1, c * BLOCK : (c + 1) * BLOCK] = (start + across < length).astype(jnp.int32)
            used = mine[c] >= 0
            place_ref[:, at : at + BLOCK] = jnp.where(used, place, -1) + 0 * across
            place = place + used.astype(jnp.int32)
    for load in loads:
        load.wait()


def score_kernel(first, count, heads, pools, map_ref, cos_ref, sin_ref, turn_ref, live_ref, after_ref, *rest):
    del after_ref
    pay_refs = rest[:count][::-1]
    key_refs = rest[count : count + heads]
    out_refs = rest[heads + count :]
    head = lax.axis_index("heads")
    width = key_refs[0].shape[1]
    groups = map_ref.shape[1] // HEAD_SIZE
    rows = CAP * BLOCK
    maps = []
    for j in range(heads):
        owner = head ^ j
        maps.append(map_ref[pl.ds(pl.multiple_of(owner * width, width), width), :])
    for i in range(count):
        k = first + i
        live = live_ref[k : k + 1, :] > 0
        query = rows_to_heads(pay_refs[i][rows:, :].astype(jnp.float32))
        query = query * turn_ref[k : k + 1, :] + pltpu.roll(query, HEAD_SIZE // 2, 1) * turn_ref[
            pools + k : pools + k + 1, :
        ]
        queries = query.astype(jnp.bfloat16)
        at = slice(i * rows, (i + 1) * rows)
        rebuilt = jnp.dot(key_refs[0][at, :], maps[0], preferred_element_type=jnp.float32)
        for j in range(1, heads):
            rebuilt += jnp.dot(key_refs[j][at, :], maps[j], preferred_element_type=jnp.float32)
        cosine = cos_ref[k * rows : (k + 1) * rows, :]
        sine = sin_ref[k * rows : (k + 1) * rows, :]
        for g in range(groups):
            one = rebuilt[:, g * HEAD_SIZE : (g + 1) * HEAD_SIZE]
            turned = (one * cosine + pltpu.roll(one, HEAD_SIZE // 2, 1) * sine).astype(jnp.bfloat16)
            mine = slice(g * QUERY_PER_GROUP, (g + 1) * QUERY_PER_GROUP)
            scores = lax.dot_general(
                queries[mine, :], turned, (((1,), (1,)), ((), ())), preferred_element_type=jnp.float32
            ) * (HEAD_SIZE ** -0.5)
            out_refs[i][mine, :] = jnp.where(live, scores, MASKED)


def compact_kernel(pools, place_ref, after_ref, *rest):
    del after_ref
    value_refs = rest[:pools][::-1]
    out_ref = rest[pools]
    width = out_ref.shape[1]
    spare = pools * CAP - out_ref.shape[0] // BLOCK
    for i in range(out_ref.shape[0] // BLOCK):
        chosen = jnp.zeros((BLOCK, width), jnp.float32)
        for slot in range(i, i + spare + 1):
            place = place_ref[:, slot * BLOCK : slot * BLOCK + LANE]
            place = jnp.concatenate([place] * (width // LANE), axis=1)
            k, c = slot // CAP, slot % CAP
            block = value_refs[k][c * BLOCK : (c + 1) * BLOCK, :].astype(jnp.float32)
            chosen = jnp.where(place == i, block, chosen)
        out_ref[i * BLOCK : (i + 1) * BLOCK, :] = chosen.astype(jnp.bfloat16)


def attend_kernel(pools, heads, map_ref, place_ref, *rest):
    score_refs = rest[:pools][::-1]
    value_refs = rest[pools : pools + heads]
    out_ref = rest[-1]
    head = lax.axis_index("heads")
    width = value_refs[0].shape[1]
    groups = map_ref.shape[1] // HEAD_SIZE
    scores = [ref[...] for ref in score_refs]
    top = functools.reduce(jnp.maximum, [jnp.max(s, axis=1, keepdims=True) for s in scores])
    weights = [jnp.exp(s - top) for s in scores]
    total = functools.reduce(jnp.add, [jnp.sum(w, axis=1, keepdims=True) for w in weights])
    slots = []
    for k in range(pools):
        attention = weights[k] / total
        for c in range(CAP):
            at = (k * CAP + c) * BLOCK
            slots.append((place_ref[:, at : at + BLOCK], attention[:, c * BLOCK : (c + 1) * BLOCK]))
    dense = []
    kept = value_refs[0].shape[0] // BLOCK
    for i in range(kept):
        chosen = jnp.zeros_like(slots[0][1])
        for place, attention in slots[i : i + len(slots) - kept + 1]:
            chosen = jnp.where(place == i, attention, chosen)
        dense.append(chosen)
    attention = jnp.concatenate(dense, axis=1).astype(jnp.bfloat16)
    mixed = [None] * groups
    for j in range(heads):
        owner = head ^ j
        context = jnp.dot(
            attention, value_refs[j][...], preferred_element_type=jnp.float32
        ).astype(jnp.bfloat16)
        rows = pl.ds(pl.multiple_of(owner * width, width), width)
        for g in range(groups):
            part = jnp.dot(
                context[g * QUERY_PER_GROUP : (g + 1) * QUERY_PER_GROUP, :],
                map_ref[rows, g * HEAD_SIZE : (g + 1) * HEAD_SIZE],
                preferred_element_type=jnp.float32,
            )
            mixed[g] = part if j == 0 else mixed[g] + part
    for g in range(groups):
        for q in range(QUERY_PER_GROUP):
            at = (g * QUERY_PER_GROUP + q) * HEAD_SIZE
            out_ref[:, at : at + HEAD_SIZE] = mixed[g][q : q + 1, :].astype(jnp.bfloat16)


def join_kernel(*refs):
    rows = [ref[...].reshape(-1, ref.shape[-1]).astype(jnp.float32) for ref in refs[:-1]]
    refs[-1][...] = jnp.concatenate(rows, axis=0).astype(jnp.bfloat16)


def project_kernel(pools, heads, reps, weight_ref, *rest):
    row_refs = rest[:pools][::-1]
    out_refs = rest[pools:-1]
    acc = rest[-1]
    left = jnp.concatenate([ref[...].astype(jnp.float32) for ref in row_refs], axis=0).astype(jnp.bfloat16)
    acc[...] = jnp.dot(left, weight_ref[...], preferred_element_type=jnp.float32)
    pool = lax.axis_index("pool")
    head = lax.axis_index("heads")
    each = pools // heads
    for d in range(heads * reps):
        for u in range(each):
            n = (pool ^ ((head ^ (d // reps)) * each + u)) * reps + d % reps
            out_refs[d][u : u + 1, :] = acc[pl.ds(n, 1), :]


def finish_kernel(heads, reps, *refs):
    out_ref = refs[-1]
    refs = refs[:-1][::-1]
    rep = lax.axis_index("rep")
    width = refs[0].shape[1]
    for t in range(reps):
        total = functools.reduce(jnp.add, [refs[j * reps + t][...] for j in range(heads)])
        columns = pl.ds(pl.multiple_of((rep ^ t) * width, width), width)
        out_ref[0, :, columns] = total.astype(jnp.bfloat16)


def per_device(queries, latents, key_latent_maps, value_latent_maps, out_weight, lengths, selected):
    pools = lax.axis_size("pool")
    heads = lax.axis_size("heads")
    reps = lax.axis_size("rep")
    half_seqs, sel_count = selected.shape[1:]
    assert half_seqs == pools and pools % heads == 0
    shard_blocks = latents.shape[2] // BLOCK
    width = latents.shape[3] // 2
    rows = CAP * BLOCK
    own_heads = queries.shape[2] // HEAD_SIZE
    bf16, f32, i32 = jnp.bfloat16, jnp.float32, jnp.int32
    shape = jax.ShapeDtypeStruct
    constants = [jnp.asarray(table) for table in rotary_tables(shard_blocks * pools)]

    def join(*blocks):
        return pl.pallas_call(
            join_kernel,
            out_shape=shape((sum(block.size for block in blocks) // queries.shape[2], queries.shape[2]), bf16),
            in_specs=[VMEM] * len(blocks),
            out_specs=VMEM,
            compiler_params=params(4),
            name="join",
        )(*blocks)

    def exchange(value, axis, size):
        taken = {step: swap(value, axis, size, step) for step in range(size - 1, 0, -1)}
        return [value] + [taken[step] for step in range(1, size)]

    def scatter(blocks, axis, size):
        taken = {step: swap(blocks[step], axis, size, step) for step in range(size - 1, 0, -1)}
        return [blocks[0]] + [taken[step] for step in range(1, size)]

    middle = pools // 2
    query_rows = queries.shape[2] // width
    packed = pl.pallas_call(
        functools.partial(gather_kernel, pools),
        out_shape=[shape((middle * rows, width), bf16)] * 2
        + [shape((rows + query_rows, width), bf16)] * pools,
        in_specs=[SMEM, HBM, VMEM],
        out_specs=[VMEM] * (pools + 2),
        scratch_shapes=[
            pltpu.VMEM((pools * rows, 2 * width), bf16),
            pltpu.SemaphoreType.DMA((pools * CAP,)),
        ],
        compiler_params=params(16),
        name="gather",
    )(in_hbm(selected), in_hbm(latents), in_hbm(queries))
    near, far, values = packed[0], packed[1], packed[2:]

    passed = [values[1], near]
    cosine, sine, turn, live, place, key_maps, value_maps, *passed = pl.pallas_call(
        functools.partial(table_kernel, pools, shard_blocks),
        out_shape=[shape((pools * rows, HEAD_SIZE), f32)] * 2
        + [shape((2 * pools, HEAD_SIZE), f32), shape((pools, rows), i32), shape((1, pools * rows), i32)]
        + [shape(key_latent_maps.shape, bf16), shape(value_latent_maps.shape, bf16)]
        + [shape(block.shape, bf16) for block in passed],
        in_specs=[SMEM, SMEM] + [VMEM] * 4 + [ANY] * 4,
        out_specs=[VMEM] * 7 + [ANY] * 2,
        scratch_shapes=[pltpu.SemaphoreType.DMA((2,))],
        input_output_aliases={8 + i: 7 + i for i in range(2)},
        compiler_params=params(16),
        cost_estimate=pl.CostEstimate(flops=0, transcendentals=0, bytes_accessed=5 << 20),
        name="tables",
    )(
        in_hbm(selected), in_hbm(lengths), *[in_hbm(table) for table in constants],
        in_hbm(key_latent_maps), in_hbm(value_latent_maps), *passed,
    )
    held, near = passed
    value_parts = scatter([values[0], held, *values[2:]], "pool", pools)
    far_parts = exchange(far, "heads", heads)
    near_parts = exchange(near, "heads", heads)

    def score(first, count, key_parts, after):
        pays = value_parts[first : first + count]
        return pl.pallas_call(
            functools.partial(score_kernel, first, count, heads, pools),
            out_shape=[shape((own_heads, rows), f32)] * count,
            in_specs=[VMEM] * 5 + [ANY] + [VMEM] * (heads + count),
            out_specs=[VMEM] * count,
            compiler_params=params(20),
            cost_estimate=pl.CostEstimate(flops=0, transcendentals=0, bytes_accessed=3 << 20),
            name="score",
        )(key_maps, cosine, sine, turn, live, after, *pays[::-1], *key_parts)

    far_scores = score(middle, middle, far_parts, place)
    dense = pl.pallas_call(
        functools.partial(compact_kernel, pools),
        out_shape=shape((sel_count * BLOCK, width), bf16),
        in_specs=[VMEM, ANY] + [VMEM] * pools,
        out_specs=VMEM,
        compiler_params=params(16),
        cost_estimate=pl.CostEstimate(flops=0, transcendentals=0, bytes_accessed=3 << 20),
        name="compact",
    )(place, far_scores[0], *value_parts[::-1])
    near_scores = score(0, middle, near_parts, far_scores[0])
    dense_parts = exchange(dense, "heads", heads)
    score_parts = scatter([*near_scores, *far_scores], "pool", pools)

    mine = pl.pallas_call(
        functools.partial(attend_kernel, pools, heads),
        out_shape=shape((1, own_heads * HEAD_SIZE), bf16),
        in_specs=[VMEM] * (2 + pools + heads),
        out_specs=VMEM,
        compiler_params=params(16),
        name="attend",
    )(value_maps, place, *score_parts[::-1], *dense_parts)
    own_rows = join(*exchange(mine, "rep", reps))
    row_parts = exchange(own_rows, "pool", pools)

    own_columns = out_weight.shape[1]
    each = pools // heads
    parts = pl.pallas_call(
        functools.partial(project_kernel, pools, heads, reps),
        out_shape=[shape((each, own_columns), f32)] * (heads * reps),
        in_specs=[VMEM] * (pools + 1),
        out_specs=[VMEM] * (heads * reps),
        scratch_shapes=[pltpu.VMEM((pools * reps, own_columns), f32)],
        compiler_params=params(24),
        name="project",
    )(in_vmem(out_weight), *row_parts[::-1])
    return pl.pallas_call(
        functools.partial(finish_kernel, heads, reps),
        out_shape=shape((1, each, reps * own_columns), bf16),
        in_specs=[VMEM] * (heads * reps),
        out_specs=VMEM,
        compiler_params=params(4),
        name="finish",
    )(*scatter(parts, ("heads", "rep"), heads * reps)[::-1])


def solution(mesh):
    return jax.shard_map(
        per_device,
        mesh=mesh,
        in_specs=(
            P(("groups", "rep"), "pool", "heads"),
            P(("groups", "rep"), None, "pool", "heads"),
            P(None, "heads"),
            P(None, "heads"),
            P("heads", ("pool", "rep")),
            P(("groups", "rep"), None),
            P(("groups", "rep"), None, None),
        ),
        out_specs=P(("groups", "rep"), "heads", "pool"),
        check_vma=False,
    )
```

```python
import functools

import jax
import jax.numpy as jnp
import numpy as np
from jax import lax
from jax.experimental import pallas as pl
from jax.experimental.pallas import tpu as pltpu
from jax.sharding import PartitionSpec as P

HEAD_SIZE = 128
LANE = 64
BLOCK = 128
CAP = 2
QUERY_PER_GROUP = 8

ROPE_BASE = 500000.0
MASKED = -1e30
FAR = 1 << 29

SMEM = pl.BlockSpec(memory_space=pltpu.SMEM)
VMEM = pl.BlockSpec(memory_space=pltpu.VMEM)
ANY = pl.BlockSpec(memory_space=pl.ANY)
HBM = pl.BlockSpec(memory_space=pltpu.HBM)


def frequencies():
    half = HEAD_SIZE // 2
    exponents = np.arange(half, dtype=np.float32) * np.float32(2.0 / HEAD_SIZE)
    freq = np.power(np.float64(ROPE_BASE), -exponents.astype(np.float64)).astype(np.float32)
    return np.concatenate([freq, freq])[None, :]


def swap(value, axes, size, step):
    return lax.ppermute(value, axes, [(i, i ^ step) for i in range(size)])


def in_hbm(value):
    return pltpu.with_memory_space_constraint(value, pltpu.HBM)


def in_vmem(value):
    return pltpu.with_memory_space_constraint(value, pltpu.VMEM)


def params(mib, **more):
    return pltpu.CompilerParams(vmem_limit_bytes=mib << 20, **more)


def slot_blocks(sel_ref, seq, shard, shard_blocks):
    first = jnp.int32(-1)
    second = jnp.int32(-1)
    for i in range(sel_ref.shape[2]):
        block = sel_ref[0, seq, i]
        here = (block >= shard * shard_blocks) & (block < (shard + 1) * shard_blocks)
        second = jnp.where(here & (first >= 0), block, second)
        first = jnp.where(here & (first < 0), block, first)
    return first, second


def heads_to_rows(line, lanes):
    count = line.shape[1] // HEAD_SIZE
    rows = jnp.concatenate([line[:, n * HEAD_SIZE : (n + 1) * HEAD_SIZE] for n in range(count)], axis=0)
    if lanes < HEAD_SIZE:
        return jnp.concatenate([rows[:, i : i + lanes] for i in range(0, HEAD_SIZE, lanes)], axis=0)
    each = count * HEAD_SIZE // lanes
    return jnp.concatenate([rows[i : i + each, :] for i in range(0, count, each)], axis=1)


def rows_to_heads(rows):
    count, lanes = rows.shape
    if lanes < HEAD_SIZE:
        each = count * lanes // HEAD_SIZE
        return jnp.concatenate([rows[i : i + each, :] for i in range(0, count, each)], axis=1)
    return jnp.concatenate([rows[:, i : i + HEAD_SIZE] for i in range(0, lanes, HEAD_SIZE)], axis=0)


def gather_kernel(pools, sel_ref, lat_ref, query_ref, keys_ref, *rest):
    value_refs = rest[:pools]
    raw, line, sems = rest[pools:]
    load = pltpu.make_async_copy(query_ref.at[0], line, sems.at[pools * CAP])
    load.start()
    shard_blocks = lat_ref.shape[2] // BLOCK
    columns = lat_ref.shape[3]
    width = columns // 2
    rows = CAP * BLOCK
    me = lax.axis_index("pool")
    copies = {}
    for k in range(pools - 1, -1, -1):
        seq = me ^ k
        for c, block in enumerate(slot_blocks(sel_ref, seq, me, shard_blocks)):
            local = jnp.maximum(block - me * shard_blocks, 0)
            copies[k, c] = pltpu.make_async_copy(
                lat_ref.at[0, seq, pl.ds(pl.multiple_of(local * BLOCK, BLOCK), BLOCK), :],
                raw.at[pl.ds((k * CAP + c) * BLOCK, BLOCK), :],
                sems.at[k * CAP + c],
            )
            copies[k, c].start()
    chunk = min(4 * LANE, columns)
    half = chunk // 2
    source = lax.broadcasted_iota(jnp.int32, (chunk, chunk), 0)
    target = lax.broadcasted_iota(jnp.int32, (chunk, chunk), 1)
    within = target & (half - 1)
    wanted = ((within >> 6) << 7) + (within & (LANE - 1)) + jnp.where(target >= half, LANE, 0)
    pick = (source == wanted).astype(jnp.float32).astype(jnp.bfloat16)
    load.wait()
    queries = heads_to_rows(line[...].astype(jnp.float32), width).astype(jnp.bfloat16)
    for copy in copies.values():
        copy.wait()
    for k in range(pools - 1, -1, -1):
        for j in range(columns // chunk):
            packed = jnp.dot(
                raw[k * rows : (k + 1) * rows, j * chunk : (j + 1) * chunk], pick,
                preferred_element_type=jnp.float32,
            ).astype(jnp.bfloat16)
            keys_ref[k * rows : (k + 1) * rows, j * half : (j + 1) * half] = packed[:, :half]
            value_refs[k][:rows, j * half : (j + 1) * half] = packed[:, half:]
        value_refs[k][rows:, :] = queries


def table_kernel(pools, shard_blocks, sel_ref, len_ref, freq_ref, key_map_ref, value_map_ref, held_ref, *rest):
    cos_ref, sin_ref, turn_ref, live_ref, place_ref, key_out_ref, value_out_ref = rest[:7]
    sems = rest[-1]
    loads = [
        pltpu.make_async_copy(key_map_ref, key_out_ref, sems.at[0]),
        pltpu.make_async_copy(value_map_ref, value_out_ref, sems.at[1]),
    ]
    for load in loads:
        load.start()
    me = lax.axis_index("pool")
    lane = lax.broadcasted_iota(jnp.int32, (BLOCK, HEAD_SIZE), 1)
    row = lax.broadcasted_iota(jnp.int32, (BLOCK, HEAD_SIZE), 0)
    front = lane < HEAD_SIZE // 2
    across = lax.broadcasted_iota(jnp.int32, (1, BLOCK), 1)
    place = jnp.int32(0)
    for k in range(pools):
        turn_ref[k : k + 1, :] = len_ref[0, me ^ k].astype(jnp.float32) * freq_ref[...]
    angle = turn_ref[0:pools, :]
    turn_ref[0:pools, :] = jnp.cos(angle)
    turn_ref[pools:, :] = jnp.where(front[:1, :], -jnp.sin(angle), jnp.sin(angle))
    for k in range(pools):
        seq = me ^ k
        found = slot_blocks(sel_ref, seq, me, shard_blocks)
        one, two = [jnp.maximum(block, 0) * BLOCK for block in found]
        angle = (jnp.where(front, one, two) + row).astype(jnp.float32) * freq_ref[...]
        for ref, table, sign in ((cos_ref, jnp.cos(angle), 1.0), (sin_ref, jnp.sin(angle), -1.0)):
            turned = pltpu.roll(table, HEAD_SIZE // 2, 1)
            at = k * CAP * BLOCK
            ref[at : at + BLOCK, :] = jnp.where(front, sign * table, turned)
            ref[at + BLOCK : at + 2 * BLOCK, :] = jnp.where(front, sign * turned, table)
        mine = slot_blocks(sel_ref, me, seq, shard_blocks)
        for c in range(CAP):
            start = jnp.where(found[c] < 0, FAR, found[c] * BLOCK)
            live_ref[k : k + 1, c * BLOCK : (c + 1) * BLOCK] = (start + across < len_ref[0, seq]).astype(jnp.int32)
            at = (k * CAP + c) * BLOCK
            used = mine[c] >= 0
            place_ref[:, at : at + BLOCK] = jnp.where(used, place, -1) + 0 * across
            place = place + used.astype(jnp.int32)
    for load in loads:
        load.wait()


def rebuild_kernel(pools, heads, map_ref, cos_ref, sin_ref, *rest):
    key_refs = rest[:heads]
    out_ref = rest[heads]
    head = lax.axis_index("heads")
    width = key_refs[0].shape[1]
    rows = CAP * BLOCK
    maps = []
    for j in range(heads):
        owner = head ^ j
        maps.append(map_ref[pl.ds(pl.multiple_of(owner * width, width), width), :])
    for k in range(pools):
        at = slice(k * rows, (k + 1) * rows)
        rebuilt = jnp.dot(key_refs[0][at, :], maps[0], preferred_element_type=jnp.float32)
        for j in range(1, heads):
            rebuilt += jnp.dot(key_refs[j][at, :], maps[j], preferred_element_type=jnp.float32)
        cosine = cos_ref[at, :]
        sine = sin_ref[at, :]
        for g in range(map_ref.shape[1] // HEAD_SIZE):
            lanes = slice(g * HEAD_SIZE, (g + 1) * HEAD_SIZE)
            one = rebuilt[:, lanes]
            out_ref[at, lanes] = (one * cosine + pltpu.roll(one, HEAD_SIZE // 2, 1) * sine).astype(jnp.bfloat16)


def score_kernel(pools, turn_ref, live_ref, place_ref, key_ref, *rest):
    pay_refs = rest[:pools][::-1]
    dense_ref = rest[pools]
    out_refs = rest[pools + 1 :]
    groups = key_ref.shape[1] // HEAD_SIZE
    rows = CAP * BLOCK
    width = dense_ref.shape[1]
    kept = dense_ref.shape[0] // BLOCK
    for k in range(pools - 1, -1, -1):
        live = live_ref[k : k + 1, :] > 0
        query = rows_to_heads(pay_refs[k][rows:, :].astype(jnp.float32))
        query = query * turn_ref[k : k + 1, :] + pltpu.roll(query, HEAD_SIZE // 2, 1) * turn_ref[
            pools + k : pools + k + 1, :
        ]
        query = query.astype(jnp.bfloat16)
        for g in range(groups):
            mine = slice(g * QUERY_PER_GROUP, (g + 1) * QUERY_PER_GROUP)
            scores = lax.dot_general(
                query[mine, :], key_ref[k * rows : (k + 1) * rows, g * HEAD_SIZE : (g + 1) * HEAD_SIZE],
                (((1,), (1,)), ((), ())), preferred_element_type=jnp.float32,
            ) * (HEAD_SIZE ** -0.5)
            out_refs[k][mine, :] = jnp.where(live, scores, MASKED)
    spare = pools * CAP - kept
    for i in range(kept):
        chosen = jnp.zeros((BLOCK, width), jnp.float32)
        for slot in range(i, i + spare + 1):
            place = place_ref[:, slot * BLOCK : slot * BLOCK + LANE]
            place = jnp.concatenate([place] * (width // LANE), axis=1)
            k, c = slot // CAP, slot % CAP
            block = pay_refs[k][c * BLOCK : (c + 1) * BLOCK, :].astype(jnp.float32)
            chosen = jnp.where(place == i, block, chosen)
        dense_ref[i * BLOCK : (i + 1) * BLOCK, :] = chosen.astype(jnp.bfloat16)


def attend_kernel(pools, heads, map_ref, place_ref, *rest):
    score_refs = rest[:pools][::-1]
    value_refs = rest[pools : pools + heads]
    out_ref = rest[-1]
    head = lax.axis_index("heads")
    width = value_refs[0].shape[1]
    groups = map_ref.shape[1] // HEAD_SIZE
    scores = [ref[...] for ref in score_refs]
    top = functools.reduce(jnp.maximum, [jnp.max(s, axis=1, keepdims=True) for s in scores])
    weights = [jnp.exp(s - top) for s in scores]
    total = functools.reduce(jnp.add, [jnp.sum(w, axis=1, keepdims=True) for w in weights])
    slots = []
    for k in range(pools):
        attention = weights[k] / total
        for c in range(CAP):
            at = (k * CAP + c) * BLOCK
            slots.append((place_ref[:, at : at + BLOCK], attention[:, c * BLOCK : (c + 1) * BLOCK]))
    dense = []
    kept = value_refs[0].shape[0] // BLOCK
    for i in range(kept):
        chosen = jnp.zeros_like(slots[0][1])
        for place, attention in slots[i : i + len(slots) - kept + 1]:
            chosen = jnp.where(place == i, attention, chosen)
        dense.append(chosen)
    attention = jnp.concatenate(dense, axis=1).astype(jnp.bfloat16)
    mixed = [None] * groups
    for j in range(heads):
        owner = head ^ j
        context = jnp.dot(
            attention, value_refs[j][...], preferred_element_type=jnp.float32
        ).astype(jnp.bfloat16)
        rows = pl.ds(pl.multiple_of(owner * width, width), width)
        for g in range(groups):
            part = jnp.dot(
                context[g * QUERY_PER_GROUP : (g + 1) * QUERY_PER_GROUP, :],
                map_ref[rows, g * HEAD_SIZE : (g + 1) * HEAD_SIZE],
                preferred_element_type=jnp.float32,
            )
            mixed[g] = part if j == 0 else mixed[g] + part
    for g in range(groups):
        for q in range(QUERY_PER_GROUP):
            at = (g * QUERY_PER_GROUP + q) * HEAD_SIZE
            out_ref[:, at : at + HEAD_SIZE] = mixed[g][q : q + 1, :].astype(jnp.bfloat16)


def join_kernel(*refs):
    rows = [ref[...].reshape(-1, ref.shape[-1]).astype(jnp.float32) for ref in refs[:-1]]
    refs[-1][...] = jnp.concatenate(rows, axis=0).astype(jnp.bfloat16)


def project_kernel(pools, heads, reps, weight_ref, *rest):
    row_refs = rest[:pools]
    out_refs = rest[pools:-1]
    acc = rest[-1]
    left = jnp.concatenate([ref[...].astype(jnp.float32) for ref in row_refs], axis=0).astype(jnp.bfloat16)
    acc[...] = jnp.dot(left, weight_ref[...], preferred_element_type=jnp.float32)
    pool = lax.axis_index("pool")
    head = lax.axis_index("heads")
    each = pools // heads
    for d in range(heads * reps):
        for u in range(each):
            n = (pool ^ ((head ^ (d // reps)) * each + u)) * reps + d % reps
            out_refs[d][u : u + 1, :] = acc[pl.ds(n, 1), :]


def finish_kernel(heads, reps, *refs):
    out_ref = refs[-1]
    refs = refs[:-1][::-1]
    rep = lax.axis_index("rep")
    width = refs[0].shape[1]
    for t in range(reps):
        total = functools.reduce(jnp.add, [refs[j * reps + t][...] for j in range(heads)])
        columns = pl.ds(pl.multiple_of((rep ^ t) * width, width), width)
        out_ref[0, :, columns] = total.astype(jnp.bfloat16)


def per_device(queries, latents, key_latent_maps, value_latent_maps, out_weight, lengths, selected):
    pools = lax.axis_size("pool")
    heads = lax.axis_size("heads")
    reps = lax.axis_size("rep")
    half_seqs, sel_count = selected.shape[1:]
    assert half_seqs == pools and pools % heads == 0
    shard_blocks = latents.shape[2] // BLOCK
    width = latents.shape[3] // 2
    rows = CAP * BLOCK
    own_heads = queries.shape[2] // HEAD_SIZE
    bf16, f32, i32 = jnp.bfloat16, jnp.float32, jnp.int32
    shape = jax.ShapeDtypeStruct
    freq = jnp.asarray(frequencies())

    def join(*blocks):
        return pl.pallas_call(
            join_kernel,
            out_shape=shape((sum(block.size for block in blocks) // queries.shape[2], queries.shape[2]), bf16),
            in_specs=[VMEM] * len(blocks),
            out_specs=VMEM,
            compiler_params=params(4),
            name="join",
        )(*blocks)

    def exchange(value, axis, size):
        taken = {step: swap(value, axis, size, step) for step in range(size - 1, 0, -1)}
        return [value] + [taken[step] for step in range(1, size)]

    def scatter(blocks, axis, size):
        taken = {step: swap(blocks[step], axis, size, step) for step in range(size - 1, 0, -1)}
        return [blocks[0]] + [taken[step] for step in range(1, size)]

    query_rows = queries.shape[2] // width
    packed = pl.pallas_call(
        functools.partial(gather_kernel, pools),
        out_shape=[shape((pools * rows, width), bf16)]
        + [shape((rows + query_rows, width), bf16)] * pools,
        in_specs=[SMEM, HBM, HBM],
        out_specs=[VMEM] * (pools + 1),
        scratch_shapes=[
            pltpu.VMEM((pools * rows, 2 * width), bf16),
            pltpu.VMEM((1, queries.shape[2]), bf16),
            pltpu.SemaphoreType.DMA((pools * CAP + 1,)),
        ],
        compiler_params=params(16),
        name="gather",
    )(in_hbm(selected), in_hbm(latents), in_hbm(queries))
    keys, values = packed[0], packed[1:]

    cosine, sine, turn, live, place, key_maps, value_maps, held = pl.pallas_call(
        functools.partial(table_kernel, pools, shard_blocks),
        out_shape=[shape((pools * rows, HEAD_SIZE), f32)] * 2
        + [shape((2 * pools, HEAD_SIZE), f32), shape((pools, rows), i32), shape((1, pools * rows), i32)]
        + [shape(key_latent_maps.shape, bf16), shape(value_latent_maps.shape, bf16)]
        + [shape(values[1].shape, bf16)],
        in_specs=[SMEM, SMEM, VMEM] + [ANY] * 3,
        out_specs=[VMEM] * 7 + [ANY],
        scratch_shapes=[pltpu.SemaphoreType.DMA((2,))],
        input_output_aliases={5: 7},
        compiler_params=params(16),
        name="tables",
    )(
        in_hbm(selected), in_hbm(lengths), in_hbm(freq), in_hbm(key_latent_maps),
        in_hbm(value_latent_maps), values[1],
    )
    key_parts = exchange(keys, "heads", heads)
    value_parts = scatter([values[0], held, *values[2:]], "pool", pools)

    turned = pl.pallas_call(
        functools.partial(rebuild_kernel, pools, heads),
        out_shape=shape((pools * rows, own_heads // QUERY_PER_GROUP * HEAD_SIZE), bf16),
        in_specs=[VMEM] * (3 + heads),
        out_specs=VMEM,
        compiler_params=params(20),
        name="rebuild",
    )(key_maps, cosine, sine, *key_parts)
    dense, *scores = pl.pallas_call(
        functools.partial(score_kernel, pools),
        out_shape=[shape((sel_count * BLOCK, width), bf16)] + [shape((own_heads, rows), f32)] * pools,
        in_specs=[VMEM] * (4 + pools),
        out_specs=[VMEM] * (1 + pools),
        compiler_params=params(16),
        name="score",
    )(turn, live, place, turned, *value_parts[::-1])
    dense_parts = exchange(dense, "heads", heads)
    score_parts = scatter(scores, "pool", pools)

    mine = pl.pallas_call(
        functools.partial(attend_kernel, pools, heads),
        out_shape=shape((1, own_heads * HEAD_SIZE), bf16),
        in_specs=[VMEM] * (2 + pools + heads),
        out_specs=VMEM,
        compiler_params=params(16),
        name="attend",
    )(value_maps, place, *score_parts[::-1], *dense_parts)
    own_rows = join(*exchange(mine, "rep", reps))
    row_parts = exchange(own_rows, "pool", pools)

    own_columns = out_weight.shape[1]
    each = pools // heads
    parts = pl.pallas_call(
        functools.partial(project_kernel, pools, heads, reps),
        out_shape=[shape((each, own_columns), f32)] * (heads * reps),
        in_specs=[VMEM] * (pools + 1),
        out_specs=[VMEM] * (heads * reps),
        scratch_shapes=[pltpu.VMEM((pools * reps, own_columns), f32)],
        compiler_params=params(24),
        name="project",
    )(in_vmem(out_weight), *row_parts)
    return pl.pallas_call(
        functools.partial(finish_kernel, heads, reps),
        out_shape=shape((1, each, reps * own_columns), bf16),
        in_specs=[VMEM] * (heads * reps),
        out_specs=VMEM,
        compiler_params=params(4),
        name="finish",
    )(*scatter(parts, ("heads", "rep"), heads * reps)[::-1])


def solution(mesh):
    return jax.shard_map(
        per_device,
        mesh=mesh,
        in_specs=(
            P(("groups", "rep"), "pool", "heads"),
            P(("groups", "rep"), None, "pool", "heads"),
            P(None, "heads"),
            P(None, "heads"),
            P("heads", ("pool", "rep")),
            P(("groups", "rep"), None),
            P(("groups", "rep"), None, None),
        ),
        out_specs=P(("groups", "rep"), "heads", "pool"),
        check_vma=False,
    )
```

```python
import functools

import jax
import jax.numpy as jnp
import numpy as np
from jax import lax
from jax.experimental import pallas as pl
from jax.experimental.pallas import tpu as pltpu
from jax.sharding import PartitionSpec as P

HEAD_SIZE = 128
LANE = 64
BLOCK = 128
CAP = 2
QUERY_PER_GROUP = 8

ROPE_BASE = 500000.0
MASKED = -1e30
FAR = 1 << 29

SMEM = pl.BlockSpec(memory_space=pltpu.SMEM)
VMEM = pl.BlockSpec(memory_space=pltpu.VMEM)
ANY = pl.BlockSpec(memory_space=pl.ANY)
HBM = pl.BlockSpec(memory_space=pltpu.HBM)


def frequencies():
    half = HEAD_SIZE // 2
    exponents = np.arange(half, dtype=np.float32) * np.float32(2.0 / HEAD_SIZE)
    freq = np.power(np.float64(ROPE_BASE), -exponents.astype(np.float64)).astype(np.float32)
    return np.concatenate([freq, freq])[None, :]


def swap(value, axes, size, step):
    return lax.ppermute(value, axes, [(i, i ^ step) for i in range(size)])


def in_hbm(value):
    return pltpu.with_memory_space_constraint(value, pltpu.HBM)


def in_vmem(value):
    return pltpu.with_memory_space_constraint(value, pltpu.VMEM)


def params(mib, **more):
    return pltpu.CompilerParams(vmem_limit_bytes=mib << 20, **more)


def slot_blocks(sel_ref, seq, shard, shard_blocks):
    first = jnp.int32(-1)
    second = jnp.int32(-1)
    for i in range(sel_ref.shape[2]):
        block = sel_ref[0, seq, i]
        here = (block >= shard * shard_blocks) & (block < (shard + 1) * shard_blocks)
        second = jnp.where(here & (first >= 0), block, second)
        first = jnp.where(here & (first < 0), block, first)
    return first, second


def heads_to_rows(line, lanes):
    count = line.shape[1] // HEAD_SIZE
    rows = jnp.concatenate([line[:, n * HEAD_SIZE : (n + 1) * HEAD_SIZE] for n in range(count)], axis=0)
    if lanes < HEAD_SIZE:
        return jnp.concatenate([rows[:, i : i + lanes] for i in range(0, HEAD_SIZE, lanes)], axis=0)
    each = count * HEAD_SIZE // lanes
    return jnp.concatenate([rows[i : i + each, :] for i in range(0, count, each)], axis=1)


def rows_to_heads(rows):
    count, lanes = rows.shape
    if lanes < HEAD_SIZE:
        each = count * lanes // HEAD_SIZE
        return jnp.concatenate([rows[i : i + each, :] for i in range(0, count, each)], axis=1)
    return jnp.concatenate([rows[:, i : i + HEAD_SIZE] for i in range(0, lanes, HEAD_SIZE)], axis=0)


def gather_kernel(pools, sel_ref, lat_ref, query_ref, keys_ref, *rest):
    value_refs = rest[:pools]
    raw, line, sems = rest[pools:]
    load = pltpu.make_async_copy(query_ref.at[0], line, sems.at[pools * CAP])
    load.start()
    shard_blocks = lat_ref.shape[2] // BLOCK
    columns = lat_ref.shape[3]
    width = columns // 2
    rows = CAP * BLOCK
    me = lax.axis_index("pool")
    copies = {}
    for k in range(pools - 1, -1, -1):
        seq = me ^ k
        for c, block in enumerate(slot_blocks(sel_ref, seq, me, shard_blocks)):
            local = jnp.maximum(block - me * shard_blocks, 0)
            copies[k, c] = pltpu.make_async_copy(
                lat_ref.at[0, seq, pl.ds(pl.multiple_of(local * BLOCK, BLOCK), BLOCK), :],
                raw.at[pl.ds((k * CAP + c) * BLOCK, BLOCK), :],
                sems.at[k * CAP + c],
            )
            copies[k, c].start()
    chunk = min(4 * LANE, columns)
    half = chunk // 2
    source = lax.broadcasted_iota(jnp.int32, (chunk, chunk), 0)
    target = lax.broadcasted_iota(jnp.int32, (chunk, chunk), 1)
    within = target & (half - 1)
    wanted = ((within >> 6) << 7) + (within & (LANE - 1)) + jnp.where(target >= half, LANE, 0)
    pick = (source == wanted).astype(jnp.float32).astype(jnp.bfloat16)
    load.wait()
    queries = heads_to_rows(line[...].astype(jnp.float32), width).astype(jnp.bfloat16)
    for copy in copies.values():
        copy.wait()
    for k in range(pools - 1, -1, -1):
        for j in range(columns // chunk):
            packed = jnp.dot(
                raw[k * rows : (k + 1) * rows, j * chunk : (j + 1) * chunk], pick,
                preferred_element_type=jnp.float32,
            ).astype(jnp.bfloat16)
            keys_ref[k * rows : (k + 1) * rows, j * half : (j + 1) * half] = packed[:, :half]
            value_refs[k][:rows, j * half : (j + 1) * half] = packed[:, half:]
        value_refs[k][rows:, :] = queries


def table_kernel(pools, shard_blocks, sel_ref, len_ref, freq_ref, key_map_ref, value_map_ref, held_ref, *rest):
    cos_ref, sin_ref, turn_ref, live_ref, place_ref, key_out_ref, value_out_ref = rest[:7]
    sems = rest[-1]
    loads = [
        pltpu.make_async_copy(key_map_ref, key_out_ref, sems.at[0]),
        pltpu.make_async_copy(value_map_ref, value_out_ref, sems.at[1]),
    ]
    for load in loads:
        load.start()
    me = lax.axis_index("pool")
    lane = lax.broadcasted_iota(jnp.int32, (BLOCK, HEAD_SIZE), 1)
    row = lax.broadcasted_iota(jnp.int32, (BLOCK, HEAD_SIZE), 0)
    front = lane < HEAD_SIZE // 2
    across = lax.broadcasted_iota(jnp.int32, (1, BLOCK), 1)
    place = jnp.int32(0)
    for k in range(pools):
        turn_ref[k : k + 1, :] = len_ref[0, me ^ k].astype(jnp.float32) * freq_ref[...]
    angle = turn_ref[0:pools, :]
    turn_ref[0:pools, :] = jnp.cos(angle)
    turn_ref[pools:, :] = jnp.where(front[:1, :], -jnp.sin(angle), jnp.sin(angle))
    for k in range(pools):
        seq = me ^ k
        found = slot_blocks(sel_ref, seq, me, shard_blocks)
        one, two = [jnp.maximum(block, 0) * BLOCK for block in found]
        angle = (jnp.where(front, one, two) + row).astype(jnp.float32) * freq_ref[...]
        for ref, table, sign in ((cos_ref, jnp.cos(angle), 1.0), (sin_ref, jnp.sin(angle), -1.0)):
            turned = pltpu.roll(table, HEAD_SIZE // 2, 1)
            at = k * CAP * BLOCK
            ref[at : at + BLOCK, :] = jnp.where(front, sign * table, turned)
            ref[at + BLOCK : at + 2 * BLOCK, :] = jnp.where(front, sign * turned, table)
        mine = slot_blocks(sel_ref, me, seq, shard_blocks)
        for c in range(CAP):
            start = jnp.where(found[c] < 0, FAR, found[c] * BLOCK)
            live_ref[k : k + 1, c * BLOCK : (c + 1) * BLOCK] = (start + across < len_ref[0, seq]).astype(jnp.int32)
            at = (k * CAP + c) * BLOCK
            used = mine[c] >= 0
            place_ref[:, at : at + BLOCK] = jnp.where(used, place, -1) + 0 * across
            place = place + used.astype(jnp.int32)
    for load in loads:
        load.wait()


def rebuild_kernel(pools, heads, map_ref, cos_ref, sin_ref, *rest):
    key_refs = rest[:heads]
    out_ref = rest[heads]
    head = lax.axis_index("heads")
    width = key_refs[0].shape[1]
    rows = CAP * BLOCK
    maps = []
    for j in range(heads):
        owner = head ^ j
        maps.append(map_ref[pl.ds(pl.multiple_of(owner * width, width), width), :])
    for k in range(pools):
        at = slice(k * rows, (k + 1) * rows)
        rebuilt = jnp.dot(key_refs[0][at, :], maps[0], preferred_element_type=jnp.float32)
        for j in range(1, heads):
            rebuilt += jnp.dot(key_refs[j][at, :], maps[j], preferred_element_type=jnp.float32)
        cosine = cos_ref[at, :]
        sine = sin_ref[at, :]
        for g in range(map_ref.shape[1] // HEAD_SIZE):
            lanes = slice(g * HEAD_SIZE, (g + 1) * HEAD_SIZE)
            one = rebuilt[:, lanes]
            out_ref[at, lanes] = (one * cosine + pltpu.roll(one, HEAD_SIZE // 2, 1) * sine).astype(jnp.bfloat16)


def score_kernel(pools, turn_ref, live_ref, place_ref, key_ref, *rest):
    pay_refs = rest[:pools][::-1]
    dense_ref = rest[pools]
    out_refs = rest[pools + 1 :]
    groups = key_ref.shape[1] // HEAD_SIZE
    rows = CAP * BLOCK
    width = dense_ref.shape[1]
    kept = dense_ref.shape[0] // BLOCK
    for k in range(pools - 1, -1, -1):
        live = live_ref[k : k + 1, :] > 0
        query = rows_to_heads(pay_refs[k][rows:, :].astype(jnp.float32))
        query = query * turn_ref[k : k + 1, :] + pltpu.roll(query, HEAD_SIZE // 2, 1) * turn_ref[
            pools + k : pools + k + 1, :
        ]
        query = query.astype(jnp.bfloat16)
        for g in range(groups):
            mine = slice(g * QUERY_PER_GROUP, (g + 1) * QUERY_PER_GROUP)
            scores = lax.dot_general(
                query[mine, :], key_ref[k * rows : (k + 1) * rows, g * HEAD_SIZE : (g + 1) * HEAD_SIZE],
                (((1,), (1,)), ((), ())), preferred_element_type=jnp.float32,
            ) * (HEAD_SIZE ** -0.5)
            out_refs[k][mine, :] = jnp.where(live, scores, MASKED)
    spare = pools * CAP - kept
    for i in range(kept):
        chosen = jnp.zeros((BLOCK, width), jnp.float32)
        for slot in range(i, i + spare + 1):
            place = place_ref[:, slot * BLOCK : slot * BLOCK + LANE]
            place = jnp.concatenate([place] * (width // LANE), axis=1)
            k, c = slot // CAP, slot % CAP
            block = pay_refs[k][c * BLOCK : (c + 1) * BLOCK, :].astype(jnp.float32)
            chosen = jnp.where(place == i, block, chosen)
        dense_ref[i * BLOCK : (i + 1) * BLOCK, :] = chosen.astype(jnp.bfloat16)


def attend_kernel(pools, heads, map_ref, place_ref, *rest):
    score_refs = rest[:pools][::-1]
    value_refs = rest[pools : pools + heads]
    out_ref = rest[-1]
    head = lax.axis_index("heads")
    width = value_refs[0].shape[1]
    groups = map_ref.shape[1] // HEAD_SIZE
    scores = [ref[...] for ref in score_refs]
    top = functools.reduce(jnp.maximum, [jnp.max(s, axis=1, keepdims=True) for s in scores])
    weights = [jnp.exp(s - top) for s in scores]
    total = functools.reduce(jnp.add, [jnp.sum(w, axis=1, keepdims=True) for w in weights])
    slots = []
    for k in range(pools):
        attention = weights[k] / total
        for c in range(CAP):
            at = (k * CAP + c) * BLOCK
            slots.append((place_ref[:, at : at + BLOCK], attention[:, c * BLOCK : (c + 1) * BLOCK]))
    dense = []
    kept = value_refs[0].shape[0] // BLOCK
    for i in range(kept):
        chosen = jnp.zeros_like(slots[0][1])
        for place, attention in slots[i : i + len(slots) - kept + 1]:
            chosen = jnp.where(place == i, attention, chosen)
        dense.append(chosen)
    attention = jnp.concatenate(dense, axis=1).astype(jnp.bfloat16)
    mixed = [None] * groups
    for j in range(heads):
        owner = head ^ j
        context = jnp.dot(
            attention, value_refs[j][...], preferred_element_type=jnp.float32
        ).astype(jnp.bfloat16)
        rows = pl.ds(pl.multiple_of(owner * width, width), width)
        for g in range(groups):
            part = jnp.dot(
                context[g * QUERY_PER_GROUP : (g + 1) * QUERY_PER_GROUP, :],
                map_ref[rows, g * HEAD_SIZE : (g + 1) * HEAD_SIZE],
                preferred_element_type=jnp.float32,
            )
            mixed[g] = part if j == 0 else mixed[g] + part
    for g in range(groups):
        for q in range(QUERY_PER_GROUP):
            at = (g * QUERY_PER_GROUP + q) * HEAD_SIZE
            out_ref[:, at : at + HEAD_SIZE] = mixed[g][q : q + 1, :].astype(jnp.bfloat16)


def project_kernel(pools, heads, reps, *rest):
    weight_refs = rest[:reps]
    row_refs = rest[reps : reps + pools]
    out_refs = rest[reps + pools : -1]
    acc = rest[-1]
    rep = lax.axis_index("rep")
    width = weight_refs[0].shape[1]
    left = jnp.concatenate([ref[...].astype(jnp.float32) for ref in row_refs], axis=0).astype(jnp.bfloat16)
    for t in range(reps):
        columns = pl.ds(pl.multiple_of((rep ^ t) * width, width), width)
        acc[:, columns] = jnp.dot(left, weight_refs[t][...], preferred_element_type=jnp.float32)
    pool = lax.axis_index("pool")
    head = lax.axis_index("heads")
    each = pools // heads
    for j in range(heads):
        for u in range(each):
            n = pool ^ ((head ^ j) * each + u)
            out_refs[j][u : u + 1, :] = acc[pl.ds(n, 1), :]


def finish_kernel(*refs):
    total = functools.reduce(jnp.add, [ref[...] for ref in refs[:-1][::-1]])
    refs[-1][0] = total.astype(jnp.bfloat16)


def per_device(queries, latents, key_latent_maps, value_latent_maps, out_weight, lengths, selected):
    pools = lax.axis_size("pool")
    heads = lax.axis_size("heads")
    reps = lax.axis_size("rep")
    half_seqs, sel_count = selected.shape[1:]
    assert half_seqs == pools and pools % heads == 0
    shard_blocks = latents.shape[2] // BLOCK
    width = latents.shape[3] // 2
    rows = CAP * BLOCK
    own_heads = queries.shape[2] // HEAD_SIZE
    bf16, f32, i32 = jnp.bfloat16, jnp.float32, jnp.int32
    shape = jax.ShapeDtypeStruct
    freq = jnp.asarray(frequencies())

    def exchange(value, axis, size):
        taken = {step: swap(value, axis, size, step) for step in range(size - 1, 0, -1)}
        return [value] + [taken[step] for step in range(1, size)]

    def scatter(blocks, axis, size):
        taken = {step: swap(blocks[step], axis, size, step) for step in range(size - 1, 0, -1)}
        return [blocks[0]] + [taken[step] for step in range(1, size)]

    query_rows = queries.shape[2] // width
    packed = pl.pallas_call(
        functools.partial(gather_kernel, pools),
        out_shape=[shape((pools * rows, width), bf16)]
        + [shape((rows + query_rows, width), bf16)] * pools,
        in_specs=[SMEM, HBM, HBM],
        out_specs=[VMEM] * (pools + 1),
        scratch_shapes=[
            pltpu.VMEM((pools * rows, 2 * width), bf16),
            pltpu.VMEM((1, queries.shape[2]), bf16),
            pltpu.SemaphoreType.DMA((pools * CAP + 1,)),
        ],
        compiler_params=params(16),
        name="gather",
    )(in_hbm(selected), in_hbm(latents), in_hbm(queries))
    keys, values = packed[0], packed[1:]

    cosine, sine, turn, live, place, key_maps, value_maps, held = pl.pallas_call(
        functools.partial(table_kernel, pools, shard_blocks),
        out_shape=[shape((pools * rows, HEAD_SIZE), f32)] * 2
        + [shape((2 * pools, HEAD_SIZE), f32), shape((pools, rows), i32), shape((1, pools * rows), i32)]
        + [shape(key_latent_maps.shape, bf16), shape(value_latent_maps.shape, bf16)]
        + [shape(values[1].shape, bf16)],
        in_specs=[SMEM, SMEM, VMEM] + [ANY] * 3,
        out_specs=[VMEM] * 7 + [ANY],
        scratch_shapes=[pltpu.SemaphoreType.DMA((2,))],
        input_output_aliases={5: 7},
        compiler_params=params(16),
        name="tables",
    )(
        in_hbm(selected), in_hbm(lengths), in_hbm(freq), in_hbm(key_latent_maps),
        in_hbm(value_latent_maps), values[1],
    )
    key_parts = exchange(keys, "heads", heads)
    value_parts = scatter([values[0], held, *values[2:]], "pool", pools)

    turned = pl.pallas_call(
        functools.partial(rebuild_kernel, pools, heads),
        out_shape=shape((pools * rows, own_heads // QUERY_PER_GROUP * HEAD_SIZE), bf16),
        in_specs=[VMEM] * (3 + heads),
        out_specs=VMEM,
        compiler_params=params(20),
        name="rebuild",
    )(key_maps, cosine, sine, *key_parts)
    dense, *scores = pl.pallas_call(
        functools.partial(score_kernel, pools),
        out_shape=[shape((sel_count * BLOCK, width), bf16)] + [shape((own_heads, rows), f32)] * pools,
        in_specs=[VMEM] * (4 + pools),
        out_specs=[VMEM] * (1 + pools),
        compiler_params=params(16),
        name="score",
    )(turn, live, place, turned, *value_parts[::-1])
    dense_parts = exchange(dense, "heads", heads)
    score_parts = scatter(scores, "pool", pools)

    mine = pl.pallas_call(
        functools.partial(attend_kernel, pools, heads),
        out_shape=shape((1, own_heads * HEAD_SIZE), bf16),
        in_specs=[VMEM] * (2 + pools + heads),
        out_specs=VMEM,
        compiler_params=params(16),
        name="attend",
    )(value_maps, place, *score_parts[::-1], *dense_parts)
    row_parts = exchange(mine, "pool", pools)

    own_columns = out_weight.shape[1]
    each = pools // heads
    weights = exchange(out_weight, "rep", reps)
    parts = pl.pallas_call(
        functools.partial(project_kernel, pools, heads, reps),
        out_shape=[shape((each, reps * own_columns), f32)] * heads,
        in_specs=[VMEM] * (reps + pools),
        out_specs=[VMEM] * heads,
        scratch_shapes=[pltpu.VMEM((pools, reps * own_columns), f32)],
        compiler_params=params(24),
        name="project",
    )(*[in_vmem(weight) for weight in weights], *row_parts)
    return pl.pallas_call(
        finish_kernel,
        out_shape=shape((1, each, reps * own_columns), bf16),
        in_specs=[VMEM] * heads,
        out_specs=VMEM,
        compiler_params=params(4),
        name="finish",
    )(*scatter(parts, "heads", heads)[::-1])


def solution(mesh):
    return jax.shard_map(
        per_device,
        mesh=mesh,
        in_specs=(
            P(("groups", "rep"), "pool", "heads"),
            P(("groups", "rep"), None, "pool", "heads"),
            P(None, "heads"),
            P(None, "heads"),
            P("heads", ("pool", "rep")),
            P(("groups", "rep"), None),
            P(("groups", "rep"), None, None),
        ),
        out_specs=P(("groups", "rep"), "heads", "pool"),
        check_vma=False,
    )
```

```python
import functools

import jax
import jax.numpy as jnp
import numpy as np
from jax import lax
from jax.experimental import pallas as pl
from jax.experimental.pallas import tpu as pltpu
from jax.sharding import PartitionSpec as P

HEAD_SIZE = 128
LANE = 64
BLOCK = 128
CAP = 2
QUERY_PER_GROUP = 8

ROPE_BASE = 500000.0
MASKED = -1e30
FAR = 1 << 29

SMEM = pl.BlockSpec(memory_space=pltpu.SMEM)
VMEM = pl.BlockSpec(memory_space=pltpu.VMEM)
ANY = pl.BlockSpec(memory_space=pl.ANY)
HBM = pl.BlockSpec(memory_space=pltpu.HBM)


def frequencies():
    half = HEAD_SIZE // 2
    exponents = np.arange(half, dtype=np.float32) * np.float32(2.0 / HEAD_SIZE)
    freq = np.power(np.float64(ROPE_BASE), -exponents.astype(np.float64)).astype(np.float32)
    return np.concatenate([freq, freq])[None, :]


def swap(value, axes, size, step):
    return lax.ppermute(value, axes, [(i, i ^ step) for i in range(size)])


def in_hbm(value):
    return pltpu.with_memory_space_constraint(value, pltpu.HBM)


def in_vmem(value):
    return pltpu.with_memory_space_constraint(value, pltpu.VMEM)


def params(mib, **more):
    return pltpu.CompilerParams(vmem_limit_bytes=mib << 20, **more)


def slot_blocks(sel_ref, seq, shard, shard_blocks):
    first = jnp.int32(-1)
    second = jnp.int32(-1)
    for i in range(sel_ref.shape[2]):
        block = sel_ref[0, seq, i]
        here = (block >= shard * shard_blocks) & (block < (shard + 1) * shard_blocks)
        second = jnp.where(here & (first >= 0), block, second)
        first = jnp.where(here & (first < 0), block, first)
    return first, second


def heads_to_rows(line, lanes):
    count = line.shape[1] // HEAD_SIZE
    rows = jnp.concatenate([line[:, n * HEAD_SIZE : (n + 1) * HEAD_SIZE] for n in range(count)], axis=0)
    if lanes < HEAD_SIZE:
        return jnp.concatenate([rows[:, i : i + lanes] for i in range(0, HEAD_SIZE, lanes)], axis=0)
    each = count * HEAD_SIZE // lanes
    return jnp.concatenate([rows[i : i + each, :] for i in range(0, count, each)], axis=1)


def rows_to_heads(rows):
    count, lanes = rows.shape
    if lanes < HEAD_SIZE:
        each = count * lanes // HEAD_SIZE
        return jnp.concatenate([rows[i : i + each, :] for i in range(0, count, each)], axis=1)
    return jnp.concatenate([rows[:, i : i + HEAD_SIZE] for i in range(0, lanes, HEAD_SIZE)], axis=0)


def gather_kernel(pools, sel_ref, lat_ref, query_ref, keys_ref, *rest):
    value_refs = rest[:-3]
    raw, line, sems = rest[-3:]
    load = pltpu.make_async_copy(query_ref.at[0], line, sems.at[pools * CAP])
    load.start()
    shard_blocks = lat_ref.shape[2] // BLOCK
    columns = lat_ref.shape[3]
    width = columns // 2
    rows = CAP * BLOCK
    me = lax.axis_index("pool")
    copies = {}
    for k in range(pools - 1, -1, -1):
        seq = me ^ k
        for c, block in enumerate(slot_blocks(sel_ref, seq, me, shard_blocks)):
            local = jnp.maximum(block - me * shard_blocks, 0)
            copies[k, c] = pltpu.make_async_copy(
                lat_ref.at[0, seq, pl.ds(pl.multiple_of(local * BLOCK, BLOCK), BLOCK), :],
                raw.at[pl.ds((k * CAP + c) * BLOCK, BLOCK), :],
                sems.at[k * CAP + c],
            )
            copies[k, c].start()
    chunk = min(4 * LANE, columns)
    half = chunk // 2
    source = lax.broadcasted_iota(jnp.int32, (chunk, chunk), 0)
    target = lax.broadcasted_iota(jnp.int32, (chunk, chunk), 1)
    within = target & (half - 1)
    wanted = ((within >> 6) << 7) + (within & (LANE - 1)) + jnp.where(target >= half, LANE, 0)
    pick = (source == wanted).astype(jnp.float32).astype(jnp.bfloat16)
    load.wait()
    queries = heads_to_rows(line[...].astype(jnp.float32), value_refs[0].shape[1]).astype(jnp.bfloat16)
    for copy in copies.values():
        copy.wait()
    for k in range(pools - 1, -1, -1):
        for j in range(columns // chunk):
            packed = jnp.dot(
                raw[k * rows : (k + 1) * rows, j * chunk : (j + 1) * chunk], pick,
                preferred_element_type=jnp.float32,
            ).astype(jnp.bfloat16)
            keys_ref[k * rows : (k + 1) * rows, j * half : (j + 1) * half] = packed[:, :half]
            value_refs[j * pools + k][:rows, :] = packed[:, half:]
        value_refs[k][rows:, :] = queries


def table_kernel(pools, shard_blocks, sel_ref, len_ref, freq_ref, key_map_ref, value_map_ref, held_ref, *rest):
    cos_ref, sin_ref, turn_ref, live_ref, place_ref, key_out_ref, value_out_ref = rest[:7]
    sems = rest[-1]
    loads = [
        pltpu.make_async_copy(key_map_ref, key_out_ref, sems.at[0]),
        pltpu.make_async_copy(value_map_ref, value_out_ref, sems.at[1]),
    ]
    for load in loads:
        load.start()
    me = lax.axis_index("pool")
    lane = lax.broadcasted_iota(jnp.int32, (BLOCK, HEAD_SIZE), 1)
    row = lax.broadcasted_iota(jnp.int32, (BLOCK, HEAD_SIZE), 0)
    front = lane < HEAD_SIZE // 2
    across = lax.broadcasted_iota(jnp.int32, (1, BLOCK), 1)
    place = jnp.int32(0)
    for k in range(pools):
        turn_ref[k : k + 1, :] = len_ref[0, me ^ k].astype(jnp.float32) * freq_ref[...]
    angle = turn_ref[0:pools, :]
    turn_ref[0:pools, :] = jnp.cos(angle)
    turn_ref[pools:, :] = jnp.where(front[:1, :], -jnp.sin(angle), jnp.sin(angle))
    for k in range(pools):
        seq = me ^ k
        found = slot_blocks(sel_ref, seq, me, shard_blocks)
        one, two = [jnp.maximum(block, 0) * BLOCK for block in found]
        angle = (jnp.where(front, one, two) + row).astype(jnp.float32) * freq_ref[...]
        for ref, table, sign in ((cos_ref, jnp.cos(angle), 1.0), (sin_ref, jnp.sin(angle), -1.0)):
            turned = pltpu.roll(table, HEAD_SIZE // 2, 1)
            at = k * CAP * BLOCK
            ref[at : at + BLOCK, :] = jnp.where(front, sign * table, turned)
            ref[at + BLOCK : at + 2 * BLOCK, :] = jnp.where(front, sign * turned, table)
        mine = slot_blocks(sel_ref, me, seq, shard_blocks)
        for c in range(CAP):
            start = jnp.where(found[c] < 0, FAR, found[c] * BLOCK)
            live_ref[k : k + 1, c * BLOCK : (c + 1) * BLOCK] = (start + across < len_ref[0, seq]).astype(jnp.int32)
            at = (k * CAP + c) * BLOCK
            used = mine[c] >= 0
            place_ref[:, at : at + BLOCK] = jnp.where(used, place, -1) + 0 * across
            place = place + used.astype(jnp.int32)
    for load in loads:
        load.wait()


def rebuild_kernel(pools, heads, map_ref, cos_ref, sin_ref, *rest):
    key_refs = rest[:heads]
    out_ref = rest[heads]
    head = lax.axis_index("heads")
    width = key_refs[0].shape[1]
    rows = CAP * BLOCK
    maps = []
    for j in range(heads):
        owner = head ^ j
        maps.append(map_ref[pl.ds(pl.multiple_of(owner * width, width), width), :])
    for k in range(pools):
        at = slice(k * rows, (k + 1) * rows)
        rebuilt = jnp.dot(key_refs[0][at, :], maps[0], preferred_element_type=jnp.float32)
        for j in range(1, heads):
            rebuilt += jnp.dot(key_refs[j][at, :], maps[j], preferred_element_type=jnp.float32)
        cosine = cos_ref[at, :]
        sine = sin_ref[at, :]
        for g in range(map_ref.shape[1] // HEAD_SIZE):
            lanes = slice(g * HEAD_SIZE, (g + 1) * HEAD_SIZE)
            one = rebuilt[:, lanes]
            out_ref[at, lanes] = (one * cosine + pltpu.roll(one, HEAD_SIZE // 2, 1) * sine).astype(jnp.bfloat16)


def score_kernel(pools, turn_ref, live_ref, place_ref, key_ref, *rest):
    pay_refs = rest[:pools][::-1]
    dense_ref = rest[pools]
    out_refs = rest[pools + 1 :]
    groups = key_ref.shape[1] // HEAD_SIZE
    rows = CAP * BLOCK
    for k in range(pools - 1, -1, -1):
        live = live_ref[k : k + 1, :] > 0
        query = rows_to_heads(pay_refs[k][rows:, :].astype(jnp.float32))
        query = query * turn_ref[k : k + 1, :] + pltpu.roll(query, HEAD_SIZE // 2, 1) * turn_ref[
            pools + k : pools + k + 1, :
        ]
        query = query.astype(jnp.bfloat16)
        for g in range(groups):
            mine = slice(g * QUERY_PER_GROUP, (g + 1) * QUERY_PER_GROUP)
            scores = lax.dot_general(
                query[mine, :], key_ref[k * rows : (k + 1) * rows, g * HEAD_SIZE : (g + 1) * HEAD_SIZE],
                (((1,), (1,)), ((), ())), preferred_element_type=jnp.float32,
            ) * (HEAD_SIZE ** -0.5)
            out_refs[k][mine, :] = jnp.where(live, scores, MASKED)
    compact(pools, place_ref, pay_refs, dense_ref)


def compact(pools, place_ref, value_refs, out_ref):
    kept = out_ref.shape[0] // BLOCK
    width = out_ref.shape[1]
    spare = pools * CAP - kept
    for i in range(kept):
        chosen = jnp.zeros((BLOCK, width), jnp.float32)
        for slot in range(i, i + spare + 1):
            place = place_ref[:, slot * BLOCK : slot * BLOCK + LANE]
            place = jnp.concatenate([place] * (width // LANE), axis=1)
            k, c = slot // CAP, slot % CAP
            block = value_refs[k][c * BLOCK : (c + 1) * BLOCK, :].astype(jnp.float32)
            chosen = jnp.where(place == i, block, chosen)
        out_ref[i * BLOCK : (i + 1) * BLOCK, :] = chosen.astype(jnp.bfloat16)


def compact_kernel(pools, place_ref, *rest):
    compact(pools, place_ref, rest[:pools][::-1], rest[-1])


def attend_kernel(pools, heads, chunks, map_ref, place_ref, *rest):
    score_refs = rest[:pools][::-1]
    value_refs = rest[pools : pools + heads * chunks]
    out_ref = rest[-1]
    head = lax.axis_index("heads")
    width = value_refs[0].shape[1]
    groups = map_ref.shape[1] // HEAD_SIZE
    scores = [ref[...] for ref in score_refs]
    top = functools.reduce(jnp.maximum, [jnp.max(s, axis=1, keepdims=True) for s in scores])
    weights = [jnp.exp(s - top) for s in scores]
    total = functools.reduce(jnp.add, [jnp.sum(w, axis=1, keepdims=True) for w in weights])
    slots = []
    for k in range(pools):
        attention = weights[k] / total
        for c in range(CAP):
            at = (k * CAP + c) * BLOCK
            slots.append((place_ref[:, at : at + BLOCK], attention[:, c * BLOCK : (c + 1) * BLOCK]))
    dense = []
    kept = value_refs[0].shape[0] // BLOCK
    for i in range(kept):
        chosen = jnp.zeros_like(slots[0][1])
        for place, attention in slots[i : i + len(slots) - kept + 1]:
            chosen = jnp.where(place == i, attention, chosen)
        dense.append(chosen)
    attention = jnp.concatenate(dense, axis=1).astype(jnp.bfloat16)
    mixed = [None] * groups
    for j in range(heads * chunks):
        owner = (head ^ (j // chunks)) * chunks + j % chunks
        context = jnp.dot(
            attention, value_refs[j][...], preferred_element_type=jnp.float32
        ).astype(jnp.bfloat16)
        rows = pl.ds(pl.multiple_of(owner * width, width), width)
        for g in range(groups):
            part = jnp.dot(
                context[g * QUERY_PER_GROUP : (g + 1) * QUERY_PER_GROUP, :],
                map_ref[rows, g * HEAD_SIZE : (g + 1) * HEAD_SIZE],
                preferred_element_type=jnp.float32,
            )
            mixed[g] = part if j == 0 else mixed[g] + part
    out_ref[...] = jnp.concatenate(mixed, axis=0).astype(jnp.bfloat16)


def join_kernel(*refs):
    lines = []
    for ref in refs[:-1]:
        block = ref[...].astype(jnp.float32)
        lines.append(jnp.concatenate([block[n : n + 1, :] for n in range(block.shape[0])], axis=1))
    refs[-1][...] = jnp.concatenate(lines, axis=0).astype(jnp.bfloat16)


def project_kernel(pools, heads, reps, weight_ref, *rest):
    row_refs = rest[:pools]
    out_refs = rest[pools:-1]
    acc = rest[-1]
    left = jnp.concatenate([ref[...].astype(jnp.float32) for ref in row_refs], axis=0).astype(jnp.bfloat16)
    acc[...] = jnp.dot(left, weight_ref[...], preferred_element_type=jnp.float32)
    pool = lax.axis_index("pool")
    head = lax.axis_index("heads")
    each = pools // heads
    for d in range(heads * reps):
        for u in range(each):
            n = (pool ^ ((head ^ (d // reps)) * each + u)) * reps + d % reps
            out_refs[d][u : u + 1, :] = acc[pl.ds(n, 1), :]


def finish_kernel(heads, reps, *refs):
    out_ref = refs[-1]
    refs = refs[:-1][::-1]
    rep = lax.axis_index("rep")
    width = refs[0].shape[1]
    for t in range(reps):
        total = functools.reduce(jnp.add, [refs[j * reps + t][...] for j in range(heads)])
        columns = pl.ds(pl.multiple_of((rep ^ t) * width, width), width)
        out_ref[0, :, columns] = total.astype(jnp.bfloat16)


def per_device(queries, latents, key_latent_maps, value_latent_maps, out_weight, lengths, selected):
    pools = lax.axis_size("pool")
    heads = lax.axis_size("heads")
    reps = lax.axis_size("rep")
    half_seqs, sel_count = selected.shape[1:]
    assert half_seqs == pools and pools % heads == 0
    shard_blocks = latents.shape[2] // BLOCK
    width = latents.shape[3] // 2
    rows = CAP * BLOCK
    own_heads = queries.shape[2] // HEAD_SIZE
    bf16, f32, i32 = jnp.bfloat16, jnp.float32, jnp.int32
    shape = jax.ShapeDtypeStruct
    freq = jnp.asarray(frequencies())

    def join(*blocks):
        return pl.pallas_call(
            join_kernel,
            out_shape=shape((len(blocks), queries.shape[2]), bf16),
            in_specs=[VMEM] * len(blocks),
            out_specs=VMEM,
            compiler_params=params(4),
            name="join",
        )(*blocks)

    def exchange(value, axis, size):
        taken = {step: swap(value, axis, size, step) for step in range(size - 1, 0, -1)}
        return [value] + [taken[step] for step in range(1, size)]

    def scatter(blocks, axis, size):
        taken = {step: swap(blocks[step], axis, size, step) for step in range(size - 1, 0, -1)}
        return [blocks[0]] + [taken[step] for step in range(1, size)]

    chunks = max(1, width // (2 * LANE))
    query_rows = queries.shape[2] // (width // chunks)
    packed = pl.pallas_call(
        functools.partial(gather_kernel, pools),
        out_shape=[shape((pools * rows, width), bf16)]
        + [shape((rows + query_rows, width // chunks), bf16)] * pools
        + [shape((rows, width // chunks), bf16)] * (pools * (chunks - 1)),
        in_specs=[SMEM, HBM, HBM],
        out_specs=[VMEM] * (pools * chunks + 1),
        scratch_shapes=[
            pltpu.VMEM((pools * rows, 2 * width), bf16),
            pltpu.VMEM((1, queries.shape[2]), bf16),
            pltpu.SemaphoreType.DMA((pools * CAP + 1,)),
        ],
        compiler_params=params(16),
        name="gather",
    )(in_hbm(selected), in_hbm(latents), in_hbm(queries))
    keys, values = packed[0], packed[1:]
    late = (chunks - 1) * pools + (1 if chunks > 1 else 1)

    cosine, sine, turn, live, place, key_maps, value_maps, held = pl.pallas_call(
        functools.partial(table_kernel, pools, shard_blocks),
        out_shape=[shape((pools * rows, HEAD_SIZE), f32)] * 2
        + [shape((2 * pools, HEAD_SIZE), f32), shape((pools, rows), i32), shape((1, pools * rows), i32)]
        + [shape(key_latent_maps.shape, bf16), shape(value_latent_maps.shape, bf16)]
        + [shape(values[late].shape, bf16)],
        in_specs=[SMEM, SMEM, VMEM] + [ANY] * 3,
        out_specs=[VMEM] * 7 + [ANY],
        input_output_aliases={5: 7},
        scratch_shapes=[pltpu.SemaphoreType.DMA((2,))],
        compiler_params=params(16),
        name="tables",
    )(
        in_hbm(selected), in_hbm(lengths), in_hbm(freq), in_hbm(key_latent_maps),
        in_hbm(value_latent_maps), values[late],
    )
    key_parts = exchange(keys, "heads", heads)
    values = [*values[:late], held, *values[late + 1 :]]
    value_parts = [scatter(values[c * pools : (c + 1) * pools], "pool", pools) for c in range(chunks)]

    turned = pl.pallas_call(
        functools.partial(rebuild_kernel, pools, heads),
        out_shape=shape((pools * rows, own_heads // QUERY_PER_GROUP * HEAD_SIZE), bf16),
        in_specs=[VMEM] * (3 + heads),
        out_specs=VMEM,
        compiler_params=params(20),
        name="rebuild",
    )(key_maps, cosine, sine, *key_parts)
    dense, *scores = pl.pallas_call(
        functools.partial(score_kernel, pools),
        out_shape=[shape((sel_count * BLOCK, width // chunks), bf16)]
        + [shape((own_heads, rows), f32)] * pools,
        in_specs=[VMEM] * (4 + pools),
        out_specs=[VMEM] * (1 + pools),
        compiler_params=params(16),
        name="score",
    )(turn, live, place, turned, *value_parts[0][::-1])
    score_parts = scatter(scores, "pool", pools)
    dense = [dense]
    for parts in value_parts[1:]:
        dense.append(pl.pallas_call(
            functools.partial(compact_kernel, pools),
            out_shape=shape((sel_count * BLOCK, width // chunks), bf16),
            in_specs=[VMEM] * (1 + pools) + [ANY] * (pools // 2),
            out_specs=VMEM,
            compiler_params=params(16),
            name="compact",
        )(place, *parts[::-1], *score_parts[pools // 2 :]))
    dense = [exchange(block, "heads", heads) for block in dense]
    dense_parts = [dense[c][j] for j in range(heads) for c in range(chunks)]

    mine = pl.pallas_call(
        functools.partial(attend_kernel, pools, heads, chunks),
        out_shape=shape((own_heads, HEAD_SIZE), bf16),
        in_specs=[VMEM] * (2 + pools + heads * chunks),
        out_specs=VMEM,
        compiler_params=params(16),
        name="attend",
    )(value_maps, place, *score_parts[::-1], *dense_parts)
    own_rows = join(*exchange(mine, "rep", reps))
    row_parts = exchange(own_rows, "pool", pools)

    own_columns = out_weight.shape[1]
    each = pools // heads
    parts = pl.pallas_call(
        functools.partial(project_kernel, pools, heads, reps),
        out_shape=[shape((each, own_columns), f32)] * (heads * reps),
        in_specs=[VMEM] * (pools + 1),
        out_specs=[VMEM] * (heads * reps),
        scratch_shapes=[pltpu.VMEM((pools * reps, own_columns), f32)],
        compiler_params=params(24),
        name="project",
    )(in_vmem(out_weight), *row_parts)
    return pl.pallas_call(
        functools.partial(finish_kernel, heads, reps),
        out_shape=shape((1, each, reps * own_columns), bf16),
        in_specs=[VMEM] * (heads * reps),
        out_specs=VMEM,
        compiler_params=params(4),
        name="finish",
    )(*scatter(parts, ("heads", "rep"), heads * reps)[::-1])


def solution(mesh):
    return jax.shard_map(
        per_device,
        mesh=mesh,
        in_specs=(
            P(("groups", "rep"), "pool", "heads"),
            P(("groups", "rep"), None, "pool", "heads"),
            P(None, "heads"),
            P(None, "heads"),
            P("heads", ("pool", "rep")),
            P(("groups", "rep"), None),
            P(("groups", "rep"), None, None),
        ),
        out_specs=P(("groups", "rep"), "heads", "pool"),
        check_vma=False,
    )
```

```python
import functools

import jax
import jax.numpy as jnp
import numpy as np
from jax import lax
from jax.experimental import pallas as pl
from jax.experimental.pallas import tpu as pltpu
from jax.sharding import PartitionSpec as P

HEAD_SIZE = 128
LANE = 64
BLOCK = 128
CAP = 2
QUERY_PER_GROUP = 8

ROPE_BASE = 500000.0
MASKED = -1e30
FAR = 1 << 29

SMEM = pl.BlockSpec(memory_space=pltpu.SMEM)
VMEM = pl.BlockSpec(memory_space=pltpu.VMEM)
ANY = pl.BlockSpec(memory_space=pl.ANY)
HBM = pl.BlockSpec(memory_space=pltpu.HBM)


def frequencies():
    half = HEAD_SIZE // 2
    exponents = np.arange(half, dtype=np.float32) * np.float32(2.0 / HEAD_SIZE)
    freq = np.power(np.float64(ROPE_BASE), -exponents.astype(np.float64)).astype(np.float32)
    return np.concatenate([freq, freq])[None, :]


def swap(value, axes, size, step):
    return lax.ppermute(value, axes, [(i, i ^ step) for i in range(size)])


def in_hbm(value):
    return pltpu.with_memory_space_constraint(value, pltpu.HBM)


def in_vmem(value):
    return pltpu.with_memory_space_constraint(value, pltpu.VMEM)


def params(mib, **more):
    return pltpu.CompilerParams(vmem_limit_bytes=mib << 20, **more)


def slot_blocks(sel_ref, seq, shard, shard_blocks):
    first = jnp.int32(-1)
    second = jnp.int32(-1)
    for i in range(sel_ref.shape[2]):
        block = sel_ref[0, seq, i]
        here = (block >= shard * shard_blocks) & (block < (shard + 1) * shard_blocks)
        second = jnp.where(here & (first >= 0), block, second)
        first = jnp.where(here & (first < 0), block, first)
    return first, second


def heads_to_rows(line, lanes):
    count = line.shape[1] // HEAD_SIZE
    rows = jnp.concatenate([line[:, n * HEAD_SIZE : (n + 1) * HEAD_SIZE] for n in range(count)], axis=0)
    if lanes < HEAD_SIZE:
        return jnp.concatenate([rows[:, i : i + lanes] for i in range(0, HEAD_SIZE, lanes)], axis=0)
    each = count * HEAD_SIZE // lanes
    return jnp.concatenate([rows[i : i + each, :] for i in range(0, count, each)], axis=1)


def rows_to_heads(rows):
    count, lanes = rows.shape
    if lanes < HEAD_SIZE:
        each = count * lanes // HEAD_SIZE
        return jnp.concatenate([rows[i : i + each, :] for i in range(0, count, each)], axis=1)
    return jnp.concatenate([rows[:, i : i + HEAD_SIZE] for i in range(0, lanes, HEAD_SIZE)], axis=0)


def gather_kernel(pools, sel_ref, lat_ref, query_ref, keys_ref, *rest):
    value_refs = rest[:pools]
    raw, line, sems = rest[pools:]
    load = pltpu.make_async_copy(query_ref.at[0], line, sems.at[pools * CAP])
    load.start()
    shard_blocks = lat_ref.shape[2] // BLOCK
    columns = lat_ref.shape[3]
    width = columns // 2
    rows = CAP * BLOCK
    me = lax.axis_index("pool")
    copies = {}
    for k in range(pools - 1, -1, -1):
        seq = me ^ k
        for c, block in enumerate(slot_blocks(sel_ref, seq, me, shard_blocks)):
            local = jnp.maximum(block - me * shard_blocks, 0)
            copies[k, c] = pltpu.make_async_copy(
                lat_ref.at[0, seq, pl.ds(pl.multiple_of(local * BLOCK, BLOCK), BLOCK), :],
                raw.at[pl.ds((k * CAP + c) * BLOCK, BLOCK), :],
                sems.at[k * CAP + c],
            )
            copies[k, c].start()
    chunk = min(4 * LANE, columns)
    half = chunk // 2
    source = lax.broadcasted_iota(jnp.int32, (chunk, chunk), 0)
    target = lax.broadcasted_iota(jnp.int32, (chunk, chunk), 1)
    within = target & (half - 1)
    wanted = ((within >> 6) << 7) + (within & (LANE - 1)) + jnp.where(target >= half, LANE, 0)
    pick = (source == wanted).astype(jnp.float32).astype(jnp.bfloat16)
    load.wait()
    queries = heads_to_rows(line[...].astype(jnp.float32), width).astype(jnp.bfloat16)
    for copy in copies.values():
        copy.wait()
    for k in range(pools - 1, -1, -1):
        for j in range(columns // chunk):
            packed = jnp.dot(
                raw[k * rows : (k + 1) * rows, j * chunk : (j + 1) * chunk], pick,
                preferred_element_type=jnp.float32,
            ).astype(jnp.bfloat16)
            keys_ref[k * rows : (k + 1) * rows, j * half : (j + 1) * half] = packed[:, :half]
            value_refs[k][:rows, j * half : (j + 1) * half] = packed[:, half:]
        value_refs[k][rows:, :] = queries


def table_kernel(pools, shard_blocks, sel_ref, len_ref, freq_ref, key_map_ref, value_map_ref, held_ref, *rest):
    cos_ref, sin_ref, turn_ref, live_ref, place_ref, key_out_ref, value_out_ref = rest[:7]
    sems = rest[-1]
    loads = [
        pltpu.make_async_copy(key_map_ref, key_out_ref, sems.at[0]),
        pltpu.make_async_copy(value_map_ref, value_out_ref, sems.at[1]),
    ]
    for load in loads:
        load.start()
    me = lax.axis_index("pool")
    lane = lax.broadcasted_iota(jnp.int32, (BLOCK, HEAD_SIZE), 1)
    row = lax.broadcasted_iota(jnp.int32, (BLOCK, HEAD_SIZE), 0)
    front = lane < HEAD_SIZE // 2
    across = lax.broadcasted_iota(jnp.int32, (1, BLOCK), 1)
    place = jnp.int32(0)
    for k in range(pools):
        turn_ref[k : k + 1, :] = len_ref[0, me ^ k].astype(jnp.float32) * freq_ref[...]
    angle = turn_ref[0:pools, :]
    turn_ref[0:pools, :] = jnp.cos(angle)
    turn_ref[pools:, :] = jnp.where(front[:1, :], -jnp.sin(angle), jnp.sin(angle))
    for k in range(pools):
        seq = me ^ k
        found = slot_blocks(sel_ref, seq, me, shard_blocks)
        one, two = [jnp.maximum(block, 0) * BLOCK for block in found]
        angle = (jnp.where(front, one, two) + row).astype(jnp.float32) * freq_ref[...]
        for ref, table, sign in ((cos_ref, jnp.cos(angle), 1.0), (sin_ref, jnp.sin(angle), -1.0)):
            turned = pltpu.roll(table, HEAD_SIZE // 2, 1)
            at = k * CAP * BLOCK
            ref[at : at + BLOCK, :] = jnp.where(front, sign * table, turned)
            ref[at + BLOCK : at + 2 * BLOCK, :] = jnp.where(front, sign * turned, table)
        mine = slot_blocks(sel_ref, me, seq, shard_blocks)
        for c in range(CAP):
            start = jnp.where(found[c] < 0, FAR, found[c] * BLOCK)
            live_ref[k : k + 1, c * BLOCK : (c + 1) * BLOCK] = (start + across < len_ref[0, seq]).astype(jnp.int32)
            at = (k * CAP + c) * BLOCK
            used = mine[c] >= 0
            place_ref[:, at : at + BLOCK] = jnp.where(used, place, -1) + 0 * across
            place = place + used.astype(jnp.int32)
    for load in loads:
        load.wait()


def rebuild_kernel(pools, heads, map_ref, cos_ref, sin_ref, *rest):
    key_refs = rest[:heads]
    out_ref = rest[heads]
    head = lax.axis_index("heads")
    width = key_refs[0].shape[1]
    rows = CAP * BLOCK
    maps = []
    for j in range(heads):
        owner = head ^ j
        maps.append(map_ref[pl.ds(pl.multiple_of(owner * width, width), width), :])
    for k in range(pools):
        at = slice(k * rows, (k + 1) * rows)
        rebuilt = jnp.dot(key_refs[0][at, :], maps[0], preferred_element_type=jnp.float32)
        for j in range(1, heads):
            rebuilt += jnp.dot(key_refs[j][at, :], maps[j], preferred_element_type=jnp.float32)
        cosine = cos_ref[at, :]
        sine = sin_ref[at, :]
        for g in range(map_ref.shape[1] // HEAD_SIZE):
            lanes = slice(g * HEAD_SIZE, (g + 1) * HEAD_SIZE)
            one = rebuilt[:, lanes]
            out_ref[at, lanes] = (one * cosine + pltpu.roll(one, HEAD_SIZE // 2, 1) * sine).astype(jnp.bfloat16)


def score_kernel(pools, turn_ref, live_ref, place_ref, key_ref, *rest):
    pay_refs = rest[:pools][::-1]
    dense_ref, out_ref = rest[pools:]
    me = lax.axis_index("pool")
    groups = key_ref.shape[1] // HEAD_SIZE
    rows = CAP * BLOCK
    width = dense_ref.shape[1]
    kept = dense_ref.shape[0] // BLOCK
    for k in range(pools - 1, -1, -1):
        live = live_ref[k : k + 1, :] > 0
        query = rows_to_heads(pay_refs[k][rows:, :].astype(jnp.float32))
        query = query * turn_ref[k : k + 1, :] + pltpu.roll(query, HEAD_SIZE // 2, 1) * turn_ref[
            pools + k : pools + k + 1, :
        ]
        query = query.astype(jnp.bfloat16)
        for g in range(groups):
            mine = slice(g * QUERY_PER_GROUP, (g + 1) * QUERY_PER_GROUP)
            scores = lax.dot_general(
                query[mine, :], key_ref[k * rows : (k + 1) * rows, g * HEAD_SIZE : (g + 1) * HEAD_SIZE],
                (((1,), (1,)), ((), ())), preferred_element_type=jnp.float32,
            ) * (HEAD_SIZE ** -0.5)
            out_ref[me ^ k, mine, :] = jnp.where(live, scores, MASKED)
    spare = pools * CAP - kept
    for i in range(kept):
        chosen = jnp.zeros((BLOCK, width), jnp.float32)
        for slot in range(i, i + spare + 1):
            place = place_ref[:, slot * BLOCK : slot * BLOCK + LANE]
            place = jnp.concatenate([place] * (width // LANE), axis=1)
            k, c = slot // CAP, slot % CAP
            block = pay_refs[k][c * BLOCK : (c + 1) * BLOCK, :].astype(jnp.float32)
            chosen = jnp.where(place == i, block, chosen)
        dense_ref[i * BLOCK : (i + 1) * BLOCK, :] = chosen.astype(jnp.bfloat16)


def attend_kernel(pools, heads, map_ref, place_ref, *rest):
    score_ref = rest[0]
    value_refs = rest[1 : 1 + heads]
    me = lax.axis_index("pool")
    out_ref = rest[-1]
    head = lax.axis_index("heads")
    width = value_refs[0].shape[1]
    groups = map_ref.shape[1] // HEAD_SIZE
    scores = [score_ref[me ^ k] for k in range(pools)]
    top = functools.reduce(jnp.maximum, [jnp.max(s, axis=1, keepdims=True) for s in scores])
    weights = [jnp.exp(s - top) for s in scores]
    total = functools.reduce(jnp.add, [jnp.sum(w, axis=1, keepdims=True) for w in weights])
    slots = []
    for k in range(pools):
        attention = weights[k] / total
        for c in range(CAP):
            at = (k * CAP + c) * BLOCK
            slots.append((place_ref[:, at : at + BLOCK], attention[:, c * BLOCK : (c + 1) * BLOCK]))
    dense = []
    kept = value_refs[0].shape[0] // BLOCK
    for i in range(kept):
        chosen = jnp.zeros_like(slots[0][1])
        for place, attention in slots[i : i + len(slots) - kept + 1]:
            chosen = jnp.where(place == i, attention, chosen)
        dense.append(chosen)
    attention = jnp.concatenate(dense, axis=1).astype(jnp.bfloat16)
    mixed = [None] * groups
    for j in range(heads):
        owner = head ^ j
        context = jnp.dot(
            attention, value_refs[j][...], preferred_element_type=jnp.float32
        ).astype(jnp.bfloat16)
        rows = pl.ds(pl.multiple_of(owner * width, width), width)
        for g in range(groups):
            part = jnp.dot(
                context[g * QUERY_PER_GROUP : (g + 1) * QUERY_PER_GROUP, :],
                map_ref[rows, g * HEAD_SIZE : (g + 1) * HEAD_SIZE],
                preferred_element_type=jnp.float32,
            )
            mixed[g] = part if j == 0 else mixed[g] + part
    for g in range(groups):
        for q in range(QUERY_PER_GROUP):
            at = (g * QUERY_PER_GROUP + q) * HEAD_SIZE
            out_ref[:, at : at + HEAD_SIZE] = mixed[g][q : q + 1, :].astype(jnp.bfloat16)


def join_kernel(*refs):
    rows = [ref[...].astype(jnp.float32) for ref in refs[:-1]]
    rows = jnp.concatenate(rows, axis=0).astype(jnp.bfloat16)
    for i in range(refs[-1].shape[0]):
        refs[-1][i] = rows


def project_kernel(pools, heads, reps, weight_ref, row_ref, *rest):
    out_refs = rest[:-1]
    acc = rest[-1]
    left = jnp.concatenate([row_ref[i].astype(jnp.float32) for i in range(pools)], axis=0).astype(jnp.bfloat16)
    acc[...] = jnp.dot(left, weight_ref[...], preferred_element_type=jnp.float32)
    head = lax.axis_index("heads")
    each = pools // heads
    for d in range(heads * reps):
        for u in range(each):
            n = ((head ^ (d // reps)) * each + u) * reps + d % reps
            out_refs[d][u : u + 1, :] = acc[pl.ds(n, 1), :]


def finish_kernel(heads, reps, *refs):
    out_ref = refs[-1]
    refs = refs[:-1][::-1]
    rep = lax.axis_index("rep")
    width = refs[0].shape[1]
    for t in range(reps):
        total = functools.reduce(jnp.add, [refs[j * reps + t][...] for j in range(heads)])
        columns = pl.ds(pl.multiple_of((rep ^ t) * width, width), width)
        out_ref[0, :, columns] = total.astype(jnp.bfloat16)


def per_device(queries, latents, key_latent_maps, value_latent_maps, out_weight, lengths, selected):
    pools = lax.axis_size("pool")
    heads = lax.axis_size("heads")
    reps = lax.axis_size("rep")
    half_seqs, sel_count = selected.shape[1:]
    assert half_seqs == pools and pools % heads == 0
    shard_blocks = latents.shape[2] // BLOCK
    width = latents.shape[3] // 2
    rows = CAP * BLOCK
    own_heads = queries.shape[2] // HEAD_SIZE
    bf16, f32, i32 = jnp.bfloat16, jnp.float32, jnp.int32
    shape = jax.ShapeDtypeStruct
    freq = jnp.asarray(frequencies())

    def join(*blocks):
        return pl.pallas_call(
            join_kernel,
            out_shape=shape((pools, len(blocks), queries.shape[2]), bf16),
            in_specs=[VMEM] * len(blocks),
            out_specs=VMEM,
            compiler_params=params(4),
            name="join",
        )(*blocks)

    def exchange(value, axis, size):
        taken = {step: swap(value, axis, size, step) for step in range(size - 1, 0, -1)}
        return [value] + [taken[step] for step in range(1, size)]

    def scatter(blocks, axis, size):
        taken = {step: swap(blocks[step], axis, size, step) for step in range(size - 1, 0, -1)}
        return [blocks[0]] + [taken[step] for step in range(1, size)]

    query_rows = queries.shape[2] // width
    packed = pl.pallas_call(
        functools.partial(gather_kernel, pools),
        out_shape=[shape((pools * rows, width), bf16)]
        + [shape((rows + query_rows, width), bf16)] * pools,
        in_specs=[SMEM, HBM, HBM],
        out_specs=[VMEM] * (pools + 1),
        scratch_shapes=[
            pltpu.VMEM((pools * rows, 2 * width), bf16),
            pltpu.VMEM((1, queries.shape[2]), bf16),
            pltpu.SemaphoreType.DMA((pools * CAP + 1,)),
        ],
        compiler_params=params(16),
        name="gather",
    )(in_hbm(selected), in_hbm(latents), in_hbm(queries))
    keys, values = packed[0], packed[1:]

    cosine, sine, turn, live, place, key_maps, value_maps, held = pl.pallas_call(
        functools.partial(table_kernel, pools, shard_blocks),
        out_shape=[shape((pools * rows, HEAD_SIZE), f32)] * 2
        + [shape((2 * pools, HEAD_SIZE), f32), shape((pools, rows), i32), shape((1, pools * rows), i32)]
        + [shape(key_latent_maps.shape, bf16), shape(value_latent_maps.shape, bf16)]
        + [shape(values[1].shape, bf16)],
        in_specs=[SMEM, SMEM, VMEM] + [ANY] * 3,
        out_specs=[VMEM] * 7 + [ANY],
        scratch_shapes=[pltpu.SemaphoreType.DMA((2,))],
        input_output_aliases={5: 7},
        compiler_params=params(16),
        name="tables",
    )(
        in_hbm(selected), in_hbm(lengths), in_hbm(freq), in_hbm(key_latent_maps),
        in_hbm(value_latent_maps), values[1],
    )
    key_parts = exchange(keys, "heads", heads)
    value_parts = scatter([values[0], held, *values[2:]], "pool", pools)

    turned = pl.pallas_call(
        functools.partial(rebuild_kernel, pools, heads),
        out_shape=shape((pools * rows, own_heads // QUERY_PER_GROUP * HEAD_SIZE), bf16),
        in_specs=[VMEM] * (3 + heads),
        out_specs=VMEM,
        compiler_params=params(20),
        name="rebuild",
    )(key_maps, cosine, sine, *key_parts)
    dense, scores = pl.pallas_call(
        functools.partial(score_kernel, pools),
        out_shape=[shape((sel_count * BLOCK, width), bf16), shape((pools, own_heads, rows), f32)],
        in_specs=[VMEM] * (4 + pools),
        out_specs=[VMEM] * 2,
        compiler_params=params(16),
        name="score",
    )(turn, live, place, turned, *value_parts[::-1])
    dense_parts = exchange(dense, "heads", heads)
    score_parts = lax.all_to_all(scores, "pool", split_axis=0, concat_axis=0, tiled=True)

    mine = pl.pallas_call(
        functools.partial(attend_kernel, pools, heads),
        out_shape=shape((1, own_heads * HEAD_SIZE), bf16),
        in_specs=[VMEM] * (3 + heads),
        out_specs=VMEM,
        compiler_params=params(16),
        name="attend",
    )(value_maps, place, score_parts, *dense_parts)
    own_rows = join(*exchange(mine, "rep", reps))
    all_rows = lax.all_to_all(own_rows, "pool", split_axis=0, concat_axis=0, tiled=True)

    own_columns = out_weight.shape[1]
    each = pools // heads
    parts = pl.pallas_call(
        functools.partial(project_kernel, pools, heads, reps),
        out_shape=[shape((each, own_columns), f32)] * (heads * reps),
        in_specs=[VMEM] * 2,
        out_specs=[VMEM] * (heads * reps),
        scratch_shapes=[pltpu.VMEM((pools * reps, own_columns), f32)],
        compiler_params=params(24),
        name="project",
    )(in_vmem(out_weight), all_rows)
    return pl.pallas_call(
        functools.partial(finish_kernel, heads, reps),
        out_shape=shape((1, each, reps * own_columns), bf16),
        in_specs=[VMEM] * (heads * reps),
        out_specs=VMEM,
        compiler_params=params(4),
        name="finish",
    )(*scatter(parts, ("heads", "rep"), heads * reps)[::-1])


def solution(mesh):
    return jax.shard_map(
        per_device,
        mesh=mesh,
        in_specs=(
            P(("groups", "rep"), "pool", "heads"),
            P(("groups", "rep"), None, "pool", "heads"),
            P(None, "heads"),
            P(None, "heads"),
            P("heads", ("pool", "rep")),
            P(("groups", "rep"), None),
            P(("groups", "rep"), None, None),
        ),
        out_specs=P(("groups", "rep"), "heads", "pool"),
        check_vma=False,
    )
```

```python
import functools

import jax
import jax.numpy as jnp
import numpy as np
from jax import lax
from jax.experimental import pallas as pl
from jax.experimental.pallas import tpu as pltpu
from jax.sharding import PartitionSpec as P

HEAD_SIZE = 128
LANE = 64
BLOCK = 128
CAP = 2
QUERY_PER_GROUP = 8

ROPE_BASE = 500000.0
MASKED = -1e30
FAR = 1 << 29

SMEM = pl.BlockSpec(memory_space=pltpu.SMEM)
VMEM = pl.BlockSpec(memory_space=pltpu.VMEM)
ANY = pl.BlockSpec(memory_space=pl.ANY)
HBM = pl.BlockSpec(memory_space=pltpu.HBM)


def frequencies():
    half = HEAD_SIZE // 2
    exponents = np.arange(half, dtype=np.float32) * np.float32(2.0 / HEAD_SIZE)
    freq = np.power(np.float64(ROPE_BASE), -exponents.astype(np.float64)).astype(np.float32)
    return np.concatenate([freq, freq])[None, :]


def swap(value, axes, size, step):
    return lax.ppermute(value, axes, [(i, i ^ step) for i in range(size)])


def in_hbm(value):
    return pltpu.with_memory_space_constraint(value, pltpu.HBM)


def in_vmem(value):
    return pltpu.with_memory_space_constraint(value, pltpu.VMEM)


def params(mib, **more):
    return pltpu.CompilerParams(vmem_limit_bytes=mib << 20, **more)


def slot_blocks(sel_ref, seq, shard, shard_blocks):
    first = jnp.int32(-1)
    second = jnp.int32(-1)
    for i in range(sel_ref.shape[2]):
        block = sel_ref[0, seq, i]
        here = (block >= shard * shard_blocks) & (block < (shard + 1) * shard_blocks)
        second = jnp.where(here & (first >= 0), block, second)
        first = jnp.where(here & (first < 0), block, first)
    return first, second


def heads_to_rows(line, lanes):
    count = line.shape[1] // HEAD_SIZE
    rows = jnp.concatenate([line[:, n * HEAD_SIZE : (n + 1) * HEAD_SIZE] for n in range(count)], axis=0)
    if lanes < HEAD_SIZE:
        return jnp.concatenate([rows[:, i : i + lanes] for i in range(0, HEAD_SIZE, lanes)], axis=0)
    each = count * HEAD_SIZE // lanes
    return jnp.concatenate([rows[i : i + each, :] for i in range(0, count, each)], axis=1)


def rows_to_heads(rows):
    count, lanes = rows.shape
    if lanes < HEAD_SIZE:
        each = count * lanes // HEAD_SIZE
        return jnp.concatenate([rows[i : i + each, :] for i in range(0, count, each)], axis=1)
    return jnp.concatenate([rows[:, i : i + HEAD_SIZE] for i in range(0, lanes, HEAD_SIZE)], axis=0)


def gather_kernel(pools, sel_ref, lat_ref, query_ref, keys_ref, *rest):
    value_refs = rest[:pools]
    raw, sems = rest[pools:]
    shard_blocks = lat_ref.shape[2] // BLOCK
    columns = lat_ref.shape[3]
    width = columns // 2
    rows = CAP * BLOCK
    me = lax.axis_index("pool")
    copies = {}
    for k in range(pools - 1, -1, -1):
        seq = me ^ k
        for c, block in enumerate(slot_blocks(sel_ref, seq, me, shard_blocks)):
            local = jnp.maximum(block - me * shard_blocks, 0)
            copies[k, c] = pltpu.make_async_copy(
                lat_ref.at[0, seq, pl.ds(pl.multiple_of(local * BLOCK, BLOCK), BLOCK), :],
                raw.at[pl.ds((k * CAP + c) * BLOCK, BLOCK), :],
                sems.at[k * CAP + c],
            )
            copies[k, c].start()
    chunk = min(4 * LANE, columns)
    half = chunk // 2
    source = lax.broadcasted_iota(jnp.int32, (chunk, chunk), 0)
    target = lax.broadcasted_iota(jnp.int32, (chunk, chunk), 1)
    within = target & (half - 1)
    wanted = ((within >> 6) << 7) + (within & (LANE - 1)) + jnp.where(target >= half, LANE, 0)
    pick = (source == wanted).astype(jnp.float32).astype(jnp.bfloat16)
    queries = heads_to_rows(query_ref[0].astype(jnp.float32), width).astype(jnp.bfloat16)
    for copy in copies.values():
        copy.wait()
    for k in range(pools - 1, -1, -1):
        for j in range(columns // chunk):
            packed = jnp.dot(
                raw[k * rows : (k + 1) * rows, j * chunk : (j + 1) * chunk], pick,
                preferred_element_type=jnp.float32,
            ).astype(jnp.bfloat16)
            keys_ref[k * rows : (k + 1) * rows, j * half : (j + 1) * half] = packed[:, :half]
            value_refs[k][:rows, j * half : (j + 1) * half] = packed[:, half:]
        value_refs[k][rows:, :] = queries


def table_kernel(pools, shard_blocks, sel_ref, len_ref, freq_ref, key_map_ref, value_map_ref, held_ref, weight_ref, *rest):
    cos_ref, sin_ref, turn_ref, live_ref, place_ref, key_out_ref, value_out_ref = rest[:7]
    weight_out_ref = rest[8]
    sems = rest[-1]
    loads = [
        pltpu.make_async_copy(key_map_ref, key_out_ref, sems.at[0]),
        pltpu.make_async_copy(value_map_ref, value_out_ref, sems.at[1]),
        pltpu.make_async_copy(weight_ref, weight_out_ref, sems.at[2]),
    ]
    for load in loads:
        load.start()
    me = lax.axis_index("pool")
    lane = lax.broadcasted_iota(jnp.int32, (BLOCK, HEAD_SIZE), 1)
    row = lax.broadcasted_iota(jnp.int32, (BLOCK, HEAD_SIZE), 0)
    front = lane < HEAD_SIZE // 2
    across = lax.broadcasted_iota(jnp.int32, (1, BLOCK), 1)
    place = jnp.int32(0)
    for k in range(pools):
        turn_ref[k : k + 1, :] = len_ref[0, me ^ k].astype(jnp.float32) * freq_ref[...]
    angle = turn_ref[0:pools, :]
    turn_ref[0:pools, :] = jnp.cos(angle)
    turn_ref[pools:, :] = jnp.where(front[:1, :], -jnp.sin(angle), jnp.sin(angle))
    for k in range(pools):
        seq = me ^ k
        found = slot_blocks(sel_ref, seq, me, shard_blocks)
        one, two = [jnp.maximum(block, 0) * BLOCK for block in found]
        angle = (jnp.where(front, one, two) + row).astype(jnp.float32) * freq_ref[...]
        for ref, table, sign in ((cos_ref, jnp.cos(angle), 1.0), (sin_ref, jnp.sin(angle), -1.0)):
            turned = pltpu.roll(table, HEAD_SIZE // 2, 1)
            at = k * CAP * BLOCK
            ref[at : at + BLOCK, :] = jnp.where(front, sign * table, turned)
            ref[at + BLOCK : at + 2 * BLOCK, :] = jnp.where(front, sign * turned, table)
        mine = slot_blocks(sel_ref, me, seq, shard_blocks)
        for c in range(CAP):
            start = jnp.where(found[c] < 0, FAR, found[c] * BLOCK)
            live_ref[k : k + 1, c * BLOCK : (c + 1) * BLOCK] = (start + across < len_ref[0, seq]).astype(jnp.int32)
            at = (k * CAP + c) * BLOCK
            used = mine[c] >= 0
            place_ref[:, at : at + BLOCK] = jnp.where(used, place, -1) + 0 * across
            place = place + used.astype(jnp.int32)
    for load in loads:
        load.wait()


def rebuild_kernel(pools, heads, map_ref, cos_ref, sin_ref, *rest):
    key_refs = rest[:heads]
    out_ref = rest[heads]
    head = lax.axis_index("heads")
    width = key_refs[0].shape[1]
    rows = CAP * BLOCK
    maps = []
    for j in range(heads):
        owner = head ^ j
        maps.append(map_ref[pl.ds(pl.multiple_of(owner * width, width), width), :])
    for k in range(pools):
        at = slice(k * rows, (k + 1) * rows)
        rebuilt = jnp.dot(key_refs[0][at, :], maps[0], preferred_element_type=jnp.float32)
        for j in range(1, heads):
            rebuilt += jnp.dot(key_refs[j][at, :], maps[j], preferred_element_type=jnp.float32)
        cosine = cos_ref[at, :]
        sine = sin_ref[at, :]
        for g in range(map_ref.shape[1] // HEAD_SIZE):
            lanes = slice(g * HEAD_SIZE, (g + 1) * HEAD_SIZE)
            one = rebuilt[:, lanes]
            out_ref[at, lanes] = (one * cosine + pltpu.roll(one, HEAD_SIZE // 2, 1) * sine).astype(jnp.bfloat16)


def score_kernel(pools, turn_ref, live_ref, place_ref, key_ref, *rest):
    pay_refs = rest[:pools][::-1]
    dense_ref = rest[pools]
    out_refs = rest[pools + 1 :]
    groups = key_ref.shape[1] // HEAD_SIZE
    rows = CAP * BLOCK
    width = dense_ref.shape[1]
    kept = dense_ref.shape[0] // BLOCK
    for k in range(pools - 1, -1, -1):
        live = live_ref[k : k + 1, :] > 0
        query = rows_to_heads(pay_refs[k][rows:, :].astype(jnp.float32))
        query = query * turn_ref[k : k + 1, :] + pltpu.roll(query, HEAD_SIZE // 2, 1) * turn_ref[
            pools + k : pools + k + 1, :
        ]
        query = query.astype(jnp.bfloat16)
        for g in range(groups):
            mine = slice(g * QUERY_PER_GROUP, (g + 1) * QUERY_PER_GROUP)
            scores = lax.dot_general(
                query[mine, :], key_ref[k * rows : (k + 1) * rows, g * HEAD_SIZE : (g + 1) * HEAD_SIZE],
                (((1,), (1,)), ((), ())), preferred_element_type=jnp.float32,
            ) * (HEAD_SIZE ** -0.5)
            out_refs[k][mine, :] = jnp.where(live, scores, MASKED)
    spare = pools * CAP - kept
    for i in range(kept):
        chosen = jnp.zeros((BLOCK, width), jnp.float32)
        for slot in range(i, i + spare + 1):
            place = place_ref[:, slot * BLOCK : slot * BLOCK + LANE]
            place = jnp.concatenate([place] * (width // LANE), axis=1)
            k, c = slot // CAP, slot % CAP
            block = pay_refs[k][c * BLOCK : (c + 1) * BLOCK, :].astype(jnp.float32)
            chosen = jnp.where(place == i, block, chosen)
        dense_ref[i * BLOCK : (i + 1) * BLOCK, :] = chosen.astype(jnp.bfloat16)


def attend_kernel(pools, heads, map_ref, place_ref, *rest):
    score_refs = rest[:pools][::-1]
    value_refs = rest[pools : pools + heads]
    out_ref = rest[-1]
    head = lax.axis_index("heads")
    width = value_refs[0].shape[1]
    groups = map_ref.shape[1] // HEAD_SIZE
    scores = [ref[...] for ref in score_refs]
    top = functools.reduce(jnp.maximum, [jnp.max(s, axis=1, keepdims=True) for s in scores])
    weights = [jnp.exp(s - top) for s in scores]
    total = functools.reduce(jnp.add, [jnp.sum(w, axis=1, keepdims=True) for w in weights])
    slots = []
    for k in range(pools):
        attention = weights[k] / total
        for c in range(CAP):
            at = (k * CAP + c) * BLOCK
            slots.append((place_ref[:, at : at + BLOCK], attention[:, c * BLOCK : (c + 1) * BLOCK]))
    dense = []
    kept = value_refs[0].shape[0] // BLOCK
    for i in range(kept):
        chosen = jnp.zeros_like(slots[0][1])
        for place, attention in slots[i : i + len(slots) - kept + 1]:
            chosen = jnp.where(place == i, attention, chosen)
        dense.append(chosen)
    attention = jnp.concatenate(dense, axis=1).astype(jnp.bfloat16)
    mixed = [None] * groups
    for j in range(heads):
        owner = head ^ j
        context = jnp.dot(
            attention, value_refs[j][...], preferred_element_type=jnp.float32
        ).astype(jnp.bfloat16)
        rows = pl.ds(pl.multiple_of(owner * width, width), width)
        for g in range(groups):
            part = jnp.dot(
                context[g * QUERY_PER_GROUP : (g + 1) * QUERY_PER_GROUP, :],
                map_ref[rows, g * HEAD_SIZE : (g + 1) * HEAD_SIZE],
                preferred_element_type=jnp.float32,
            )
            mixed[g] = part if j == 0 else mixed[g] + part
    for g in range(groups):
        for q in range(QUERY_PER_GROUP):
            at = (g * QUERY_PER_GROUP + q) * HEAD_SIZE
            out_ref[:, at : at + HEAD_SIZE] = mixed[g][q : q + 1, :].astype(jnp.bfloat16)


def join_kernel(*refs):
    rows = [ref[...].reshape(-1, ref.shape[-1]).astype(jnp.float32) for ref in refs[:-1]]
    refs[-1][...] = jnp.concatenate(rows, axis=0).astype(jnp.bfloat16)


def project_kernel(pools, heads, reps, weight_ref, *rest):
    row_refs = rest[:pools]
    out_refs = rest[pools:-1]
    acc = rest[-1]
    left = jnp.concatenate([ref[...].astype(jnp.float32) for ref in row_refs], axis=0).astype(jnp.bfloat16)
    acc[...] = jnp.dot(left, weight_ref[...], preferred_element_type=jnp.float32)
    pool = lax.axis_index("pool")
    head = lax.axis_index("heads")
    each = pools // heads
    for d in range(heads * reps):
        for u in range(each):
            n = (pool ^ ((head ^ (d // reps)) * each + u)) * reps + d % reps
            out_refs[d][u : u + 1, :] = acc[pl.ds(n, 1), :]


def finish_kernel(heads, reps, *refs):
    out_ref = refs[-1]
    refs = refs[:-1][::-1]
    rep = lax.axis_index("rep")
    width = refs[0].shape[1]
    for t in range(reps):
        total = functools.reduce(jnp.add, [refs[j * reps + t][...] for j in range(heads)])
        columns = pl.ds(pl.multiple_of((rep ^ t) * width, width), width)
        out_ref[0, :, columns] = total.astype(jnp.bfloat16)


def per_device(queries, latents, key_latent_maps, value_latent_maps, out_weight, lengths, selected):
    pools = lax.axis_size("pool")
    heads = lax.axis_size("heads")
    reps = lax.axis_size("rep")
    half_seqs, sel_count = selected.shape[1:]
    assert half_seqs == pools and pools % heads == 0
    shard_blocks = latents.shape[2] // BLOCK
    width = latents.shape[3] // 2
    rows = CAP * BLOCK
    own_heads = queries.shape[2] // HEAD_SIZE
    bf16, f32, i32 = jnp.bfloat16, jnp.float32, jnp.int32
    shape = jax.ShapeDtypeStruct
    freq = jnp.asarray(frequencies())

    def join(*blocks):
        return pl.pallas_call(
            join_kernel,
            out_shape=shape((sum(block.size for block in blocks) // queries.shape[2], queries.shape[2]), bf16),
            in_specs=[VMEM] * len(blocks),
            out_specs=VMEM,
            compiler_params=params(4),
            name="join",
        )(*blocks)

    def exchange(value, axis, size):
        taken = {step: swap(value, axis, size, step) for step in range(size - 1, 0, -1)}
        return [value] + [taken[step] for step in range(1, size)]

    def scatter(blocks, axis, size):
        taken = {step: swap(blocks[step], axis, size, step) for step in range(size - 1, 0, -1)}
        return [blocks[0]] + [taken[step] for step in range(1, size)]

    query_rows = queries.shape[2] // width
    packed = pl.pallas_call(
        functools.partial(gather_kernel, pools),
        out_shape=[shape((pools * rows, width), bf16)]
        + [shape((rows + query_rows, width), bf16)] * pools,
        in_specs=[SMEM, HBM, VMEM],
        out_specs=[VMEM] * (pools + 1),
        scratch_shapes=[
            pltpu.VMEM((pools * rows, 2 * width), bf16),
            pltpu.SemaphoreType.DMA((pools * CAP,)),
        ],
        compiler_params=params(16),
        name="gather",
    )(in_hbm(selected), in_hbm(latents), in_hbm(queries))
    keys, values = packed[0], packed[1:]

    cosine, sine, turn, live, place, key_maps, value_maps, held, weight = pl.pallas_call(
        functools.partial(table_kernel, pools, shard_blocks),
        out_shape=[shape((pools * rows, HEAD_SIZE), f32)] * 2
        + [shape((2 * pools, HEAD_SIZE), f32), shape((pools, rows), i32), shape((1, pools * rows), i32)]
        + [shape(key_latent_maps.shape, bf16), shape(value_latent_maps.shape, bf16)]
        + [shape(values[1].shape, bf16), shape(out_weight.shape, bf16)],
        in_specs=[SMEM, SMEM, VMEM] + [ANY] * 3 + [HBM],
        out_specs=[VMEM] * 7 + [ANY, VMEM],
        scratch_shapes=[pltpu.SemaphoreType.DMA((3,))],
        input_output_aliases={5: 7},
        compiler_params=params(16),
        name="tables",
    )(
        in_hbm(selected), in_hbm(lengths), in_hbm(freq), in_hbm(key_latent_maps),
        in_hbm(value_latent_maps), values[1], in_hbm(out_weight),
    )
    key_parts = exchange(keys, "heads", heads)
    value_parts = scatter([values[0], held, *values[2:]], "pool", pools)

    turned = pl.pallas_call(
        functools.partial(rebuild_kernel, pools, heads),
        out_shape=shape((pools * rows, own_heads // QUERY_PER_GROUP * HEAD_SIZE), bf16),
        in_specs=[VMEM] * (3 + heads),
        out_specs=VMEM,
        compiler_params=params(20),
        name="rebuild",
    )(key_maps, cosine, sine, *key_parts)
    dense, *scores = pl.pallas_call(
        functools.partial(score_kernel, pools),
        out_shape=[shape((sel_count * BLOCK, width), bf16)] + [shape((own_heads, rows), f32)] * pools,
        in_specs=[VMEM] * (4 + pools),
        out_specs=[VMEM] * (1 + pools),
        compiler_params=params(16),
        name="score",
    )(turn, live, place, turned, *value_parts[::-1])
    dense_parts = exchange(dense, "heads", heads)
    score_parts = scatter(scores, "pool", pools)

    mine = pl.pallas_call(
        functools.partial(attend_kernel, pools, heads),
        out_shape=shape((1, own_heads * HEAD_SIZE), bf16),
        in_specs=[VMEM] * (2 + pools + heads),
        out_specs=VMEM,
        compiler_params=params(16),
        name="attend",
    )(value_maps, place, *score_parts[::-1], *dense_parts)
    own_rows = join(*exchange(mine, "rep", reps))
    row_parts = exchange(own_rows, "pool", pools)

    own_columns = out_weight.shape[1]
    each = pools // heads
    parts = pl.pallas_call(
        functools.partial(project_kernel, pools, heads, reps),
        out_shape=[shape((each, own_columns), f32)] * (heads * reps),
        in_specs=[VMEM] * (pools + 1),
        out_specs=[VMEM] * (heads * reps),
        scratch_shapes=[pltpu.VMEM((pools * reps, own_columns), f32)],
        compiler_params=params(24),
        name="project",
    )(weight, *row_parts)
    return pl.pallas_call(
        functools.partial(finish_kernel, heads, reps),
        out_shape=shape((1, each, reps * own_columns), bf16),
        in_specs=[VMEM] * (heads * reps),
        out_specs=VMEM,
        compiler_params=params(4),
        name="finish",
    )(*scatter(parts, ("heads", "rep"), heads * reps)[::-1])


def solution(mesh):
    return jax.shard_map(
        per_device,
        mesh=mesh,
        in_specs=(
            P(("groups", "rep"), "pool", "heads"),
            P(("groups", "rep"), None, "pool", "heads"),
            P(None, "heads"),
            P(None, "heads"),
            P("heads", ("pool", "rep")),
            P(("groups", "rep"), None),
            P(("groups", "rep"), None, None),
        ),
        out_specs=P(("groups", "rep"), "heads", "pool"),
        check_vma=False,
    )
```

```python
import functools

import jax
import jax.numpy as jnp
import numpy as np
from jax import lax
from jax.experimental import pallas as pl
from jax.experimental.pallas import tpu as pltpu
from jax.sharding import PartitionSpec as P

HEAD_SIZE = 128
LANE = 64
BLOCK = 128
CAP = 2
QUERY_PER_GROUP = 8

ROPE_BASE = 500000.0
MASKED = -1e30
FAR = 1 << 29

SMEM = pl.BlockSpec(memory_space=pltpu.SMEM)
VMEM = pl.BlockSpec(memory_space=pltpu.VMEM)
ANY = pl.BlockSpec(memory_space=pl.ANY)
HBM = pl.BlockSpec(memory_space=pltpu.HBM)


def frequencies():
    half = HEAD_SIZE // 2
    exponents = np.arange(half, dtype=np.float32) * np.float32(2.0 / HEAD_SIZE)
    freq = np.power(np.float64(ROPE_BASE), -exponents.astype(np.float64)).astype(np.float32)
    return np.concatenate([freq, freq])[None, :]


def swap(value, axes, size, step):
    return lax.ppermute(value, axes, [(i, i ^ step) for i in range(size)])


def in_hbm(value):
    return pltpu.with_memory_space_constraint(value, pltpu.HBM)


def in_vmem(value):
    return pltpu.with_memory_space_constraint(value, pltpu.VMEM)


def params(mib, **more):
    return pltpu.CompilerParams(vmem_limit_bytes=mib << 20, **more)


def slot_blocks(sel_ref, seq, shard, shard_blocks):
    first = jnp.int32(-1)
    second = jnp.int32(-1)
    for i in range(sel_ref.shape[2]):
        block = sel_ref[0, seq, i]
        here = (block >= shard * shard_blocks) & (block < (shard + 1) * shard_blocks)
        second = jnp.where(here & (first >= 0), block, second)
        first = jnp.where(here & (first < 0), block, first)
    return first, second


def heads_to_rows(line, lanes):
    count = line.shape[1] // HEAD_SIZE
    rows = jnp.concatenate([line[:, n * HEAD_SIZE : (n + 1) * HEAD_SIZE] for n in range(count)], axis=0)
    if lanes < HEAD_SIZE:
        return jnp.concatenate([rows[:, i : i + lanes] for i in range(0, HEAD_SIZE, lanes)], axis=0)
    each = count * HEAD_SIZE // lanes
    return jnp.concatenate([rows[i : i + each, :] for i in range(0, count, each)], axis=1)


def rows_to_heads(rows):
    count, lanes = rows.shape
    if lanes < HEAD_SIZE:
        each = count * lanes // HEAD_SIZE
        return jnp.concatenate([rows[i : i + each, :] for i in range(0, count, each)], axis=1)
    return jnp.concatenate([rows[:, i : i + HEAD_SIZE] for i in range(0, lanes, HEAD_SIZE)], axis=0)


def gather_kernel(pools, sel_ref, lat_ref, query_ref, keys_ref, *rest):
    value_refs = rest[:pools]
    raw, sems = rest[pools:]
    shard_blocks = lat_ref.shape[2] // BLOCK
    columns = lat_ref.shape[3]
    width = columns // 2
    rows = CAP * BLOCK
    me = lax.axis_index("pool")
    copies = {}
    for k in range(pools - 1, -1, -1):
        seq = me ^ k
        for c, block in enumerate(slot_blocks(sel_ref, seq, me, shard_blocks)):
            local = jnp.maximum(block - me * shard_blocks, 0)
            copies[k, c] = pltpu.make_async_copy(
                lat_ref.at[0, seq, pl.ds(pl.multiple_of(local * BLOCK, BLOCK), BLOCK), :],
                raw.at[pl.ds((k * CAP + c) * BLOCK, BLOCK), :],
                sems.at[k * CAP + c],
            )
            copies[k, c].start()
    chunk = min(4 * LANE, columns)
    half = chunk // 2
    source = lax.broadcasted_iota(jnp.int32, (chunk, chunk), 0)
    target = lax.broadcasted_iota(jnp.int32, (chunk, chunk), 1)
    within = target & (half - 1)
    wanted = ((within >> 6) << 7) + (within & (LANE - 1)) + jnp.where(target >= half, LANE, 0)
    pick = (source == wanted).astype(jnp.float32).astype(jnp.bfloat16)
    queries = heads_to_rows(query_ref[0].astype(jnp.float32), width).astype(jnp.bfloat16)
    for copy in copies.values():
        copy.wait()
    for k in range(pools - 1, -1, -1):
        for j in range(columns // chunk):
            packed = jnp.dot(
                raw[k * rows : (k + 1) * rows, j * chunk : (j + 1) * chunk], pick,
                preferred_element_type=jnp.float32,
            ).astype(jnp.bfloat16)
            keys_ref[k * rows : (k + 1) * rows, j * half : (j + 1) * half] = packed[:, :half]
            value_refs[k][:rows, j * half : (j + 1) * half] = packed[:, half:]
        value_refs[k][rows:, :] = queries


def table_kernel(pools, shard_blocks, sel_ref, len_ref, freq_ref, key_map_ref, value_map_ref, held_ref, *rest):
    cos_ref, sin_ref, turn_ref, live_ref, place_ref, key_out_ref, value_out_ref = rest[:7]
    sems = rest[-1]
    loads = [
        pltpu.make_async_copy(key_map_ref, key_out_ref, sems.at[0]),
        pltpu.make_async_copy(value_map_ref, value_out_ref, sems.at[1]),
    ]
    for load in loads:
        load.start()
    me = lax.axis_index("pool")
    lane = lax.broadcasted_iota(jnp.int32, (BLOCK, HEAD_SIZE), 1)
    row = lax.broadcasted_iota(jnp.int32, (BLOCK, HEAD_SIZE), 0)
    front = lane < HEAD_SIZE // 2
    across = lax.broadcasted_iota(jnp.int32, (1, BLOCK), 1)
    place = jnp.int32(0)
    for k in range(pools):
        turn_ref[k : k + 1, :] = len_ref[0, me ^ k].astype(jnp.float32) * freq_ref[...]
    angle = turn_ref[0:pools, :]
    turn_ref[0:pools, :] = jnp.cos(angle)
    turn_ref[pools:, :] = jnp.where(front[:1, :], -jnp.sin(angle), jnp.sin(angle))
    for k in range(pools):
        seq = me ^ k
        found = slot_blocks(sel_ref, seq, me, shard_blocks)
        one, two = [jnp.maximum(block, 0) * BLOCK for block in found]
        angle = (jnp.where(front, one, two) + row).astype(jnp.float32) * freq_ref[...]
        for ref, table, sign in ((cos_ref, jnp.cos(angle), 1.0), (sin_ref, jnp.sin(angle), -1.0)):
            turned = pltpu.roll(table, HEAD_SIZE // 2, 1)
            at = k * CAP * BLOCK
            ref[at : at + BLOCK, :] = jnp.where(front, sign * table, turned)
            ref[at + BLOCK : at + 2 * BLOCK, :] = jnp.where(front, sign * turned, table)
        mine = slot_blocks(sel_ref, me, seq, shard_blocks)
        for c in range(CAP):
            start = jnp.where(found[c] < 0, FAR, found[c] * BLOCK)
            live_ref[k : k + 1, c * BLOCK : (c + 1) * BLOCK] = (start + across < len_ref[0, seq]).astype(jnp.int32)
            at = (k * CAP + c) * BLOCK
            used = mine[c] >= 0
            place_ref[:, at : at + BLOCK] = jnp.where(used, place, -1) + 0 * across
            place = place + used.astype(jnp.int32)
    for load in loads:
        load.wait()


def stage_kernel(weight_ref, after_ref, out_ref, sem):
    del after_ref
    load = pltpu.make_async_copy(weight_ref, out_ref, sem)
    load.start()
    load.wait()


def rebuild_kernel(pools, heads, map_ref, cos_ref, sin_ref, after_ref, *rest):
    del after_ref
    key_refs = rest[:heads]
    out_ref = rest[heads]
    head = lax.axis_index("heads")
    width = key_refs[0].shape[1]
    rows = CAP * BLOCK
    maps = []
    for j in range(heads):
        owner = head ^ j
        maps.append(map_ref[pl.ds(pl.multiple_of(owner * width, width), width), :])
    for k in range(pools):
        at = slice(k * rows, (k + 1) * rows)
        rebuilt = jnp.dot(key_refs[0][at, :], maps[0], preferred_element_type=jnp.float32)
        for j in range(1, heads):
            rebuilt += jnp.dot(key_refs[j][at, :], maps[j], preferred_element_type=jnp.float32)
        cosine = cos_ref[at, :]
        sine = sin_ref[at, :]
        for g in range(map_ref.shape[1] // HEAD_SIZE):
            lanes = slice(g * HEAD_SIZE, (g + 1) * HEAD_SIZE)
            one = rebuilt[:, lanes]
            out_ref[at, lanes] = (one * cosine + pltpu.roll(one, HEAD_SIZE // 2, 1) * sine).astype(jnp.bfloat16)


def score_kernel(pools, turn_ref, live_ref, place_ref, key_ref, *rest):
    pay_refs = rest[:pools][::-1]
    dense_ref = rest[pools]
    out_refs = rest[pools + 1 :]
    groups = key_ref.shape[1] // HEAD_SIZE
    rows = CAP * BLOCK
    width = dense_ref.shape[1]
    kept = dense_ref.shape[0] // BLOCK
    for k in range(pools - 1, -1, -1):
        live = live_ref[k : k + 1, :] > 0
        query = rows_to_heads(pay_refs[k][rows:, :].astype(jnp.float32))
        query = query * turn_ref[k : k + 1, :] + pltpu.roll(query, HEAD_SIZE // 2, 1) * turn_ref[
            pools + k : pools + k + 1, :
        ]
        query = query.astype(jnp.bfloat16)
        for g in range(groups):
            mine = slice(g * QUERY_PER_GROUP, (g + 1) * QUERY_PER_GROUP)
            scores = lax.dot_general(
                query[mine, :], key_ref[k * rows : (k + 1) * rows, g * HEAD_SIZE : (g + 1) * HEAD_SIZE],
                (((1,), (1,)), ((), ())), preferred_element_type=jnp.float32,
            ) * (HEAD_SIZE ** -0.5)
            out_refs[k][mine, :] = jnp.where(live, scores, MASKED)
    spare = pools * CAP - kept
    for i in range(kept):
        chosen = jnp.zeros((BLOCK, width), jnp.float32)
        for slot in range(i, i + spare + 1):
            place = place_ref[:, slot * BLOCK : slot * BLOCK + LANE]
            place = jnp.concatenate([place] * (width // LANE), axis=1)
            k, c = slot // CAP, slot % CAP
            block = pay_refs[k][c * BLOCK : (c + 1) * BLOCK, :].astype(jnp.float32)
            chosen = jnp.where(place == i, block, chosen)
        dense_ref[i * BLOCK : (i + 1) * BLOCK, :] = chosen.astype(jnp.bfloat16)


def attend_kernel(pools, heads, map_ref, place_ref, *rest):
    score_refs = rest[:pools][::-1]
    value_refs = rest[pools : pools + heads]
    out_ref = rest[-1]
    head = lax.axis_index("heads")
    width = value_refs[0].shape[1]
    groups = map_ref.shape[1] // HEAD_SIZE
    scores = [ref[...] for ref in score_refs]
    top = functools.reduce(jnp.maximum, [jnp.max(s, axis=1, keepdims=True) for s in scores])
    weights = [jnp.exp(s - top) for s in scores]
    total = functools.reduce(jnp.add, [jnp.sum(w, axis=1, keepdims=True) for w in weights])
    slots = []
    for k in range(pools):
        attention = weights[k] / total
        for c in range(CAP):
            at = (k * CAP + c) * BLOCK
            slots.append((place_ref[:, at : at + BLOCK], attention[:, c * BLOCK : (c + 1) * BLOCK]))
    dense = []
    kept = value_refs[0].shape[0] // BLOCK
    for i in range(kept):
        chosen = jnp.zeros_like(slots[0][1])
        for place, attention in slots[i : i + len(slots) - kept + 1]:
            chosen = jnp.where(place == i, attention, chosen)
        dense.append(chosen)
    attention = jnp.concatenate(dense, axis=1).astype(jnp.bfloat16)
    mixed = [None] * groups
    for j in range(heads):
        owner = head ^ j
        context = jnp.dot(
            attention, value_refs[j][...], preferred_element_type=jnp.float32
        ).astype(jnp.bfloat16)
        rows = pl.ds(pl.multiple_of(owner * width, width), width)
        for g in range(groups):
            part = jnp.dot(
                context[g * QUERY_PER_GROUP : (g + 1) * QUERY_PER_GROUP, :],
                map_ref[rows, g * HEAD_SIZE : (g + 1) * HEAD_SIZE],
                preferred_element_type=jnp.float32,
            )
            mixed[g] = part if j == 0 else mixed[g] + part
    for g in range(groups):
        for q in range(QUERY_PER_GROUP):
            at = (g * QUERY_PER_GROUP + q) * HEAD_SIZE
            out_ref[:, at : at + HEAD_SIZE] = mixed[g][q : q + 1, :].astype(jnp.bfloat16)


def join_kernel(*refs):
    rows = [ref[...].reshape(-1, ref.shape[-1]).astype(jnp.float32) for ref in refs[:-1]]
    refs[-1][...] = jnp.concatenate(rows, axis=0).astype(jnp.bfloat16)


def project_kernel(pools, heads, reps, weight_ref, *rest):
    row_refs = rest[:pools]
    out_refs = rest[pools:-1]
    acc = rest[-1]
    left = jnp.concatenate([ref[...].astype(jnp.float32) for ref in row_refs], axis=0).astype(jnp.bfloat16)
    acc[...] = jnp.dot(left, weight_ref[...], preferred_element_type=jnp.float32)
    pool = lax.axis_index("pool")
    head = lax.axis_index("heads")
    each = pools // heads
    for d in range(heads * reps):
        for u in range(each):
            n = (pool ^ ((head ^ (d // reps)) * each + u)) * reps + d % reps
            out_refs[d][u : u + 1, :] = acc[pl.ds(n, 1), :]


def finish_kernel(heads, reps, *refs):
    out_ref = refs[-1]
    refs = refs[:-1][::-1]
    rep = lax.axis_index("rep")
    width = refs[0].shape[1]
    for t in range(reps):
        total = functools.reduce(jnp.add, [refs[j * reps + t][...] for j in range(heads)])
        columns = pl.ds(pl.multiple_of((rep ^ t) * width, width), width)
        out_ref[0, :, columns] = total.astype(jnp.bfloat16)


def per_device(queries, latents, key_latent_maps, value_latent_maps, out_weight, lengths, selected):
    pools = lax.axis_size("pool")
    heads = lax.axis_size("heads")
    reps = lax.axis_size("rep")
    half_seqs, sel_count = selected.shape[1:]
    assert half_seqs == pools and pools % heads == 0
    shard_blocks = latents.shape[2] // BLOCK
    width = latents.shape[3] // 2
    rows = CAP * BLOCK
    own_heads = queries.shape[2] // HEAD_SIZE
    bf16, f32, i32 = jnp.bfloat16, jnp.float32, jnp.int32
    shape = jax.ShapeDtypeStruct
    freq = jnp.asarray(frequencies())

    def join(*blocks):
        return pl.pallas_call(
            join_kernel,
            out_shape=shape((sum(block.size for block in blocks) // queries.shape[2], queries.shape[2]), bf16),
            in_specs=[VMEM] * len(blocks),
            out_specs=VMEM,
            compiler_params=params(4),
            name="join",
        )(*blocks)

    def exchange(value, axis, size):
        taken = {step: swap(value, axis, size, step) for step in range(size - 1, 0, -1)}
        return [value] + [taken[step] for step in range(1, size)]

    def scatter(blocks, axis, size):
        taken = {step: swap(blocks[step], axis, size, step) for step in range(size - 1, 0, -1)}
        return [blocks[0]] + [taken[step] for step in range(1, size)]

    query_rows = queries.shape[2] // width
    packed = pl.pallas_call(
        functools.partial(gather_kernel, pools),
        out_shape=[shape((pools * rows, width), bf16)]
        + [shape((rows + query_rows, width), bf16)] * pools,
        in_specs=[SMEM, HBM, VMEM],
        out_specs=[VMEM] * (pools + 1),
        scratch_shapes=[
            pltpu.VMEM((pools * rows, 2 * width), bf16),
            pltpu.SemaphoreType.DMA((pools * CAP,)),
        ],
        compiler_params=params(16),
        name="gather",
    )(in_hbm(selected), in_hbm(latents), in_hbm(queries))
    keys, values = packed[0], packed[1:]

    cosine, sine, turn, live, place, key_maps, value_maps, held = pl.pallas_call(
        functools.partial(table_kernel, pools, shard_blocks),
        out_shape=[shape((pools * rows, HEAD_SIZE), f32)] * 2
        + [shape((2 * pools, HEAD_SIZE), f32), shape((pools, rows), i32), shape((1, pools * rows), i32)]
        + [shape(key_latent_maps.shape, bf16), shape(value_latent_maps.shape, bf16)]
        + [shape(values[1].shape, bf16)],
        in_specs=[SMEM, SMEM, VMEM] + [ANY] * 3,
        out_specs=[VMEM] * 7 + [ANY],
        scratch_shapes=[pltpu.SemaphoreType.DMA((2,))],
        input_output_aliases={5: 7},
        compiler_params=params(16),
        name="tables",
    )(
        in_hbm(selected), in_hbm(lengths), in_hbm(freq), in_hbm(key_latent_maps),
        in_hbm(value_latent_maps), values[1],
    )
    key_parts = exchange(keys, "heads", heads)
    value_parts = scatter([values[0], held, *values[2:]], "pool", pools)

    weight = pl.pallas_call(
        stage_kernel,
        out_shape=shape(out_weight.shape, bf16),
        in_specs=[HBM, ANY],
        out_specs=VMEM,
        scratch_shapes=[pltpu.SemaphoreType.DMA],
        compiler_params=params(4),
        name="stage",
    )(in_hbm(out_weight), place)
    turned = pl.pallas_call(
        functools.partial(rebuild_kernel, pools, heads),
        out_shape=shape((pools * rows, own_heads // QUERY_PER_GROUP * HEAD_SIZE), bf16),
        in_specs=[VMEM] * 3 + [ANY] + [VMEM] * heads,
        out_specs=VMEM,
        compiler_params=params(20),
        name="rebuild",
    )(key_maps, cosine, sine, weight, *key_parts)
    dense, *scores = pl.pallas_call(
        functools.partial(score_kernel, pools),
        out_shape=[shape((sel_count * BLOCK, width), bf16)] + [shape((own_heads, rows), f32)] * pools,
        in_specs=[VMEM] * (4 + pools),
        out_specs=[VMEM] * (1 + pools),
        compiler_params=params(16),
        name="score",
    )(turn, live, place, turned, *value_parts[::-1])
    dense_parts = exchange(dense, "heads", heads)
    score_parts = scatter(scores, "pool", pools)

    mine = pl.pallas_call(
        functools.partial(attend_kernel, pools, heads),
        out_shape=shape((1, own_heads * HEAD_SIZE), bf16),
        in_specs=[VMEM] * (2 + pools + heads),
        out_specs=VMEM,
        compiler_params=params(16),
        name="attend",
    )(value_maps, place, *score_parts[::-1], *dense_parts)
    own_rows = join(*exchange(mine, "rep", reps))
    row_parts = exchange(own_rows, "pool", pools)

    own_columns = out_weight.shape[1]
    each = pools // heads
    parts = pl.pallas_call(
        functools.partial(project_kernel, pools, heads, reps),
        out_shape=[shape((each, own_columns), f32)] * (heads * reps),
        in_specs=[VMEM] * (pools + 1),
        out_specs=[VMEM] * (heads * reps),
        scratch_shapes=[pltpu.VMEM((pools * reps, own_columns), f32)],
        compiler_params=params(24),
        name="project",
    )(weight, *row_parts)
    return pl.pallas_call(
        functools.partial(finish_kernel, heads, reps),
        out_shape=shape((1, each, reps * own_columns), bf16),
        in_specs=[VMEM] * (heads * reps),
        out_specs=VMEM,
        compiler_params=params(4),
        name="finish",
    )(*scatter(parts, ("heads", "rep"), heads * reps)[::-1])


def solution(mesh):
    return jax.shard_map(
        per_device,
        mesh=mesh,
        in_specs=(
            P(("groups", "rep"), "pool", "heads"),
            P(("groups", "rep"), None, "pool", "heads"),
            P(None, "heads"),
            P(None, "heads"),
            P("heads", ("pool", "rep")),
            P(("groups", "rep"), None),
            P(("groups", "rep"), None, None),
        ),
        out_specs=P(("groups", "rep"), "heads", "pool"),
        check_vma=False,
    )
```

```python
import functools

import jax
import jax.numpy as jnp
import numpy as np
from jax import lax
from jax.experimental import pallas as pl
from jax.experimental.pallas import tpu as pltpu
from jax.sharding import PartitionSpec as P

HEAD_SIZE = 128
LANE = 64
BLOCK = 128
CAP = 2
QUERY_PER_GROUP = 8

ROPE_BASE = 500000.0
MASKED = -1e30
FAR = 1 << 29

SMEM = pl.BlockSpec(memory_space=pltpu.SMEM)
VMEM = pl.BlockSpec(memory_space=pltpu.VMEM)
ANY = pl.BlockSpec(memory_space=pl.ANY)
HBM = pl.BlockSpec(memory_space=pltpu.HBM)


def frequencies():
    half = HEAD_SIZE // 2
    exponents = np.arange(half, dtype=np.float32) * np.float32(2.0 / HEAD_SIZE)
    freq = np.power(np.float64(ROPE_BASE), -exponents.astype(np.float64)).astype(np.float32)
    return np.concatenate([freq, freq])[None, :]


def swap(value, axes, size, step):
    return lax.ppermute(value, axes, [(i, i ^ step) for i in range(size)])


def in_hbm(value):
    return pltpu.with_memory_space_constraint(value, pltpu.HBM)


def in_vmem(value):
    return pltpu.with_memory_space_constraint(value, pltpu.VMEM)


def served(size):
    middle = size // 2
    return [middle] + [k for k in range(size - 1, -1, -1) if k != middle]


def params(mib, **more):
    return pltpu.CompilerParams(vmem_limit_bytes=mib << 20, **more)


def slot_blocks(sel_ref, seq, shard, shard_blocks):
    first = jnp.int32(-1)
    second = jnp.int32(-1)
    for i in range(sel_ref.shape[2]):
        block = sel_ref[0, seq, i]
        here = (block >= shard * shard_blocks) & (block < (shard + 1) * shard_blocks)
        second = jnp.where(here & (first >= 0), block, second)
        first = jnp.where(here & (first < 0), block, first)
    return first, second


def heads_to_rows(line, lanes):
    count = line.shape[1] // HEAD_SIZE
    rows = jnp.concatenate([line[:, n * HEAD_SIZE : (n + 1) * HEAD_SIZE] for n in range(count)], axis=0)
    if lanes < HEAD_SIZE:
        return jnp.concatenate([rows[:, i : i + lanes] for i in range(0, HEAD_SIZE, lanes)], axis=0)
    each = count * HEAD_SIZE // lanes
    return jnp.concatenate([rows[i : i + each, :] for i in range(0, count, each)], axis=1)


def rows_to_heads(rows):
    count, lanes = rows.shape
    if lanes < HEAD_SIZE:
        each = count * lanes // HEAD_SIZE
        return jnp.concatenate([rows[i : i + each, :] for i in range(0, count, each)], axis=1)
    return jnp.concatenate([rows[:, i : i + HEAD_SIZE] for i in range(0, lanes, HEAD_SIZE)], axis=0)


def gather_kernel(pools, sel_ref, lat_ref, query_ref, keys_ref, *rest):
    value_refs = rest[:pools]
    raw, sems = rest[pools:]
    shard_blocks = lat_ref.shape[2] // BLOCK
    columns = lat_ref.shape[3]
    width = columns // 2
    rows = CAP * BLOCK
    me = lax.axis_index("pool")
    copies = {}
    for k in range(pools - 1, -1, -1):
        seq = me ^ k
        for c, block in enumerate(slot_blocks(sel_ref, seq, me, shard_blocks)):
            local = jnp.maximum(block - me * shard_blocks, 0)
            copies[k, c] = pltpu.make_async_copy(
                lat_ref.at[0, seq, pl.ds(pl.multiple_of(local * BLOCK, BLOCK), BLOCK), :],
                raw.at[pl.ds((k * CAP + c) * BLOCK, BLOCK), :],
                sems.at[k * CAP + c],
            )
            copies[k, c].start()
    chunk = min(4 * LANE, columns)
    half = chunk // 2
    source = lax.broadcasted_iota(jnp.int32, (chunk, chunk), 0)
    target = lax.broadcasted_iota(jnp.int32, (chunk, chunk), 1)
    within = target & (half - 1)
    wanted = ((within >> 6) << 7) + (within & (LANE - 1)) + jnp.where(target >= half, LANE, 0)
    pick = (source == wanted).astype(jnp.float32).astype(jnp.bfloat16)
    queries = heads_to_rows(query_ref[0].astype(jnp.float32), width).astype(jnp.bfloat16)
    for copy in copies.values():
        copy.wait()
    for k in range(pools - 1, -1, -1):
        for j in range(columns // chunk):
            packed = jnp.dot(
                raw[k * rows : (k + 1) * rows, j * chunk : (j + 1) * chunk], pick,
                preferred_element_type=jnp.float32,
            ).astype(jnp.bfloat16)
            keys_ref[k * rows : (k + 1) * rows, j * half : (j + 1) * half] = packed[:, :half]
            value_refs[k][:rows, j * half : (j + 1) * half] = packed[:, half:]
        value_refs[k][rows:, :] = queries


def table_kernel(pools, shard_blocks, sel_ref, len_ref, freq_ref, key_map_ref, value_map_ref, held_ref, *rest):
    cos_ref, sin_ref, turn_ref, live_ref, place_ref, key_out_ref, value_out_ref = rest[:7]
    sems = rest[-1]
    loads = [
        pltpu.make_async_copy(key_map_ref, key_out_ref, sems.at[0]),
        pltpu.make_async_copy(value_map_ref, value_out_ref, sems.at[1]),
    ]
    for load in loads:
        load.start()
    me = lax.axis_index("pool")
    lane = lax.broadcasted_iota(jnp.int32, (BLOCK, HEAD_SIZE), 1)
    row = lax.broadcasted_iota(jnp.int32, (BLOCK, HEAD_SIZE), 0)
    front = lane < HEAD_SIZE // 2
    across = lax.broadcasted_iota(jnp.int32, (1, BLOCK), 1)
    place = jnp.int32(0)
    for k in range(pools):
        turn_ref[k : k + 1, :] = len_ref[0, me ^ k].astype(jnp.float32) * freq_ref[...]
    angle = turn_ref[0:pools, :]
    turn_ref[0:pools, :] = jnp.cos(angle)
    turn_ref[pools:, :] = jnp.where(front[:1, :], -jnp.sin(angle), jnp.sin(angle))
    for k in range(pools):
        seq = me ^ k
        found = slot_blocks(sel_ref, seq, me, shard_blocks)
        one, two = [jnp.maximum(block, 0) * BLOCK for block in found]
        angle = (jnp.where(front, one, two) + row).astype(jnp.float32) * freq_ref[...]
        for ref, table, sign in ((cos_ref, jnp.cos(angle), 1.0), (sin_ref, jnp.sin(angle), -1.0)):
            turned = pltpu.roll(table, HEAD_SIZE // 2, 1)
            at = k * CAP * BLOCK
            ref[at : at + BLOCK, :] = jnp.where(front, sign * table, turned)
            ref[at + BLOCK : at + 2 * BLOCK, :] = jnp.where(front, sign * turned, table)
        mine = slot_blocks(sel_ref, me, seq, shard_blocks)
        for c in range(CAP):
            start = jnp.where(found[c] < 0, FAR, found[c] * BLOCK)
            live_ref[k : k + 1, c * BLOCK : (c + 1) * BLOCK] = (start + across < len_ref[0, seq]).astype(jnp.int32)
            at = (k * CAP + c) * BLOCK
            used = mine[c] >= 0
            place_ref[:, at : at + BLOCK] = jnp.where(used, place, -1) + 0 * across
            place = place + used.astype(jnp.int32)
    for load in loads:
        load.wait()


def stage_kernel(weight_ref, after_ref, out_ref, sem):
    del after_ref
    load = pltpu.make_async_copy(weight_ref, out_ref, sem)
    load.start()
    load.wait()


def rebuild_kernel(pools, heads, map_ref, cos_ref, sin_ref, after_ref, *rest):
    del after_ref
    key_refs = rest[:heads]
    out_ref = rest[heads]
    head = lax.axis_index("heads")
    width = key_refs[0].shape[1]
    rows = CAP * BLOCK
    maps = []
    for j in range(heads):
        owner = head ^ j
        maps.append(map_ref[pl.ds(pl.multiple_of(owner * width, width), width), :])
    for k in range(pools):
        at = slice(k * rows, (k + 1) * rows)
        rebuilt = jnp.dot(key_refs[0][at, :], maps[0], preferred_element_type=jnp.float32)
        for j in range(1, heads):
            rebuilt += jnp.dot(key_refs[j][at, :], maps[j], preferred_element_type=jnp.float32)
        cosine = cos_ref[at, :]
        sine = sin_ref[at, :]
        for g in range(map_ref.shape[1] // HEAD_SIZE):
            lanes = slice(g * HEAD_SIZE, (g + 1) * HEAD_SIZE)
            one = rebuilt[:, lanes]
            out_ref[at, lanes] = (one * cosine + pltpu.roll(one, HEAD_SIZE // 2, 1) * sine).astype(jnp.bfloat16)


def score_kernel(pools, turn_ref, live_ref, place_ref, key_ref, *rest):
    pay_refs = rest[:pools][::-1]
    dense_ref = rest[pools]
    out_refs = rest[pools + 1 :]
    groups = key_ref.shape[1] // HEAD_SIZE
    rows = CAP * BLOCK
    width = dense_ref.shape[1]
    kept = dense_ref.shape[0] // BLOCK
    for k in range(pools - 1, -1, -1):
        live = live_ref[k : k + 1, :] > 0
        query = rows_to_heads(pay_refs[k][rows:, :].astype(jnp.float32))
        query = query * turn_ref[k : k + 1, :] + pltpu.roll(query, HEAD_SIZE // 2, 1) * turn_ref[
            pools + k : pools + k + 1, :
        ]
        query = query.astype(jnp.bfloat16)
        for g in range(groups):
            mine = slice(g * QUERY_PER_GROUP, (g + 1) * QUERY_PER_GROUP)
            scores = lax.dot_general(
                query[mine, :], key_ref[k * rows : (k + 1) * rows, g * HEAD_SIZE : (g + 1) * HEAD_SIZE],
                (((1,), (1,)), ((), ())), preferred_element_type=jnp.float32,
            ) * (HEAD_SIZE ** -0.5)
            out_refs[k][mine, :] = jnp.where(live, scores, MASKED)
    spare = pools * CAP - kept
    for i in range(kept):
        chosen = jnp.zeros((BLOCK, width), jnp.float32)
        for slot in range(i, i + spare + 1):
            place = place_ref[:, slot * BLOCK : slot * BLOCK + LANE]
            place = jnp.concatenate([place] * (width // LANE), axis=1)
            k, c = slot // CAP, slot % CAP
            block = pay_refs[k][c * BLOCK : (c + 1) * BLOCK, :].astype(jnp.float32)
            chosen = jnp.where(place == i, block, chosen)
        dense_ref[i * BLOCK : (i + 1) * BLOCK, :] = chosen.astype(jnp.bfloat16)


def attend_kernel(pools, heads, map_ref, place_ref, *rest):
    score_refs = [rest[served(pools).index(k)] for k in range(pools)]
    value_refs = rest[pools : pools + heads]
    out_ref = rest[-1]
    head = lax.axis_index("heads")
    width = value_refs[0].shape[1]
    groups = map_ref.shape[1] // HEAD_SIZE
    scores = [ref[...] for ref in score_refs]
    top = functools.reduce(jnp.maximum, [jnp.max(s, axis=1, keepdims=True) for s in scores])
    weights = [jnp.exp(s - top) for s in scores]
    total = functools.reduce(jnp.add, [jnp.sum(w, axis=1, keepdims=True) for w in weights])
    slots = []
    for k in range(pools):
        attention = weights[k] / total
        for c in range(CAP):
            at = (k * CAP + c) * BLOCK
            slots.append((place_ref[:, at : at + BLOCK], attention[:, c * BLOCK : (c + 1) * BLOCK]))
    dense = []
    kept = value_refs[0].shape[0] // BLOCK
    for i in range(kept):
        chosen = jnp.zeros_like(slots[0][1])
        for place, attention in slots[i : i + len(slots) - kept + 1]:
            chosen = jnp.where(place == i, attention, chosen)
        dense.append(chosen)
    attention = jnp.concatenate(dense, axis=1).astype(jnp.bfloat16)
    mixed = [None] * groups
    for j in range(heads):
        owner = head ^ j
        context = jnp.dot(
            attention, value_refs[j][...], preferred_element_type=jnp.float32
        ).astype(jnp.bfloat16)
        rows = pl.ds(pl.multiple_of(owner * width, width), width)
        for g in range(groups):
            part = jnp.dot(
                context[g * QUERY_PER_GROUP : (g + 1) * QUERY_PER_GROUP, :],
                map_ref[rows, g * HEAD_SIZE : (g + 1) * HEAD_SIZE],
                preferred_element_type=jnp.float32,
            )
            mixed[g] = part if j == 0 else mixed[g] + part
    for g in range(groups):
        for q in range(QUERY_PER_GROUP):
            at = (g * QUERY_PER_GROUP + q) * HEAD_SIZE
            out_ref[:, at : at + HEAD_SIZE] = mixed[g][q : q + 1, :].astype(jnp.bfloat16)


def join_kernel(*refs):
    rows = [ref[...].reshape(-1, ref.shape[-1]).astype(jnp.float32) for ref in refs[:-1]]
    refs[-1][...] = jnp.concatenate(rows, axis=0).astype(jnp.bfloat16)


def project_kernel(pools, heads, reps, weight_ref, *rest):
    row_refs = [rest[served(pools)[::-1].index(k)] for k in range(pools)]
    out_refs = rest[pools:-1]
    acc = rest[-1]
    left = jnp.concatenate([ref[...].astype(jnp.float32) for ref in row_refs], axis=0).astype(jnp.bfloat16)
    acc[...] = jnp.dot(left, weight_ref[...], preferred_element_type=jnp.float32)
    pool = lax.axis_index("pool")
    head = lax.axis_index("heads")
    each = pools // heads
    for d in range(heads * reps):
        for u in range(each):
            n = (pool ^ ((head ^ (d // reps)) * each + u)) * reps + d % reps
            out_refs[d][u : u + 1, :] = acc[pl.ds(n, 1), :]


def finish_kernel(heads, reps, *refs):
    out_ref = refs[-1]
    refs = refs[:-1][::-1]
    rep = lax.axis_index("rep")
    width = refs[0].shape[1]
    for t in range(reps):
        total = functools.reduce(jnp.add, [refs[j * reps + t][...] for j in range(heads)])
        columns = pl.ds(pl.multiple_of((rep ^ t) * width, width), width)
        out_ref[0, :, columns] = total.astype(jnp.bfloat16)


def per_device(queries, latents, key_latent_maps, value_latent_maps, out_weight, lengths, selected):
    pools = lax.axis_size("pool")
    heads = lax.axis_size("heads")
    reps = lax.axis_size("rep")
    half_seqs, sel_count = selected.shape[1:]
    assert half_seqs == pools and pools % heads == 0
    shard_blocks = latents.shape[2] // BLOCK
    width = latents.shape[3] // 2
    rows = CAP * BLOCK
    own_heads = queries.shape[2] // HEAD_SIZE
    bf16, f32, i32 = jnp.bfloat16, jnp.float32, jnp.int32
    shape = jax.ShapeDtypeStruct
    freq = jnp.asarray(frequencies())

    def join(*blocks):
        return pl.pallas_call(
            join_kernel,
            out_shape=shape((sum(block.size for block in blocks) // queries.shape[2], queries.shape[2]), bf16),
            in_specs=[VMEM] * len(blocks),
            out_specs=VMEM,
            compiler_params=params(4),
            name="join",
        )(*blocks)

    def exchange(value, axis, size):
        taken = {step: swap(value, axis, size, step) for step in range(size - 1, 0, -1)}
        return [value] + [taken[step] for step in range(1, size)]

    def scatter(blocks, axis, size):
        taken = {step: swap(blocks[step], axis, size, step) for step in range(size - 1, 0, -1)}
        return [blocks[0]] + [taken[step] for step in range(1, size)]

    query_rows = queries.shape[2] // width
    packed = pl.pallas_call(
        functools.partial(gather_kernel, pools),
        out_shape=[shape((pools * rows, width), bf16)]
        + [shape((rows + query_rows, width), bf16)] * pools,
        in_specs=[SMEM, HBM, VMEM],
        out_specs=[VMEM] * (pools + 1),
        scratch_shapes=[
            pltpu.VMEM((pools * rows, 2 * width), bf16),
            pltpu.SemaphoreType.DMA((pools * CAP,)),
        ],
        compiler_params=params(16),
        name="gather",
    )(in_hbm(selected), in_hbm(latents), in_hbm(queries))
    keys, values = packed[0], packed[1:]

    cosine, sine, turn, live, place, key_maps, value_maps, held = pl.pallas_call(
        functools.partial(table_kernel, pools, shard_blocks),
        out_shape=[shape((pools * rows, HEAD_SIZE), f32)] * 2
        + [shape((2 * pools, HEAD_SIZE), f32), shape((pools, rows), i32), shape((1, pools * rows), i32)]
        + [shape(key_latent_maps.shape, bf16), shape(value_latent_maps.shape, bf16)]
        + [shape(values[1].shape, bf16)],
        in_specs=[SMEM, SMEM, VMEM] + [ANY] * 3,
        out_specs=[VMEM] * 7 + [ANY],
        scratch_shapes=[pltpu.SemaphoreType.DMA((2,))],
        input_output_aliases={5: 7},
        compiler_params=params(16),
        name="tables",
    )(
        in_hbm(selected), in_hbm(lengths), in_hbm(freq), in_hbm(key_latent_maps),
        in_hbm(value_latent_maps), values[1],
    )
    key_parts = exchange(keys, "heads", heads)
    value_parts = scatter([values[0], held, *values[2:]], "pool", pools)

    weight = pl.pallas_call(
        stage_kernel,
        out_shape=shape(out_weight.shape, bf16),
        in_specs=[HBM, ANY],
        out_specs=VMEM,
        scratch_shapes=[pltpu.SemaphoreType.DMA],
        compiler_params=params(4),
        name="stage",
    )(in_hbm(out_weight), place)
    turned = pl.pallas_call(
        functools.partial(rebuild_kernel, pools, heads),
        out_shape=shape((pools * rows, own_heads // QUERY_PER_GROUP * HEAD_SIZE), bf16),
        in_specs=[VMEM] * 3 + [ANY] + [VMEM] * heads,
        out_specs=VMEM,
        compiler_params=params(20),
        name="rebuild",
    )(key_maps, cosine, sine, weight, *key_parts)
    dense, *scores = pl.pallas_call(
        functools.partial(score_kernel, pools),
        out_shape=[shape((sel_count * BLOCK, width), bf16)] + [shape((own_heads, rows), f32)] * pools,
        in_specs=[VMEM] * (4 + pools),
        out_specs=[VMEM] * (1 + pools),
        compiler_params=params(16),
        name="score",
    )(turn, live, place, turned, *value_parts[::-1])
    dense_parts = exchange(dense, "heads", heads)
    score_parts = scatter(scores, "pool", pools)

    mine = pl.pallas_call(
        functools.partial(attend_kernel, pools, heads),
        out_shape=shape((1, own_heads * HEAD_SIZE), bf16),
        in_specs=[VMEM] * (2 + pools + heads),
        out_specs=VMEM,
        compiler_params=params(16),
        name="attend",
    )(value_maps, place, *[score_parts[k] for k in served(pools)], *dense_parts)
    own_rows = join(*exchange(mine, "rep", reps))
    row_parts = exchange(own_rows, "pool", pools)

    own_columns = out_weight.shape[1]
    each = pools // heads
    parts = pl.pallas_call(
        functools.partial(project_kernel, pools, heads, reps),
        out_shape=[shape((each, own_columns), f32)] * (heads * reps),
        in_specs=[VMEM] * (pools + 1),
        out_specs=[VMEM] * (heads * reps),
        scratch_shapes=[pltpu.VMEM((pools * reps, own_columns), f32)],
        compiler_params=params(24),
        name="project",
    )(weight, *[row_parts[k] for k in served(pools)[::-1]])
    return pl.pallas_call(
        functools.partial(finish_kernel, heads, reps),
        out_shape=shape((1, each, reps * own_columns), bf16),
        in_specs=[VMEM] * (heads * reps),
        out_specs=VMEM,
        compiler_params=params(4),
        name="finish",
    )(*scatter(parts, ("heads", "rep"), heads * reps)[::-1])


def solution(mesh):
    return jax.shard_map(
        per_device,
        mesh=mesh,
        in_specs=(
            P(("groups", "rep"), "pool", "heads"),
            P(("groups", "rep"), None, "pool", "heads"),
            P(None, "heads"),
            P(None, "heads"),
            P("heads", ("pool", "rep")),
            P(("groups", "rep"), None),
            P(("groups", "rep"), None, None),
        ),
        out_specs=P(("groups", "rep"), "heads", "pool"),
        check_vma=False,
    )
```

```python
import functools

import jax
import jax.numpy as jnp
import numpy as np
from jax import lax
from jax.experimental import pallas as pl
from jax.experimental.pallas import tpu as pltpu
from jax.sharding import PartitionSpec as P

HEAD_SIZE = 128
LANE = 64
BLOCK = 128
CAP = 2
QUERY_PER_GROUP = 8

ROPE_BASE = 500000.0
MASKED = -1e30
FAR = 1 << 29

SMEM = pl.BlockSpec(memory_space=pltpu.SMEM)
VMEM = pl.BlockSpec(memory_space=pltpu.VMEM)
ANY = pl.BlockSpec(memory_space=pl.ANY)
HBM = pl.BlockSpec(memory_space=pltpu.HBM)


def frequencies():
    half = HEAD_SIZE // 2
    exponents = np.arange(half, dtype=np.float32) * np.float32(2.0 / HEAD_SIZE)
    freq = np.power(np.float64(ROPE_BASE), -exponents.astype(np.float64)).astype(np.float32)
    return np.concatenate([freq, freq])[None, :]


def swap(value, axes, size, step):
    return lax.ppermute(value, axes, [(i, i ^ step) for i in range(size)])


def in_hbm(value):
    return pltpu.with_memory_space_constraint(value, pltpu.HBM)


def in_vmem(value):
    return pltpu.with_memory_space_constraint(value, pltpu.VMEM)


def params(mib, **more):
    return pltpu.CompilerParams(vmem_limit_bytes=mib << 20, **more)


def slot_blocks(sel_ref, seq, shard, shard_blocks):
    first = jnp.int32(-1)
    second = jnp.int32(-1)
    for i in range(sel_ref.shape[2]):
        block = sel_ref[0, seq, i]
        here = (block >= shard * shard_blocks) & (block < (shard + 1) * shard_blocks)
        second = jnp.where(here & (first >= 0), block, second)
        first = jnp.where(here & (first < 0), block, first)
    return first, second


def heads_to_rows(line, lanes):
    count = line.shape[1] // HEAD_SIZE
    rows = jnp.concatenate([line[:, n * HEAD_SIZE : (n + 1) * HEAD_SIZE] for n in range(count)], axis=0)
    if lanes < HEAD_SIZE:
        return jnp.concatenate([rows[:, i : i + lanes] for i in range(0, HEAD_SIZE, lanes)], axis=0)
    each = count * HEAD_SIZE // lanes
    return jnp.concatenate([rows[i : i + each, :] for i in range(0, count, each)], axis=1)


def rows_to_heads(rows):
    count, lanes = rows.shape
    if lanes < HEAD_SIZE:
        each = count * lanes // HEAD_SIZE
        return jnp.concatenate([rows[i : i + each, :] for i in range(0, count, each)], axis=1)
    return jnp.concatenate([rows[:, i : i + HEAD_SIZE] for i in range(0, lanes, HEAD_SIZE)], axis=0)


def gather_kernel(pools, sel_ref, lat_ref, query_ref, keys_ref, *rest):
    value_refs = rest[:pools]
    raw, sems = rest[pools:]
    shard_blocks = lat_ref.shape[2] // BLOCK
    columns = lat_ref.shape[3]
    width = columns // 2
    rows = CAP * BLOCK
    me = lax.axis_index("pool")
    copies = {}
    for k in range(pools - 1, -1, -1):
        seq = me ^ k
        for c, block in enumerate(slot_blocks(sel_ref, seq, me, shard_blocks)):
            local = jnp.maximum(block - me * shard_blocks, 0)
            copies[k, c] = pltpu.make_async_copy(
                lat_ref.at[0, seq, pl.ds(pl.multiple_of(local * BLOCK, BLOCK), BLOCK), :],
                raw.at[pl.ds((k * CAP + c) * BLOCK, BLOCK), :],
                sems.at[k * CAP + c],
            )
            copies[k, c].start()
    chunk = min(4 * LANE, columns)
    half = chunk // 2
    source = lax.broadcasted_iota(jnp.int32, (chunk, chunk), 0)
    target = lax.broadcasted_iota(jnp.int32, (chunk, chunk), 1)
    within = target & (half - 1)
    wanted = ((within >> 6) << 7) + (within & (LANE - 1)) + jnp.where(target >= half, LANE, 0)
    pick = (source == wanted).astype(jnp.float32).astype(jnp.bfloat16)
    queries = heads_to_rows(query_ref[0].astype(jnp.float32), width).astype(jnp.bfloat16)
    for copy in copies.values():
        copy.wait()
    for j in range(columns // chunk):
        packed = jnp.dot(
            raw[:, j * chunk : (j + 1) * chunk], pick, preferred_element_type=jnp.float32
        ).astype(jnp.bfloat16)
        keys_ref[:, j * half : (j + 1) * half] = packed[:, :half]
        for k in range(pools):
            value_refs[k][:rows, j * half : (j + 1) * half] = packed[k * rows : (k + 1) * rows, half:]
    for k in range(pools):
        value_refs[k][rows:, :] = queries


def table_kernel(pools, shard_blocks, sel_ref, len_ref, freq_ref, key_map_ref, value_map_ref, held_ref, *rest):
    cos_ref, sin_ref, turn_ref, live_ref, place_ref, key_out_ref, value_out_ref = rest[:7]
    sems = rest[-1]
    loads = [
        pltpu.make_async_copy(key_map_ref, key_out_ref, sems.at[0]),
        pltpu.make_async_copy(value_map_ref, value_out_ref, sems.at[1]),
    ]
    for load in loads:
        load.start()
    me = lax.axis_index("pool")
    lane = lax.broadcasted_iota(jnp.int32, (BLOCK, HEAD_SIZE), 1)
    row = lax.broadcasted_iota(jnp.int32, (BLOCK, HEAD_SIZE), 0)
    front = lane < HEAD_SIZE // 2
    across = lax.broadcasted_iota(jnp.int32, (1, BLOCK), 1)
    place = jnp.int32(0)
    for k in range(pools):
        turn_ref[k : k + 1, :] = len_ref[0, me ^ k].astype(jnp.float32) * freq_ref[...]
    angle = turn_ref[0:pools, :]
    turn_ref[0:pools, :] = jnp.cos(angle)
    turn_ref[pools:, :] = jnp.where(front[:1, :], -jnp.sin(angle), jnp.sin(angle))
    for k in range(pools):
        seq = me ^ k
        found = slot_blocks(sel_ref, seq, me, shard_blocks)
        one, two = [jnp.maximum(block, 0) * BLOCK for block in found]
        angle = (jnp.where(front, one, two) + row).astype(jnp.float32) * freq_ref[...]
        for ref, table, sign in ((cos_ref, jnp.cos(angle), 1.0), (sin_ref, jnp.sin(angle), -1.0)):
            turned = pltpu.roll(table, HEAD_SIZE // 2, 1)
            at = k * CAP * BLOCK
            ref[at : at + BLOCK, :] = jnp.where(front, sign * table, turned)
            ref[at + BLOCK : at + 2 * BLOCK, :] = jnp.where(front, sign * turned, table)
        mine = slot_blocks(sel_ref, me, seq, shard_blocks)
        for c in range(CAP):
            start = jnp.where(found[c] < 0, FAR, found[c] * BLOCK)
            live_ref[k : k + 1, c * BLOCK : (c + 1) * BLOCK] = (start + across < len_ref[0, seq]).astype(jnp.int32)
            at = (k * CAP + c) * BLOCK
            used = mine[c] >= 0
            place_ref[:, at : at + BLOCK] = jnp.where(used, place, -1) + 0 * across
            place = place + used.astype(jnp.int32)
    for load in loads:
        load.wait()


def stage_kernel(weight_ref, after_ref, out_ref, sem):
    del after_ref
    load = pltpu.make_async_copy(weight_ref, out_ref, sem)
    load.start()
    load.wait()


def rebuild_kernel(pools, heads, map_ref, cos_ref, sin_ref, after_ref, *rest):
    del after_ref
    key_refs = rest[:heads]
    out_ref = rest[heads]
    head = lax.axis_index("heads")
    width = key_refs[0].shape[1]
    rows = CAP * BLOCK
    maps = []
    for j in range(heads):
        owner = head ^ j
        maps.append(map_ref[pl.ds(pl.multiple_of(owner * width, width), width), :])
    for k in range(pools):
        at = slice(k * rows, (k + 1) * rows)
        rebuilt = jnp.dot(key_refs[0][at, :], maps[0], preferred_element_type=jnp.float32)
        for j in range(1, heads):
            rebuilt += jnp.dot(key_refs[j][at, :], maps[j], preferred_element_type=jnp.float32)
        cosine = cos_ref[at, :]
        sine = sin_ref[at, :]
        for g in range(map_ref.shape[1] // HEAD_SIZE):
            lanes = slice(g * HEAD_SIZE, (g + 1) * HEAD_SIZE)
            one = rebuilt[:, lanes]
            out_ref[at, lanes] = (one * cosine + pltpu.roll(one, HEAD_SIZE // 2, 1) * sine).astype(jnp.bfloat16)


def score_kernel(pools, turn_ref, live_ref, place_ref, key_ref, *rest):
    pay_refs = rest[:pools][::-1]
    dense_ref = rest[pools]
    out_refs = rest[pools + 1 :]
    groups = key_ref.shape[1] // HEAD_SIZE
    rows = CAP * BLOCK
    width = dense_ref.shape[1]
    kept = dense_ref.shape[0] // BLOCK
    for k in range(pools - 1, -1, -1):
        live = live_ref[k : k + 1, :] > 0
        query = rows_to_heads(pay_refs[k][rows:, :].astype(jnp.float32))
        query = query * turn_ref[k : k + 1, :] + pltpu.roll(query, HEAD_SIZE // 2, 1) * turn_ref[
            pools + k : pools + k + 1, :
        ]
        query = query.astype(jnp.bfloat16)
        for g in range(groups):
            mine = slice(g * QUERY_PER_GROUP, (g + 1) * QUERY_PER_GROUP)
            scores = lax.dot_general(
                query[mine, :], key_ref[k * rows : (k + 1) * rows, g * HEAD_SIZE : (g + 1) * HEAD_SIZE],
                (((1,), (1,)), ((), ())), preferred_element_type=jnp.float32,
            ) * (HEAD_SIZE ** -0.5)
            out_refs[k][mine, :] = jnp.where(live, scores, MASKED)
    spare = pools * CAP - kept
    for i in range(kept):
        chosen = jnp.zeros((BLOCK, width), jnp.float32)
        for slot in range(i, i + spare + 1):
            place = place_ref[:, slot * BLOCK : slot * BLOCK + LANE]
            place = jnp.concatenate([place] * (width // LANE), axis=1)
            k, c = slot // CAP, slot % CAP
            block = pay_refs[k][c * BLOCK : (c + 1) * BLOCK, :].astype(jnp.float32)
            chosen = jnp.where(place == i, block, chosen)
        dense_ref[i * BLOCK : (i + 1) * BLOCK, :] = chosen.astype(jnp.bfloat16)


def attend_kernel(pools, heads, map_ref, place_ref, *rest):
    score_refs = rest[:pools][::-1]
    value_refs = rest[pools : pools + heads]
    out_ref = rest[-1]
    head = lax.axis_index("heads")
    width = value_refs[0].shape[1]
    groups = map_ref.shape[1] // HEAD_SIZE
    scores = [ref[...] for ref in score_refs]
    top = functools.reduce(jnp.maximum, [jnp.max(s, axis=1, keepdims=True) for s in scores])
    weights = [jnp.exp(s - top) for s in scores]
    total = functools.reduce(jnp.add, [jnp.sum(w, axis=1, keepdims=True) for w in weights])
    slots = []
    for k in range(pools):
        attention = weights[k] / total
        for c in range(CAP):
            at = (k * CAP + c) * BLOCK
            slots.append((place_ref[:, at : at + BLOCK], attention[:, c * BLOCK : (c + 1) * BLOCK]))
    dense = []
    kept = value_refs[0].shape[0] // BLOCK
    for i in range(kept):
        chosen = jnp.zeros_like(slots[0][1])
        for place, attention in slots[i : i + len(slots) - kept + 1]:
            chosen = jnp.where(place == i, attention, chosen)
        dense.append(chosen)
    attention = jnp.concatenate(dense, axis=1).astype(jnp.bfloat16)
    mixed = [None] * groups
    for j in range(heads):
        owner = head ^ j
        context = jnp.dot(
            attention, value_refs[j][...], preferred_element_type=jnp.float32
        ).astype(jnp.bfloat16)
        rows = pl.ds(pl.multiple_of(owner * width, width), width)
        for g in range(groups):
            part = jnp.dot(
                context[g * QUERY_PER_GROUP : (g + 1) * QUERY_PER_GROUP, :],
                map_ref[rows, g * HEAD_SIZE : (g + 1) * HEAD_SIZE],
                preferred_element_type=jnp.float32,
            )
            mixed[g] = part if j == 0 else mixed[g] + part
    for g in range(groups):
        for q in range(QUERY_PER_GROUP):
            at = (g * QUERY_PER_GROUP + q) * HEAD_SIZE
            out_ref[:, at : at + HEAD_SIZE] = mixed[g][q : q + 1, :].astype(jnp.bfloat16)


def join_kernel(*refs):
    rows = [ref[...].reshape(-1, ref.shape[-1]).astype(jnp.float32) for ref in refs[:-1]]
    refs[-1][...] = jnp.concatenate(rows, axis=0).astype(jnp.bfloat16)


def project_kernel(pools, heads, reps, weight_ref, *rest):
    row_refs = rest[:pools]
    out_refs = rest[pools:-1]
    acc = rest[-1]
    left = jnp.concatenate([ref[...].astype(jnp.float32) for ref in row_refs], axis=0).astype(jnp.bfloat16)
    acc[...] = jnp.dot(left, weight_ref[...], preferred_element_type=jnp.float32)
    pool = lax.axis_index("pool")
    head = lax.axis_index("heads")
    each = pools // heads
    for d in range(heads * reps):
        for u in range(each):
            n = (pool ^ ((head ^ (d // reps)) * each + u)) * reps + d % reps
            out_refs[d][u : u + 1, :] = acc[pl.ds(n, 1), :]


def finish_kernel(heads, reps, *refs):
    out_ref = refs[-1]
    refs = refs[:-1][::-1]
    rep = lax.axis_index("rep")
    width = refs[0].shape[1]
    for t in range(reps):
        total = functools.reduce(jnp.add, [refs[j * reps + t][...] for j in range(heads)])
        columns = pl.ds(pl.multiple_of((rep ^ t) * width, width), width)
        out_ref[0, :, columns] = total.astype(jnp.bfloat16)


def per_device(queries, latents, key_latent_maps, value_latent_maps, out_weight, lengths, selected):
    pools = lax.axis_size("pool")
    heads = lax.axis_size("heads")
    reps = lax.axis_size("rep")
    half_seqs, sel_count = selected.shape[1:]
    assert half_seqs == pools and pools % heads == 0
    shard_blocks = latents.shape[2] // BLOCK
    width = latents.shape[3] // 2
    rows = CAP * BLOCK
    own_heads = queries.shape[2] // HEAD_SIZE
    bf16, f32, i32 = jnp.bfloat16, jnp.float32, jnp.int32
    shape = jax.ShapeDtypeStruct
    freq = jnp.asarray(frequencies())

    def join(*blocks):
        return pl.pallas_call(
            join_kernel,
            out_shape=shape((sum(block.size for block in blocks) // queries.shape[2], queries.shape[2]), bf16),
            in_specs=[VMEM] * len(blocks),
            out_specs=VMEM,
            compiler_params=params(4),
            name="join",
        )(*blocks)

    def exchange(value, axis, size):
        taken = {step: swap(value, axis, size, step) for step in range(size - 1, 0, -1)}
        return [value] + [taken[step] for step in range(1, size)]

    def scatter(blocks, axis, size):
        taken = {step: swap(blocks[step], axis, size, step) for step in range(size - 1, 0, -1)}
        return [blocks[0]] + [taken[step] for step in range(1, size)]

    query_rows = queries.shape[2] // width
    packed = pl.pallas_call(
        functools.partial(gather_kernel, pools),
        out_shape=[shape((pools * rows, width), bf16)]
        + [shape((rows + query_rows, width), bf16)] * pools,
        in_specs=[SMEM, HBM, VMEM],
        out_specs=[VMEM] * (pools + 1),
        scratch_shapes=[
            pltpu.VMEM((pools * rows, 2 * width), bf16),
            pltpu.SemaphoreType.DMA((pools * CAP,)),
        ],
        compiler_params=params(16),
        name="gather",
    )(in_hbm(selected), in_hbm(latents), in_hbm(queries))
    keys, values = packed[0], packed[1:]

    cosine, sine, turn, live, place, key_maps, value_maps, held = pl.pallas_call(
        functools.partial(table_kernel, pools, shard_blocks),
        out_shape=[shape((pools * rows, HEAD_SIZE), f32)] * 2
        + [shape((2 * pools, HEAD_SIZE), f32), shape((pools, rows), i32), shape((1, pools * rows), i32)]
        + [shape(key_latent_maps.shape, bf16), shape(value_latent_maps.shape, bf16)]
        + [shape(values[1].shape, bf16)],
        in_specs=[SMEM, SMEM, VMEM] + [ANY] * 3,
        out_specs=[VMEM] * 7 + [ANY],
        scratch_shapes=[pltpu.SemaphoreType.DMA((2,))],
        input_output_aliases={5: 7},
        compiler_params=params(16),
        name="tables",
    )(
        in_hbm(selected), in_hbm(lengths), in_hbm(freq), in_hbm(key_latent_maps),
        in_hbm(value_latent_maps), values[1],
    )
    key_parts = exchange(keys, "heads", heads)
    value_parts = scatter([values[0], held, *values[2:]], "pool", pools)

    weight = pl.pallas_call(
        stage_kernel,
        out_shape=shape(out_weight.shape, bf16),
        in_specs=[HBM, ANY],
        out_specs=VMEM,
        scratch_shapes=[pltpu.SemaphoreType.DMA],
        compiler_params=params(4),
        name="stage",
    )(in_hbm(out_weight), place)
    turned = pl.pallas_call(
        functools.partial(rebuild_kernel, pools, heads),
        out_shape=shape((pools * rows, own_heads // QUERY_PER_GROUP * HEAD_SIZE), bf16),
        in_specs=[VMEM] * 3 + [ANY] + [VMEM] * heads,
        out_specs=VMEM,
        compiler_params=params(20),
        name="rebuild",
    )(key_maps, cosine, sine, weight, *key_parts)
    dense, *scores = pl.pallas_call(
        functools.partial(score_kernel, pools),
        out_shape=[shape((sel_count * BLOCK, width), bf16)] + [shape((own_heads, rows), f32)] * pools,
        in_specs=[VMEM] * (4 + pools),
        out_specs=[VMEM] * (1 + pools),
        compiler_params=params(16),
        name="score",
    )(turn, live, place, turned, *value_parts[::-1])
    dense_parts = exchange(dense, "heads", heads)
    score_parts = scatter(scores, "pool", pools)

    mine = pl.pallas_call(
        functools.partial(attend_kernel, pools, heads),
        out_shape=shape((1, own_heads * HEAD_SIZE), bf16),
        in_specs=[VMEM] * (2 + pools + heads),
        out_specs=VMEM,
        compiler_params=params(16),
        name="attend",
    )(value_maps, place, *score_parts[::-1], *dense_parts)
    own_rows = join(*exchange(mine, "rep", reps))
    row_parts = exchange(own_rows, "pool", pools)

    own_columns = out_weight.shape[1]
    each = pools // heads
    parts = pl.pallas_call(
        functools.partial(project_kernel, pools, heads, reps),
        out_shape=[shape((each, own_columns), f32)] * (heads * reps),
        in_specs=[VMEM] * (pools + 1),
        out_specs=[VMEM] * (heads * reps),
        scratch_shapes=[pltpu.VMEM((pools * reps, own_columns), f32)],
        compiler_params=params(24),
        name="project",
    )(weight, *row_parts)
    return pl.pallas_call(
        functools.partial(finish_kernel, heads, reps),
        out_shape=shape((1, each, reps * own_columns), bf16),
        in_specs=[VMEM] * (heads * reps),
        out_specs=VMEM,
        compiler_params=params(4),
        name="finish",
    )(*scatter(parts, ("heads", "rep"), heads * reps)[::-1])


def solution(mesh):
    return jax.shard_map(
        per_device,
        mesh=mesh,
        in_specs=(
            P(("groups", "rep"), "pool", "heads"),
            P(("groups", "rep"), None, "pool", "heads"),
            P(None, "heads"),
            P(None, "heads"),
            P("heads", ("pool", "rep")),
            P(("groups", "rep"), None),
            P(("groups", "rep"), None, None),
        ),
        out_specs=P(("groups", "rep"), "heads", "pool"),
        check_vma=False,
    )
```

```python
import functools

import jax
import jax.numpy as jnp
import numpy as np
from jax import lax
from jax.experimental import pallas as pl
from jax.experimental.pallas import tpu as pltpu
from jax.sharding import PartitionSpec as P

HEAD_SIZE = 128
LANE = 64
BLOCK = 128
CAP = 2
QUERY_PER_GROUP = 8

ROPE_BASE = 500000.0
MASKED = -1e30
FAR = 1 << 29

SMEM = pl.BlockSpec(memory_space=pltpu.SMEM)
VMEM = pl.BlockSpec(memory_space=pltpu.VMEM)
ANY = pl.BlockSpec(memory_space=pl.ANY)
HBM = pl.BlockSpec(memory_space=pltpu.HBM)


def frequencies():
    half = HEAD_SIZE // 2
    exponents = np.arange(half, dtype=np.float32) * np.float32(2.0 / HEAD_SIZE)
    freq = np.power(np.float64(ROPE_BASE), -exponents.astype(np.float64)).astype(np.float32)
    return np.concatenate([freq, freq])[None, :]


def swap(value, axes, size, step):
    return lax.ppermute(value, axes, [(i, i ^ step) for i in range(size)])


def in_hbm(value):
    return pltpu.with_memory_space_constraint(value, pltpu.HBM)


def in_vmem(value):
    return pltpu.with_memory_space_constraint(value, pltpu.VMEM)


def params(mib, **more):
    return pltpu.CompilerParams(vmem_limit_bytes=mib << 20, **more)


def slot_blocks(sel_ref, seq, shard, shard_blocks):
    first = jnp.int32(-1)
    second = jnp.int32(-1)
    for i in range(sel_ref.shape[2]):
        block = sel_ref[0, seq, i]
        here = (block >= shard * shard_blocks) & (block < (shard + 1) * shard_blocks)
        second = jnp.where(here & (first >= 0), block, second)
        first = jnp.where(here & (first < 0), block, first)
    return first, second


def heads_to_rows(line, lanes):
    count = line.shape[1] // HEAD_SIZE
    rows = jnp.concatenate([line[:, n * HEAD_SIZE : (n + 1) * HEAD_SIZE] for n in range(count)], axis=0)
    if lanes < HEAD_SIZE:
        return jnp.concatenate([rows[:, i : i + lanes] for i in range(0, HEAD_SIZE, lanes)], axis=0)
    each = count * HEAD_SIZE // lanes
    return jnp.concatenate([rows[i : i + each, :] for i in range(0, count, each)], axis=1)


def rows_to_heads(rows):
    count, lanes = rows.shape
    if lanes < HEAD_SIZE:
        each = count * lanes // HEAD_SIZE
        return jnp.concatenate([rows[i : i + each, :] for i in range(0, count, each)], axis=1)
    return jnp.concatenate([rows[:, i : i + HEAD_SIZE] for i in range(0, lanes, HEAD_SIZE)], axis=0)


def gather_kernel(pools, sel_ref, lat_ref, query_ref, keys_ref, *rest):
    value_refs = rest[:pools]
    raw, sems = rest[pools:]
    shard_blocks = lat_ref.shape[2] // BLOCK
    columns = lat_ref.shape[3]
    width = columns // 2
    rows = CAP * BLOCK
    me = lax.axis_index("pool")
    copies = {}
    for k in range(pools - 1, -1, -1):
        seq = me ^ k
        for c, block in enumerate(slot_blocks(sel_ref, seq, me, shard_blocks)):
            local = jnp.maximum(block - me * shard_blocks, 0)
            copies[k, c] = pltpu.make_async_copy(
                lat_ref.at[0, seq, pl.ds(pl.multiple_of(local * BLOCK, BLOCK), BLOCK), :],
                raw.at[pl.ds((k * CAP + c) * BLOCK, BLOCK), :],
                sems.at[k * CAP + c],
            )
            copies[k, c].start()
    chunk = min(4 * LANE, columns)
    half = chunk // 2
    source = lax.broadcasted_iota(jnp.int32, (chunk, chunk), 0)
    target = lax.broadcasted_iota(jnp.int32, (chunk, chunk), 1)
    within = target & (half - 1)
    wanted = ((within >> 6) << 7) + (within & (LANE - 1)) + jnp.where(target >= half, LANE, 0)
    pick = (source == wanted).astype(jnp.float32).astype(jnp.bfloat16)
    queries = heads_to_rows(query_ref[0].astype(jnp.float32), width).astype(jnp.bfloat16)
    for copy in copies.values():
        copy.wait()
    for j in range(columns // chunk):
        packed = jnp.dot(
            raw[:, j * chunk : (j + 1) * chunk], pick, preferred_element_type=jnp.float32
        ).astype(jnp.bfloat16)
        keys_ref[:, j * half : (j + 1) * half] = packed[:, :half]
        for k in range(pools):
            value_refs[k][:rows, j * half : (j + 1) * half] = packed[k * rows : (k + 1) * rows, half:]
    for k in range(pools):
        value_refs[k][rows:, :] = queries


def table_kernel(pools, shard_blocks, sel_ref, len_ref, freq_ref, key_map_ref, value_map_ref, held_ref, *rest):
    cos_ref, sin_ref, turn_ref, live_ref, place_ref, key_out_ref, value_out_ref = rest[:7]
    sems = rest[-1]
    loads = [
        pltpu.make_async_copy(key_map_ref, key_out_ref, sems.at[0]),
        pltpu.make_async_copy(value_map_ref, value_out_ref, sems.at[1]),
    ]
    for load in loads:
        load.start()
    me = lax.axis_index("pool")
    lane = lax.broadcasted_iota(jnp.int32, (BLOCK, HEAD_SIZE), 1)
    row = lax.broadcasted_iota(jnp.int32, (BLOCK, HEAD_SIZE), 0)
    front = lane < HEAD_SIZE // 2
    across = lax.broadcasted_iota(jnp.int32, (1, BLOCK), 1)
    place = jnp.int32(0)
    for k in range(pools):
        turn_ref[k : k + 1, :] = len_ref[0, me ^ k].astype(jnp.float32) * freq_ref[...]
    angle = turn_ref[0:pools, :]
    turn_ref[0:pools, :] = jnp.cos(angle)
    turn_ref[pools:, :] = jnp.where(front[:1, :], -jnp.sin(angle), jnp.sin(angle))
    for k in range(pools):
        seq = me ^ k
        found = slot_blocks(sel_ref, seq, me, shard_blocks)
        one, two = [jnp.maximum(block, 0) * BLOCK for block in found]
        angle = (jnp.where(front, one, two) + row).astype(jnp.float32) * freq_ref[...]
        for ref, table, sign in ((cos_ref, jnp.cos(angle), 1.0), (sin_ref, jnp.sin(angle), -1.0)):
            turned = pltpu.roll(table, HEAD_SIZE // 2, 1)
            at = k * CAP * BLOCK
            ref[at : at + BLOCK, :] = jnp.where(front, sign * table, turned)
            ref[at + BLOCK : at + 2 * BLOCK, :] = jnp.where(front, sign * turned, table)
        mine = slot_blocks(sel_ref, me, seq, shard_blocks)
        for c in range(CAP):
            start = jnp.where(found[c] < 0, FAR, found[c] * BLOCK)
            live_ref[k : k + 1, c * BLOCK : (c + 1) * BLOCK] = (start + across < len_ref[0, seq]).astype(jnp.int32)
            at = (k * CAP + c) * BLOCK
            used = mine[c] >= 0
            place_ref[:, at : at + BLOCK] = jnp.where(used, place, -1) + 0 * across
            place = place + used.astype(jnp.int32)
    for load in loads:
        load.wait()


def stage_kernel(weight_ref, after_ref, out_ref, sem):
    del after_ref
    load = pltpu.make_async_copy(weight_ref, out_ref, sem)
    load.start()
    load.wait()


def rebuild_kernel(pools, heads, map_ref, cos_ref, sin_ref, after_ref, *rest):
    del after_ref
    key_refs = rest[:heads]
    out_ref = rest[heads]
    head = lax.axis_index("heads")
    width = key_refs[0].shape[1]
    maps = []
    for j in range(heads):
        owner = head ^ j
        maps.append(map_ref[pl.ds(pl.multiple_of(owner * width, width), width), :])
    for g in range(0, map_ref.shape[1] // HEAD_SIZE, 2):
        pair = slice(g * HEAD_SIZE, min((g + 2) * HEAD_SIZE, map_ref.shape[1]))
        rebuilt = jnp.dot(key_refs[0][...], maps[0][:, pair], preferred_element_type=jnp.float32)
        for j in range(1, heads):
            rebuilt += jnp.dot(key_refs[j][...], maps[j][:, pair], preferred_element_type=jnp.float32)
        for at in range(0, pair.stop - pair.start, HEAD_SIZE):
            one = rebuilt[:, at : at + HEAD_SIZE]
            turned = one * cos_ref[...] + pltpu.roll(one, HEAD_SIZE // 2, 1) * sin_ref[...]
            out_ref[:, pair.start + at : pair.start + at + HEAD_SIZE] = turned.astype(jnp.bfloat16)


def score_kernel(pools, turn_ref, live_ref, place_ref, key_ref, *rest):
    pay_refs = rest[:pools][::-1]
    dense_ref = rest[pools]
    out_refs = rest[pools + 1 :]
    groups = key_ref.shape[1] // HEAD_SIZE
    rows = CAP * BLOCK
    width = dense_ref.shape[1]
    kept = dense_ref.shape[0] // BLOCK
    for k in range(pools - 1, -1, -1):
        live = live_ref[k : k + 1, :] > 0
        query = rows_to_heads(pay_refs[k][rows:, :].astype(jnp.float32))
        query = query * turn_ref[k : k + 1, :] + pltpu.roll(query, HEAD_SIZE // 2, 1) * turn_ref[
            pools + k : pools + k + 1, :
        ]
        query = query.astype(jnp.bfloat16)
        for g in range(groups):
            mine = slice(g * QUERY_PER_GROUP, (g + 1) * QUERY_PER_GROUP)
            scores = lax.dot_general(
                query[mine, :], key_ref[k * rows : (k + 1) * rows, g * HEAD_SIZE : (g + 1) * HEAD_SIZE],
                (((1,), (1,)), ((), ())), preferred_element_type=jnp.float32,
            ) * (HEAD_SIZE ** -0.5)
            out_refs[k][mine, :] = jnp.where(live, scores, MASKED)
    spare = pools * CAP - kept
    for i in range(kept):
        chosen = jnp.zeros((BLOCK, width), jnp.float32)
        for slot in range(i, i + spare + 1):
            place = place_ref[:, slot * BLOCK : slot * BLOCK + LANE]
            place = jnp.concatenate([place] * (width // LANE), axis=1)
            k, c = slot // CAP, slot % CAP
            block = pay_refs[k][c * BLOCK : (c + 1) * BLOCK, :].astype(jnp.float32)
            chosen = jnp.where(place == i, block, chosen)
        dense_ref[i * BLOCK : (i + 1) * BLOCK, :] = chosen.astype(jnp.bfloat16)


def attend_kernel(pools, heads, map_ref, place_ref, *rest):
    score_refs = rest[:pools][::-1]
    value_refs = rest[pools : pools + heads]
    out_ref = rest[-1]
    head = lax.axis_index("heads")
    width = value_refs[0].shape[1]
    groups = map_ref.shape[1] // HEAD_SIZE
    scores = [ref[...] for ref in score_refs]
    top = functools.reduce(jnp.maximum, [jnp.max(s, axis=1, keepdims=True) for s in scores])
    weights = [jnp.exp(s - top) for s in scores]
    total = functools.reduce(jnp.add, [jnp.sum(w, axis=1, keepdims=True) for w in weights])
    slots = []
    for k in range(pools):
        attention = weights[k] / total
        for c in range(CAP):
            at = (k * CAP + c) * BLOCK
            slots.append((place_ref[:, at : at + BLOCK], attention[:, c * BLOCK : (c + 1) * BLOCK]))
    dense = []
    kept = value_refs[0].shape[0] // BLOCK
    for i in range(kept):
        chosen = jnp.zeros_like(slots[0][1])
        for place, attention in slots[i : i + len(slots) - kept + 1]:
            chosen = jnp.where(place == i, attention, chosen)
        dense.append(chosen)
    attention = jnp.concatenate(dense, axis=1).astype(jnp.bfloat16)
    mixed = [None] * groups
    for j in range(heads):
        owner = head ^ j
        context = jnp.dot(
            attention, value_refs[j][...], preferred_element_type=jnp.float32
        ).astype(jnp.bfloat16)
        rows = pl.ds(pl.multiple_of(owner * width, width), width)
        for g in range(groups):
            part = jnp.dot(
                context[g * QUERY_PER_GROUP : (g + 1) * QUERY_PER_GROUP, :],
                map_ref[rows, g * HEAD_SIZE : (g + 1) * HEAD_SIZE],
                preferred_element_type=jnp.float32,
            )
            mixed[g] = part if j == 0 else mixed[g] + part
    for g in range(groups):
        for q in range(QUERY_PER_GROUP):
            at = (g * QUERY_PER_GROUP + q) * HEAD_SIZE
            out_ref[:, at : at + HEAD_SIZE] = mixed[g][q : q + 1, :].astype(jnp.bfloat16)


def join_kernel(*refs):
    rows = [ref[...].reshape(-1, ref.shape[-1]).astype(jnp.float32) for ref in refs[:-1]]
    refs[-1][...] = jnp.concatenate(rows, axis=0).astype(jnp.bfloat16)


def project_kernel(pools, heads, reps, weight_ref, *rest):
    row_refs = rest[:pools]
    out_refs = rest[pools:-1]
    acc = rest[-1]
    left = jnp.concatenate([ref[...].astype(jnp.float32) for ref in row_refs], axis=0).astype(jnp.bfloat16)
    acc[...] = jnp.dot(left, weight_ref[...], preferred_element_type=jnp.float32)
    pool = lax.axis_index("pool")
    head = lax.axis_index("heads")
    each = pools // heads
    for d in range(heads * reps):
        for u in range(each):
            n = (pool ^ ((head ^ (d // reps)) * each + u)) * reps + d % reps
            out_refs[d][u : u + 1, :] = acc[pl.ds(n, 1), :]


def finish_kernel(heads, reps, *refs):
    out_ref = refs[-1]
    refs = refs[:-1][::-1]
    rep = lax.axis_index("rep")
    width = refs[0].shape[1]
    for t in range(reps):
        total = functools.reduce(jnp.add, [refs[j * reps + t][...] for j in range(heads)])
        columns = pl.ds(pl.multiple_of((rep ^ t) * width, width), width)
        out_ref[0, :, columns] = total.astype(jnp.bfloat16)


def per_device(queries, latents, key_latent_maps, value_latent_maps, out_weight, lengths, selected):
    pools = lax.axis_size("pool")
    heads = lax.axis_size("heads")
    reps = lax.axis_size("rep")
    half_seqs, sel_count = selected.shape[1:]
    assert half_seqs == pools and pools % heads == 0
    shard_blocks = latents.shape[2] // BLOCK
    width = latents.shape[3] // 2
    rows = CAP * BLOCK
    own_heads = queries.shape[2] // HEAD_SIZE
    bf16, f32, i32 = jnp.bfloat16, jnp.float32, jnp.int32
    shape = jax.ShapeDtypeStruct
    freq = jnp.asarray(frequencies())

    def join(*blocks):
        return pl.pallas_call(
            join_kernel,
            out_shape=shape((sum(block.size for block in blocks) // queries.shape[2], queries.shape[2]), bf16),
            in_specs=[VMEM] * len(blocks),
            out_specs=VMEM,
            compiler_params=params(4),
            name="join",
        )(*blocks)

    def exchange(value, axis, size):
        taken = {step: swap(value, axis, size, step) for step in range(size - 1, 0, -1)}
        return [value] + [taken[step] for step in range(1, size)]

    def scatter(blocks, axis, size):
        taken = {step: swap(blocks[step], axis, size, step) for step in range(size - 1, 0, -1)}
        return [blocks[0]] + [taken[step] for step in range(1, size)]

    query_rows = queries.shape[2] // width
    packed = pl.pallas_call(
        functools.partial(gather_kernel, pools),
        out_shape=[shape((pools * rows, width), bf16)]
        + [shape((rows + query_rows, width), bf16)] * pools,
        in_specs=[SMEM, HBM, VMEM],
        out_specs=[VMEM] * (pools + 1),
        scratch_shapes=[
            pltpu.VMEM((pools * rows, 2 * width), bf16),
            pltpu.SemaphoreType.DMA((pools * CAP,)),
        ],
        compiler_params=params(16),
        name="gather",
    )(in_hbm(selected), in_hbm(latents), in_hbm(queries))
    keys, values = packed[0], packed[1:]

    cosine, sine, turn, live, place, key_maps, value_maps, held = pl.pallas_call(
        functools.partial(table_kernel, pools, shard_blocks),
        out_shape=[shape((pools * rows, HEAD_SIZE), f32)] * 2
        + [shape((2 * pools, HEAD_SIZE), f32), shape((pools, rows), i32), shape((1, pools * rows), i32)]
        + [shape(key_latent_maps.shape, bf16), shape(value_latent_maps.shape, bf16)]
        + [shape(values[1].shape, bf16)],
        in_specs=[SMEM, SMEM, VMEM] + [ANY] * 3,
        out_specs=[VMEM] * 7 + [ANY],
        scratch_shapes=[pltpu.SemaphoreType.DMA((2,))],
        input_output_aliases={5: 7},
        compiler_params=params(16),
        name="tables",
    )(
        in_hbm(selected), in_hbm(lengths), in_hbm(freq), in_hbm(key_latent_maps),
        in_hbm(value_latent_maps), values[1],
    )
    key_parts = exchange(keys, "heads", heads)
    value_parts = scatter([values[0], held, *values[2:]], "pool", pools)

    weight = pl.pallas_call(
        stage_kernel,
        out_shape=shape(out_weight.shape, bf16),
        in_specs=[HBM, ANY],
        out_specs=VMEM,
        scratch_shapes=[pltpu.SemaphoreType.DMA],
        compiler_params=params(4),
        name="stage",
    )(in_hbm(out_weight), place)
    turned = pl.pallas_call(
        functools.partial(rebuild_kernel, pools, heads),
        out_shape=shape((pools * rows, own_heads // QUERY_PER_GROUP * HEAD_SIZE), bf16),
        in_specs=[VMEM] * 3 + [ANY] + [VMEM] * heads,
        out_specs=VMEM,
        compiler_params=params(20),
        name="rebuild",
    )(key_maps, cosine, sine, weight, *key_parts)
    dense, *scores = pl.pallas_call(
        functools.partial(score_kernel, pools),
        out_shape=[shape((sel_count * BLOCK, width), bf16)] + [shape((own_heads, rows), f32)] * pools,
        in_specs=[VMEM] * (4 + pools),
        out_specs=[VMEM] * (1 + pools),
        compiler_params=params(16),
        name="score",
    )(turn, live, place, turned, *value_parts[::-1])
    dense_parts = exchange(dense, "heads", heads)
    score_parts = scatter(scores, "pool", pools)

    mine = pl.pallas_call(
        functools.partial(attend_kernel, pools, heads),
        out_shape=shape((1, own_heads * HEAD_SIZE), bf16),
        in_specs=[VMEM] * (2 + pools + heads),
        out_specs=VMEM,
        compiler_params=params(16),
        name="attend",
    )(value_maps, place, *score_parts[::-1], *dense_parts)
    own_rows = join(*exchange(mine, "rep", reps))
    row_parts = exchange(own_rows, "pool", pools)

    own_columns = out_weight.shape[1]
    each = pools // heads
    parts = pl.pallas_call(
        functools.partial(project_kernel, pools, heads, reps),
        out_shape=[shape((each, own_columns), f32)] * (heads * reps),
        in_specs=[VMEM] * (pools + 1),
        out_specs=[VMEM] * (heads * reps),
        scratch_shapes=[pltpu.VMEM((pools * reps, own_columns), f32)],
        compiler_params=params(24),
        name="project",
    )(weight, *row_parts)
    return pl.pallas_call(
        functools.partial(finish_kernel, heads, reps),
        out_shape=shape((1, each, reps * own_columns), bf16),
        in_specs=[VMEM] * (heads * reps),
        out_specs=VMEM,
        compiler_params=params(4),
        name="finish",
    )(*scatter(parts, ("heads", "rep"), heads * reps)[::-1])


def solution(mesh):
    return jax.shard_map(
        per_device,
        mesh=mesh,
        in_specs=(
            P(("groups", "rep"), "pool", "heads"),
            P(("groups", "rep"), None, "pool", "heads"),
            P(None, "heads"),
            P(None, "heads"),
            P("heads", ("pool", "rep")),
            P(("groups", "rep"), None),
            P(("groups", "rep"), None, None),
        ),
        out_specs=P(("groups", "rep"), "heads", "pool"),
        check_vma=False,
    )
```

```python
import functools

import jax
import jax.numpy as jnp
import numpy as np
from jax import lax
from jax.experimental import pallas as pl
from jax.experimental.pallas import tpu as pltpu
from jax.sharding import PartitionSpec as P

HEAD_SIZE = 128
LANE = 64
BLOCK = 128
CAP = 2
QUERY_PER_GROUP = 8

ROPE_BASE = 500000.0
MASKED = -1e30
FAR = 1 << 29

SMEM = pl.BlockSpec(memory_space=pltpu.SMEM)
VMEM = pl.BlockSpec(memory_space=pltpu.VMEM)
ANY = pl.BlockSpec(memory_space=pl.ANY)
HBM = pl.BlockSpec(memory_space=pltpu.HBM)


def frequencies():
    half = HEAD_SIZE // 2
    exponents = np.arange(half, dtype=np.float32) * np.float32(2.0 / HEAD_SIZE)
    freq = np.power(np.float64(ROPE_BASE), -exponents.astype(np.float64)).astype(np.float32)
    return np.concatenate([freq, freq])[None, :]


def swap(value, axes, size, step):
    return lax.ppermute(value, axes, [(i, i ^ step) for i in range(size)])


def in_hbm(value):
    return pltpu.with_memory_space_constraint(value, pltpu.HBM)


def in_vmem(value):
    return pltpu.with_memory_space_constraint(value, pltpu.VMEM)


def served(size):
    middle = size // 2
    return [middle] + [k for k in range(size - 1, -1, -1) if k != middle]


def params(mib, **more):
    return pltpu.CompilerParams(vmem_limit_bytes=mib << 20, **more)


def slot_blocks(sel_ref, seq, shard, shard_blocks):
    first = jnp.int32(-1)
    second = jnp.int32(-1)
    for i in range(sel_ref.shape[2]):
        block = sel_ref[0, seq, i]
        here = (block >= shard * shard_blocks) & (block < (shard + 1) * shard_blocks)
        second = jnp.where(here & (first >= 0), block, second)
        first = jnp.where(here & (first < 0), block, first)
    return first, second


def heads_to_rows(line, lanes):
    count = line.shape[1] // HEAD_SIZE
    rows = jnp.concatenate([line[:, n * HEAD_SIZE : (n + 1) * HEAD_SIZE] for n in range(count)], axis=0)
    if lanes < HEAD_SIZE:
        return jnp.concatenate([rows[:, i : i + lanes] for i in range(0, HEAD_SIZE, lanes)], axis=0)
    each = count * HEAD_SIZE // lanes
    return jnp.concatenate([rows[i : i + each, :] for i in range(0, count, each)], axis=1)


def rows_to_heads(rows):
    count, lanes = rows.shape
    if lanes < HEAD_SIZE:
        each = count * lanes // HEAD_SIZE
        return jnp.concatenate([rows[i : i + each, :] for i in range(0, count, each)], axis=1)
    return jnp.concatenate([rows[:, i : i + HEAD_SIZE] for i in range(0, lanes, HEAD_SIZE)], axis=0)


def gather_kernel(pools, sel_ref, lat_ref, query_ref, keys_ref, *rest):
    value_refs = rest[:pools]
    raw, sems = rest[pools:]
    shard_blocks = lat_ref.shape[2] // BLOCK
    columns = lat_ref.shape[3]
    width = columns // 2
    rows = CAP * BLOCK
    me = lax.axis_index("pool")
    copies = {}
    for k in range(pools - 1, -1, -1):
        seq = me ^ k
        for c, block in enumerate(slot_blocks(sel_ref, seq, me, shard_blocks)):
            local = jnp.maximum(block - me * shard_blocks, 0)
            copies[k, c] = pltpu.make_async_copy(
                lat_ref.at[0, seq, pl.ds(pl.multiple_of(local * BLOCK, BLOCK), BLOCK), :],
                raw.at[pl.ds((k * CAP + c) * BLOCK, BLOCK), :],
                sems.at[k * CAP + c],
            )
            copies[k, c].start()
    chunk = min(4 * LANE, columns)
    half = chunk // 2
    source = lax.broadcasted_iota(jnp.int32, (chunk, chunk), 0)
    target = lax.broadcasted_iota(jnp.int32, (chunk, chunk), 1)
    within = target & (half - 1)
    wanted = ((within >> 6) << 7) + (within & (LANE - 1)) + jnp.where(target >= half, LANE, 0)
    pick = (source == wanted).astype(jnp.float32).astype(jnp.bfloat16)
    queries = heads_to_rows(query_ref[0].astype(jnp.float32), width).astype(jnp.bfloat16)
    for copy in copies.values():
        copy.wait()
    for j in range(columns // chunk):
        packed = jnp.dot(
            raw[:, j * chunk : (j + 1) * chunk], pick, preferred_element_type=jnp.float32
        ).astype(jnp.bfloat16)
        keys_ref[:, j * half : (j + 1) * half] = packed[:, :half]
        for k in range(pools):
            value_refs[k][:rows, j * half : (j + 1) * half] = packed[k * rows : (k + 1) * rows, half:]
    for k in range(pools):
        value_refs[k][rows:, :] = queries


def table_kernel(pools, shard_blocks, sel_ref, len_ref, freq_ref, key_map_ref, value_map_ref, held_ref, *rest):
    cos_ref, sin_ref, turn_ref, live_ref, place_ref, key_out_ref, value_out_ref = rest[:7]
    sems = rest[-1]
    loads = [
        pltpu.make_async_copy(key_map_ref, key_out_ref, sems.at[0]),
        pltpu.make_async_copy(value_map_ref, value_out_ref, sems.at[1]),
    ]
    for load in loads:
        load.start()
    me = lax.axis_index("pool")
    lane = lax.broadcasted_iota(jnp.int32, (BLOCK, HEAD_SIZE), 1)
    row = lax.broadcasted_iota(jnp.int32, (BLOCK, HEAD_SIZE), 0)
    front = lane < HEAD_SIZE // 2
    across = lax.broadcasted_iota(jnp.int32, (1, BLOCK), 1)
    place = jnp.int32(0)
    for k in range(pools):
        turn_ref[k : k + 1, :] = len_ref[0, me ^ k].astype(jnp.float32) * freq_ref[...]
    angle = turn_ref[0:pools, :]
    turn_ref[0:pools, :] = jnp.cos(angle)
    turn_ref[pools:, :] = jnp.where(front[:1, :], -jnp.sin(angle), jnp.sin(angle))
    for k in range(pools):
        seq = me ^ k
        found = slot_blocks(sel_ref, seq, me, shard_blocks)
        one, two = [jnp.maximum(block, 0) * BLOCK for block in found]
        angle = (jnp.where(front, one, two) + row).astype(jnp.float32) * freq_ref[...]
        for ref, table, sign in ((cos_ref, jnp.cos(angle), 1.0), (sin_ref, jnp.sin(angle), -1.0)):
            turned = pltpu.roll(table, HEAD_SIZE // 2, 1)
            at = k * CAP * BLOCK
            ref[at : at + BLOCK, :] = jnp.where(front, sign * table, turned)
            ref[at + BLOCK : at + 2 * BLOCK, :] = jnp.where(front, sign * turned, table)
        mine = slot_blocks(sel_ref, me, seq, shard_blocks)
        for c in range(CAP):
            start = jnp.where(found[c] < 0, FAR, found[c] * BLOCK)
            live_ref[k : k + 1, c * BLOCK : (c + 1) * BLOCK] = (start + across < len_ref[0, seq]).astype(jnp.int32)
            at = (k * CAP + c) * BLOCK
            used = mine[c] >= 0
            place_ref[:, at : at + BLOCK] = jnp.where(used, place, -1) + 0 * across
            place = place + used.astype(jnp.int32)
    for load in loads:
        load.wait()


def stage_kernel(weight_ref, after_ref, out_ref, sem):
    del after_ref
    load = pltpu.make_async_copy(weight_ref, out_ref, sem)
    load.start()
    load.wait()


def rebuild_kernel(pools, heads, map_ref, cos_ref, sin_ref, after_ref, *rest):
    del after_ref
    key_refs = rest[:heads]
    out_ref = rest[heads]
    head = lax.axis_index("heads")
    width = key_refs[0].shape[1]
    rows = CAP * BLOCK
    maps = []
    for j in range(heads):
        owner = head ^ j
        maps.append(map_ref[pl.ds(pl.multiple_of(owner * width, width), width), :])
    for k in range(pools):
        at = slice(k * rows, (k + 1) * rows)
        rebuilt = jnp.dot(key_refs[0][at, :], maps[0], preferred_element_type=jnp.float32)
        for j in range(1, heads):
            rebuilt += jnp.dot(key_refs[j][at, :], maps[j], preferred_element_type=jnp.float32)
        cosine = cos_ref[at, :]
        sine = sin_ref[at, :]
        for g in range(map_ref.shape[1] // HEAD_SIZE):
            lanes = slice(g * HEAD_SIZE, (g + 1) * HEAD_SIZE)
            one = rebuilt[:, lanes]
            out_ref[at, lanes] = (one * cosine + pltpu.roll(one, HEAD_SIZE // 2, 1) * sine).astype(jnp.bfloat16)


def score_kernel(pools, turn_ref, live_ref, place_ref, key_ref, *rest):
    pay_refs = rest[:pools][::-1]
    dense_ref = rest[pools]
    out_refs = rest[pools + 1 :]
    groups = key_ref.shape[1] // HEAD_SIZE
    rows = CAP * BLOCK
    width = dense_ref.shape[1]
    kept = dense_ref.shape[0] // BLOCK
    for k in range(pools - 1, -1, -1):
        live = live_ref[k : k + 1, :] > 0
        query = rows_to_heads(pay_refs[k][rows:, :].astype(jnp.float32))
        query = query * turn_ref[k : k + 1, :] + pltpu.roll(query, HEAD_SIZE // 2, 1) * turn_ref[
            pools + k : pools + k + 1, :
        ]
        query = query.astype(jnp.bfloat16)
        for g in range(groups):
            mine = slice(g * QUERY_PER_GROUP, (g + 1) * QUERY_PER_GROUP)
            scores = lax.dot_general(
                query[mine, :], key_ref[k * rows : (k + 1) * rows, g * HEAD_SIZE : (g + 1) * HEAD_SIZE],
                (((1,), (1,)), ((), ())), preferred_element_type=jnp.float32,
            ) * (HEAD_SIZE ** -0.5)
            out_refs[k][mine, :] = jnp.where(live, scores, MASKED)
    spare = pools * CAP - kept
    for i in range(kept):
        chosen = jnp.zeros((BLOCK, width), jnp.float32)
        for slot in range(i, i + spare + 1):
            place = place_ref[:, slot * BLOCK : slot * BLOCK + LANE]
            place = jnp.concatenate([place] * (width // LANE), axis=1)
            k, c = slot // CAP, slot % CAP
            block = pay_refs[k][c * BLOCK : (c + 1) * BLOCK, :].astype(jnp.float32)
            chosen = jnp.where(place == i, block, chosen)
        dense_ref[i * BLOCK : (i + 1) * BLOCK, :] = chosen.astype(jnp.bfloat16)


def attend_kernel(pools, heads, map_ref, place_ref, *rest):
    score_refs = [rest[served(pools).index(k)] for k in range(pools)]
    value_refs = rest[pools : pools + heads]
    out_ref = rest[-1]
    head = lax.axis_index("heads")
    width = value_refs[0].shape[1]
    groups = map_ref.shape[1] // HEAD_SIZE
    scores = [ref[...] for ref in score_refs]
    top = functools.reduce(jnp.maximum, [jnp.max(s, axis=1, keepdims=True) for s in scores])
    weights = [jnp.exp(s - top) for s in scores]
    total = functools.reduce(jnp.add, [jnp.sum(w, axis=1, keepdims=True) for w in weights])
    slots = []
    for k in range(pools):
        attention = weights[k] / total
        for c in range(CAP):
            at = (k * CAP + c) * BLOCK
            slots.append((place_ref[:, at : at + BLOCK], attention[:, c * BLOCK : (c + 1) * BLOCK]))
    dense = []
    kept = value_refs[0].shape[0] // BLOCK
    for i in range(kept):
        chosen = jnp.zeros_like(slots[0][1])
        for place, attention in slots[i : i + len(slots) - kept + 1]:
            chosen = jnp.where(place == i, attention, chosen)
        dense.append(chosen)
    attention = jnp.concatenate(dense, axis=1).astype(jnp.bfloat16)
    mixed = [None] * groups
    for j in range(heads):
        owner = head ^ j
        context = jnp.dot(
            attention, value_refs[j][...], preferred_element_type=jnp.float32
        ).astype(jnp.bfloat16)
        rows = pl.ds(pl.multiple_of(owner * width, width), width)
        for g in range(groups):
            part = jnp.dot(
                context[g * QUERY_PER_GROUP : (g + 1) * QUERY_PER_GROUP, :],
                map_ref[rows, g * HEAD_SIZE : (g + 1) * HEAD_SIZE],
                preferred_element_type=jnp.float32,
            )
            mixed[g] = part if j == 0 else mixed[g] + part
    for g in range(groups):
        for q in range(QUERY_PER_GROUP):
            at = (g * QUERY_PER_GROUP + q) * HEAD_SIZE
            out_ref[:, at : at + HEAD_SIZE] = mixed[g][q : q + 1, :].astype(jnp.bfloat16)


def join_kernel(*refs):
    rows = [ref[...].reshape(-1, ref.shape[-1]).astype(jnp.float32) for ref in refs[:-1]]
    refs[-1][...] = jnp.concatenate(rows, axis=0).astype(jnp.bfloat16)


def project_kernel(pools, heads, reps, weight_ref, *rest):
    row_refs = [rest[served(pools)[::-1].index(k)] for k in range(pools)]
    out_refs = rest[pools:-1]
    acc = rest[-1]
    left = jnp.concatenate([ref[...].astype(jnp.float32) for ref in row_refs], axis=0).astype(jnp.bfloat16)
    acc[...] = jnp.dot(left, weight_ref[...], preferred_element_type=jnp.float32)
    pool = lax.axis_index("pool")
    head = lax.axis_index("heads")
    each = pools // heads
    for d in range(heads * reps):
        for u in range(each):
            n = (pool ^ ((head ^ (d // reps)) * each + u)) * reps + d % reps
            out_refs[d][u : u + 1, :] = acc[pl.ds(n, 1), :]


def finish_kernel(heads, reps, *refs):
    out_ref = refs[-1]
    refs = refs[:-1][::-1]
    rep = lax.axis_index("rep")
    width = refs[0].shape[1]
    for t in range(reps):
        total = functools.reduce(jnp.add, [refs[j * reps + t][...] for j in range(heads)])
        columns = pl.ds(pl.multiple_of((rep ^ t) * width, width), width)
        out_ref[0, :, columns] = total.astype(jnp.bfloat16)


def per_device(queries, latents, key_latent_maps, value_latent_maps, out_weight, lengths, selected):
    pools = lax.axis_size("pool")
    heads = lax.axis_size("heads")
    reps = lax.axis_size("rep")
    half_seqs, sel_count = selected.shape[1:]
    assert half_seqs == pools and pools % heads == 0
    shard_blocks = latents.shape[2] // BLOCK
    width = latents.shape[3] // 2
    rows = CAP * BLOCK
    own_heads = queries.shape[2] // HEAD_SIZE
    bf16, f32, i32 = jnp.bfloat16, jnp.float32, jnp.int32
    shape = jax.ShapeDtypeStruct
    freq = jnp.asarray(frequencies())

    def join(*blocks):
        return pl.pallas_call(
            join_kernel,
            out_shape=shape((sum(block.size for block in blocks) // queries.shape[2], queries.shape[2]), bf16),
            in_specs=[VMEM] * len(blocks),
            out_specs=VMEM,
            compiler_params=params(4),
            name="join",
        )(*blocks)

    def exchange(value, axis, size):
        taken = {step: swap(value, axis, size, step) for step in range(size - 1, 0, -1)}
        return [value] + [taken[step] for step in range(1, size)]

    def scatter(blocks, axis, size):
        taken = {step: swap(blocks[step], axis, size, step) for step in range(size - 1, 0, -1)}
        return [blocks[0]] + [taken[step] for step in range(1, size)]

    query_rows = queries.shape[2] // width
    packed = pl.pallas_call(
        functools.partial(gather_kernel, pools),
        out_shape=[shape((pools * rows, width), bf16)]
        + [shape((rows + query_rows, width), bf16)] * pools,
        in_specs=[SMEM, HBM, VMEM],
        out_specs=[VMEM] * (pools + 1),
        scratch_shapes=[
            pltpu.VMEM((pools * rows, 2 * width), bf16),
            pltpu.SemaphoreType.DMA((pools * CAP,)),
        ],
        compiler_params=params(16),
        name="gather",
    )(in_hbm(selected), in_hbm(latents), in_hbm(queries))
    keys, values = packed[0], packed[1:]

    cosine, sine, turn, live, place, key_maps, value_maps, held = pl.pallas_call(
        functools.partial(table_kernel, pools, shard_blocks),
        out_shape=[shape((pools * rows, HEAD_SIZE), f32)] * 2
        + [shape((2 * pools, HEAD_SIZE), f32), shape((pools, rows), i32), shape((1, pools * rows), i32)]
        + [shape(key_latent_maps.shape, bf16), shape(value_latent_maps.shape, bf16)]
        + [shape(values[1].shape, bf16)],
        in_specs=[SMEM, SMEM, VMEM] + [ANY] * 3,
        out_specs=[VMEM] * 7 + [ANY],
        scratch_shapes=[pltpu.SemaphoreType.DMA((2,))],
        input_output_aliases={5: 7},
        compiler_params=params(16),
        name="tables",
    )(
        in_hbm(selected), in_hbm(lengths), in_hbm(freq), in_hbm(key_latent_maps),
        in_hbm(value_latent_maps), values[1],
    )
    key_parts = exchange(keys, "heads", heads)
    value_parts = scatter([values[0], held, *values[2:]], "pool", pools)

    weight = pl.pallas_call(
        stage_kernel,
        out_shape=shape(out_weight.shape, bf16),
        in_specs=[HBM, ANY],
        out_specs=VMEM,
        scratch_shapes=[pltpu.SemaphoreType.DMA],
        compiler_params=params(4),
        name="stage",
    )(in_hbm(out_weight), place)
    turned = pl.pallas_call(
        functools.partial(rebuild_kernel, pools, heads),
        out_shape=shape((pools * rows, own_heads // QUERY_PER_GROUP * HEAD_SIZE), bf16),
        in_specs=[VMEM] * 3 + [ANY] + [VMEM] * heads,
        out_specs=VMEM,
        compiler_params=params(20),
        name="rebuild",
    )(key_maps, cosine, sine, weight, *key_parts)
    dense, *scores = pl.pallas_call(
        functools.partial(score_kernel, pools),
        out_shape=[shape((sel_count * BLOCK, width), bf16)] + [shape((own_heads, rows), f32)] * pools,
        in_specs=[VMEM] * (4 + pools),
        out_specs=[VMEM] * (1 + pools),
        compiler_params=params(16),
        name="score",
    )(turn, live, place, turned, *value_parts[::-1])
    dense_parts = exchange(dense, "heads", heads)
    score_parts = scatter(scores, "pool", pools)

    mine = pl.pallas_call(
        functools.partial(attend_kernel, pools, heads),
        out_shape=shape((1, own_heads * HEAD_SIZE), bf16),
        in_specs=[VMEM] * (2 + pools + heads),
        out_specs=VMEM,
        compiler_params=params(16),
        name="attend",
    )(value_maps, place, *[score_parts[k] for k in served(pools)], *dense_parts)
    own_rows = join(*exchange(mine, "rep", reps))
    row_parts = exchange(own_rows, "pool", pools)

    own_columns = out_weight.shape[1]
    each = pools // heads
    parts = pl.pallas_call(
        functools.partial(project_kernel, pools, heads, reps),
        out_shape=[shape((each, own_columns), f32)] * (heads * reps),
        in_specs=[VMEM] * (pools + 1),
        out_specs=[VMEM] * (heads * reps),
        scratch_shapes=[pltpu.VMEM((pools * reps, own_columns), f32)],
        compiler_params=params(24),
        name="project",
    )(weight, *[row_parts[k] for k in served(pools)[::-1]])
    return pl.pallas_call(
        functools.partial(finish_kernel, heads, reps),
        out_shape=shape((1, each, reps * own_columns), bf16),
        in_specs=[VMEM] * (heads * reps),
        out_specs=VMEM,
        compiler_params=params(4),
        name="finish",
    )(*scatter(parts, ("heads", "rep"), heads * reps)[::-1])


def solution(mesh):
    return jax.shard_map(
        per_device,
        mesh=mesh,
        in_specs=(
            P(("groups", "rep"), "pool", "heads"),
            P(("groups", "rep"), None, "pool", "heads"),
            P(None, "heads"),
            P(None, "heads"),
            P("heads", ("pool", "rep")),
            P(("groups", "rep"), None),
            P(("groups", "rep"), None, None),
        ),
        out_specs=P(("groups", "rep"), "heads", "pool"),
        check_vma=False,
    )
```
